256 devices in a mesh: seq: 16 (over z, core), mp: 8 (over x, y_lo), roll: 2 (over y_hi).
Axes of the slice: x: 4, y: 4 (y_hi: 2, y_lo: 2; y = y_hi * 2 + y_lo), z: 8, core: 2. Of those that a mesh axis runs over, the one named last changes fastest.
Arguments:
- tokens: bfloat16 [2, 2048, 2304], P('roll', 'seq', 'mp'), may hold values from -6 to 6
- cotangent: bfloat16 [2, 2048, 2304], P('roll', 'seq', 'mp'), may hold values from -6 to 6
- doc_ids: int32 [2, 2048], P('roll', 'seq'), may hold values from 0 to 3, never falling along the last dimension, each value on 1 to 1024 neighbouring positions
- projections: bfloat16 [2304, 4, 2048], P(('seq', 'roll'), None, 'mp'), may hold values from -0.125 to 0.125
- conv_weight: float32 [3, 4, 2048], P(None, None, 'mp'), may hold values from -3 to 3
- gate_down: bfloat16 [2304, 128], replicated, may hold values from -0.125 to 0.125
- gate_up: bfloat16 [128, 2048], P(None, 'mp'), may hold values from -0.5 to 0.5
- decay_log: float32 [16], P('mp'), may hold values from -9.5 to -3
- beta_weight: bfloat16 [2304, 16], P(None, 'mp'), may hold values from -0.125 to 0.125
- norm_gain: float32 [128], replicated, may hold values from 0.1 to 1.9
Outputs:
- layer_out: bfloat16 [2, 2048, 2304], P('roll', 'seq', 'mp')
- engine_tiles: bfloat16 [2304, 4, 2048], P('seq', None, 'mp')
The draws below stay inside these ranges and needn't reach their ends.
Inputs may be any that keep to these rules, and one draw needn't show every extreme that they name: doc_ids never decrease along a sequence and start at 0; each sequence holds 4 documents, the longest 1024 tokens.
All inputs are finite; a program needn't handle non-finite values.
Results may differ from the reference program's by a relative error of at most 0.0035.
The reference program's roundings to bfloat16 on the way (of `low`, `hidden` and `d_projected`) count: a program that leaves them out, or rounds other values in their place, can miss the bound.
Values may be sent and summed in bfloat16 or wider, within the bound.
No kernel may reach another device: no remote copies, remote signals or barrier semaphores. Data moves between devices by JAX's collectives and lax.ppermute only.
A program may use at most 64 MiB of HBM per device.

```python
import math
import jax
import jax.numpy as jnp
import numpy as np
from jax import lax

D = 2304
DK = 128
RANK = 128
TAPS = 4
DOCS = 4
HEADS = 16
HKT = 2048
LENGTH = 2048
SEQS = 2
DOC_MOST = 1024
N_MP = 8


def levels(rng, dims, shards, least, largest):
    def one(position, blocks):
        draws = jax.random.uniform(jax.random.fold_in(jax.random.fold_in(rng, 6), position), (blocks,), jnp.float32, least / len(shards), largest / len(shards))
        return jnp.repeat(jnp.exp(draws), dims[position] // blocks).reshape((-1,) + (1,) * (len(dims) - position - 1))

    gain = one(*shards[0])
    for cut in shards[1:]:
        gain = gain * one(*cut)
    return gain


def profile(count, total, reach, lean):
    loads = [(1 << 20) // math.isqrt(grade ** lean) + 1 for grade in range(2, count + 1)]
    spare, holding = total - reach - (count - 1), [1] * (count - 1)
    while spare > 0:
        free = [i for i in range(count - 1) if holding[i] < reach]
        mass, left = sum([loads[i] for i in free]), spare
        for i in free:
            extra = min(reach - holding[i], max(1, left * loads[i] // mass), spare)
            holding[i] = holding[i] + extra
            spare = spare - extra
    return np.array([reach] + holding)


def ragged_sizes(own_key, amount, total, reach, lean):
    if amount == 2:
        one = jax.random.randint(own_key, (), max(1, total - reach), min(reach, total - 1) + 1)
        return jnp.stack([one, total - one])
    tallies = jnp.asarray(profile(amount, total, reach, lean), jnp.int32)
    pairs = (amount - 1) // 2
    source_of, receiver = tallies[1:1 + 2 * pairs:2], tallies[2:2 + 2 * pairs:2]
    margin = jnp.minimum(source_of - 1, reach - receiver)
    shifted = jax.random.randint(jax.random.fold_in(own_key, 1), (pairs,), 0, 1 << 20) % (margin + 1)
    tallies = tallies.at[1:1 + 2 * pairs:2].set(source_of - shifted).at[2:2 + 2 * pairs:2].set(receiver + shifted)
    return tallies[jax.random.permutation(jax.random.fold_in(own_key, 2), amount)]


def scatter_about(own_key, extent, deviation, limit, cuts=(), held_as=jnp.bfloat16):
    values = jax.random.normal(own_key, extent, jnp.float32) * deviation
    if len(cuts) > 0:
        values = levels(own_key, extent, cuts, -0.22, 0.18) * values
    return jnp.clip(values, min=-limit, max=limit).astype(held_as)


def setup_inputs(seed: int = 0) -> dict:
    key_list = jax.random.split(jax.random.key(seed), 11)
    tokens = scatter_about(key_list[0], (SEQS, LENGTH, D), 1.0, 6.0, ((0, 2), (1, 16), (2, 8)))
    cotangent = scatter_about(key_list[1], (SEQS, LENGTH, D), 1.0, 6.0, ((0, 2), (1, 16), (2, 8)))
    doc_ids = jax.vmap(lambda own: jnp.searchsorted(jnp.cumsum(ragged_sizes(own, DOCS, LENGTH, DOC_MOST, 0)), jnp.arange(LENGTH), side="right"))(jax.random.split(key_list[2], SEQS)).reshape((SEQS, LENGTH)).astype(jnp.int32)
    projections = scatter_about(key_list[3], (D, 4, HKT), D ** -0.5, 0.125, ((0, 32), (2, 8)))
    conv_weight = scatter_about(key_list[4], (3, TAPS, HKT), 0.5, 3.0, ((2, 8),), jnp.float32)
    gate_down = scatter_about(key_list[5], (D, RANK), D ** -0.5, 0.125)
    gate_up = scatter_about(key_list[6], (RANK, HKT), RANK ** -0.5, 0.5, ((1, 8),))
    decay_log = jnp.clip(-9.5 + 6.5 * jax.random.uniform(key_list[7], (HEADS,), jnp.float32) ** levels(key_list[7], (HEADS,), ((0, 8),), -0.2, 0.2), -9.5, -3.0)
    beta_weight = scatter_about(key_list[8], (D, HEADS), D ** -0.5, 0.125, ((1, 8),))
    norm_gain = jnp.clip(1.0 + 0.18 * jax.random.normal(key_list[9], (DK,), jnp.float32), 0.1, 1.9)
    return {"tokens": tokens, "cotangent": cotangent, "doc_ids": doc_ids, "projections": projections, "conv_weight": conv_weight, "gate_down": gate_down, "gate_up": gate_up, "decay_log": decay_log, "beta_weight": beta_weight, "norm_gain": norm_gain}


top_precision = lax.Precision.HIGHEST
block_len = 64
learn_rate = 0.01

def unit_rows(values):
    return values * lax.rsqrt(lax.optimization_barrier(jnp.sum(values * values, axis=-1, keepdims=True)) + 1e-06)

def prepare(extended, doc_ext, conv_weight, heads):
    taps = conv_weight.shape[1]
    length_here = extended.shape[0] - taps + 1
    current = doc_ext[taps - 1:]
    total = jnp.zeros((length_here,) + extended.shape[1:], jnp.float32)
    for tap_index in range(taps):
        same_doc = (doc_ext[tap_index:tap_index + length_here] == current).astype(jnp.float32)
        total = total + extended[tap_index:tap_index + length_here] * conv_weight[:, tap_index, :][None] * same_doc[:, None, None]
    active = jax.nn.silu(total)
    head_size = extended.shape[2] // heads
    split = active.reshape(length_here, 3, heads, head_size)
    return (unit_rows(split[:, 0]), unit_rows(split[:, 1]), split[:, 2])

def block_terms(query, keys, log_decay, beta, doc_list, prior):
    length_here = query.shape[0]
    summed = jnp.cumsum(log_decay, axis=0)
    growth = jnp.exp(summed)
    key_grow = keys * growth
    key_shrink = keys * jnp.exp(-summed)
    query_grow = query * growth
    paired = (doc_list[:, None] == doc_list[None, :]).astype(jnp.float32)
    carried = (doc_list == prior).astype(jnp.float32)
    strict = jnp.tri(length_here, k=-1, dtype=jnp.float32)
    inclusive = jnp.tri(length_here, dtype=jnp.float32)
    inner = jnp.einsum('ihd,jhd->hij', key_grow, key_shrink, precision=top_precision) * (paired * strict)[None] * beta.T[:, :, None]
    scores = jnp.einsum('ihd,jhd->hij', query_grow, key_shrink, precision=top_precision) * (paired * inclusive)[None]
    system = jnp.eye(length_here, dtype=jnp.float32)[None] + inner
    tail_keys = keys * jnp.exp(summed[-1][None] - summed) * paired[-1][:, None, None]
    keep_last = carried[-1] * growth[-1]
    return (key_grow, query_grow, carried, scores, system, tail_keys, keep_last)

def block_out(terms, values, beta, state):
    key_grow, query_grow, carried, scores, system, tail_keys, keep_last = terms
    from_keys = jnp.einsum('ihd,hde->hie', key_grow, state, precision=top_precision)
    target = beta.T[:, :, None] * (jnp.transpose(values, (1, 0, 2)) - carried[None, :, None] * from_keys)
    pseudo = jax.scipy.linalg.solve_triangular(system, target, lower=True, unit_diagonal=True)
    from_query = jnp.einsum('ihd,hde->hie', query_grow, state, precision=top_precision)
    output = carried[None, :, None] * from_query + jnp.einsum('hij,hje->hie', scores, pseudo, precision=top_precision)
    updated = keep_last[:, :, None] * state + jnp.einsum('jhd,hje->hde', tail_keys, pseudo, precision=top_precision)
    return (output, updated)

def run_blocks(query, keys, values, log_decay, beta, doc_ext, state):
    length_here = query.shape[0]
    rim_rows = doc_ext.shape[0] - length_here
    count = length_here // block_len
    doc_list = doc_ext[rim_rows:]
    priors = doc_ext[rim_rows - 1:rim_rows - 1 + length_here:block_len]

    def blocked(array):
        return array.reshape((count, block_len) + array.shape[1:])

    def advance(current, pieces):
        part_query, part_keys, part_values, part_decay, part_beta, part_docs, part_prior = pieces
        terms = block_terms(part_query, part_keys, part_decay, part_beta, part_docs, part_prior)
        output, updated = block_out(terms, part_values, part_beta, current)
        return (updated, output)
    final, outputs = lax.scan(jax.checkpoint(advance), state, (blocked(query), blocked(keys), blocked(values), blocked(log_decay), blocked(beta), blocked(doc_list), priors))
    outputs = jnp.transpose(outputs, (0, 2, 1, 3)).reshape(length_here, outputs.shape[1], outputs.shape[3])
    return (outputs, final)

def finish(query, keys, values, log_decay, beta, doc_ext, state, norm_gain):
    outputs, final = run_blocks(query, keys, values, log_decay, beta, doc_ext, state)
    scale = lax.rsqrt(lax.optimization_barrier(jnp.mean(outputs * outputs, axis=-1, keepdims=True)) + 1e-05)
    normed = outputs * scale * norm_gain
    return (normed.reshape(outputs.shape[0], -1), final)

def reference(tokens, cotangent, doc_ids, projections, conv_weight, gate_down, gate_up, decay_log, beta_weight, norm_gain):
    seq_count, length_all, model_width = tokens.shape
    heads_all = decay_log.shape[0]
    head_size = norm_gain.shape[0]
    group = heads_all // N_MP
    columns = group * head_size
    rim_rows = conv_weight.shape[1] - 1
    grads = jnp.zeros(projections.shape, jnp.float32)
    results = []
    for seq_index in range(seq_count):
        features = tokens[seq_index]
        upstream = cotangent[seq_index]
        doc_ext = jnp.concatenate([jnp.full((rim_rows,), -1, jnp.int32), doc_ids[seq_index].astype(jnp.int32)])
        low = jnp.dot(features.astype(jnp.float32), gate_down.astype(jnp.float32), preferred_element_type=jnp.float32).astype(jnp.bfloat16)
        total = jnp.zeros((length_all, model_width), jnp.float32)
        pieces = []
        for group_index in range(N_MP):
            lower = group_index * columns
            w_part = projections[:, :, lower:lower + columns]
            projected = jnp.einsum('td,dcn->tcn', features.astype(jnp.float32), w_part[:, :3].astype(jnp.float32), preferred_element_type=jnp.float32)
            extended = jnp.concatenate([jnp.zeros((rim_rows,) + projected.shape[1:], jnp.float32), projected])
            conv_part = conv_weight[:, :, lower:lower + columns]
            (query, keys, values), prep_back = jax.vjp(lambda ext: prepare(ext, doc_ext, conv_part, group), extended)
            rates = jnp.dot(low.astype(jnp.float32), gate_up[:, lower:lower + columns].astype(jnp.float32), preferred_element_type=jnp.float32).reshape(length_all, group, head_size)
            log_decay = -jnp.exp(decay_log[group_index * group:(group_index + 1) * group])[None, :, None] * jax.nn.softplus(rates)
            beta = jax.nn.sigmoid(jnp.dot(features.astype(jnp.float32), beta_weight[:, group_index * group:(group_index + 1) * group].astype(jnp.float32), preferred_element_type=jnp.float32))
            zero_state = jnp.zeros((group, head_size, head_size), jnp.float32)
            (normed, final), core_back = jax.vjp(lambda qa, ka, va: finish(qa, ka, va, log_decay, beta, doc_ext, zero_state, norm_gain), query, keys, values)
            hidden = normed.astype(jnp.bfloat16)
            total = total + jnp.einsum('tn,dn->td', hidden.astype(jnp.float32), w_part[:, 3].astype(jnp.float32), preferred_element_type=jnp.float32)
            d_hidden = jnp.einsum('td,dn->tn', upstream.astype(jnp.float32), w_part[:, 3].astype(jnp.float32), preferred_element_type=jnp.float32)
            d_query, d_keys, d_values = core_back((d_hidden, jnp.zeros_like(final)))
            d_extended, = prep_back((d_query, d_keys, d_values))
            d_projected = d_extended[rim_rows:].astype(jnp.bfloat16)
            first = jnp.einsum('td,tcn->dcn', features.astype(jnp.float32), d_projected.astype(jnp.float32), preferred_element_type=jnp.float32)
            last = jnp.einsum('td,tn->dn', upstream.astype(jnp.float32), hidden.astype(jnp.float32), preferred_element_type=jnp.float32)
            pieces.append(jnp.concatenate([first, last[:, None]], axis=1))
        grads = grads + jnp.concatenate(pieces, axis=2)
        results.append(total.astype(jnp.bfloat16))
    engine_tiles = (projections.astype(jnp.float32) - learn_rate * grads).astype(jnp.bfloat16)
    return (jnp.stack(results), engine_tiles)
```

```python
import jax
import jax.numpy as jnp
from jax import lax
from jax.experimental import pallas as pl
from jax.experimental.pallas import tpu as pltpu
from jax.sharding import Mesh
from jax.sharding import PartitionSpec as P

BLOCK = 64
TAPS = 4
HALO = 16
RATE = 0.01
TOKEN_MOST = 6.0
LAST_POWER = 16.0
TOP = 15.0
F32 = jnp.float32
F16 = jnp.float16
BF16 = jnp.bfloat16
HIGH = lax.Precision.HIGHEST
VMEM_LIMIT = 56 * 1024 * 1024


def mm(a, b):
    return lax.dot_general(a, b, (((1,), (0,)), ((), ())), precision=HIGH, preferred_element_type=F32)


def mm_nt(a, b):
    return lax.dot_general(a, b, (((1,), (1,)), ((), ())), precision=HIGH, preferred_element_type=F32)


def mm_tn(a, b):
    return mm(a.T, b)


def softplus(x):
    return jnp.maximum(x, 0.0) + jnp.log1p(jnp.exp(-jnp.abs(x)))


def masks(docs_ref, doc_row_ref):
    length = docs_ref.shape[0]
    row = lax.broadcasted_iota(jnp.int32, (length, length), 0)
    col = lax.broadcasted_iota(jnp.int32, (length, length), 1)
    inside = (row // BLOCK == col // BLOCK) & (row >= col)
    paired = docs_ref[:, 3:4] == doc_row_ref[...]
    inclusive = inside & paired
    strict = inclusive & (row > col)
    return row, col, inside, inclusive, strict


def carried_of(docs_ref):
    return (docs_ref[:, 3:4] == docs_ref[:, 4:5]).astype(F32)


def gather_kernel(
    place_ref, features_ref, upstream_ref, gate_weights_ref, *refs
):
    pieces, (proj_ref, d_hidden_ref, gates_ref) = refs[:-3], refs[-3:]
    size = features_ref.shape[0]
    head = d_hidden_ref.shape[1]
    here = upstream_ref.shape[3]
    length = 2 * here
    proj = jnp.zeros(proj_ref.shape, F32)
    d_hidden = jnp.zeros(d_hidden_ref.shape, F32)
    gates = jnp.zeros(gates_ref.shape, F32)
    for k, piece in enumerate(pieces):
        index = lax.rem(place_ref[0] + offset_of(k) + size, size)
        proj = proj + jnp.dot(features_ref[index].T, piece[:, : 3 * head], preferred_element_type=F32)
        both = jnp.concatenate([upstream_ref[0, index].T, upstream_ref[1, index].T])
        d_hidden = d_hidden + jnp.dot(both, piece[:, 3 * head :], preferred_element_type=F32)
    for k in range(size):
        gates = gates + jnp.dot(
            features_ref[k, :, :length].T, gate_weights_ref[k], preferred_element_type=F32
        )
    proj_ref[...] = proj
    d_hidden_ref[...] = d_hidden
    gates_ref[...] = gates


def offset_of(k):
    return ((k + 1) // 2) * (-1 if k % 2 else 1)


def pre_kernel(
    place_ref, features_ref, upstream_ref, piece_ref, proj_in_ref, d_hidden_in_ref,
    gates_ref, gate_up_ref, rate_ref, conv_ref, docs_ref, doc_row_ref,
    total_ref, grow_ref, inv_ref, score_ref, wu_ref, qo_ref, maps_ref, device_map_ref, d_hidden_ref,
    ext_ref,
):
    length, head = d_hidden_ref.shape
    count = length // BLOCK
    size = features_ref.shape[0]
    index = lax.rem(place_ref[0] + size // 2, size)
    proj = proj_in_ref[...] + jnp.dot(features_ref[index].T, piece_ref[:, : 3 * head], preferred_element_type=F32)
    both = jnp.concatenate([upstream_ref[0, index].T, upstream_ref[1, index].T])
    d_hidden_ref[...] = d_hidden_in_ref[...] + jnp.dot(both, piece_ref[:, 3 * head :], preferred_element_type=F32)
    ext_ref[:HALO] = proj[length:]
    ext_ref[HALO:] = proj[:length]
    total = jnp.zeros((length, 3 * head), F32)
    for j in range(TAPS):
        same = (docs_ref[:, j : j + 1] == docs_ref[:, 3:4]).astype(F32)
        total = total + ext_ref[HALO - 3 + j : HALO - 3 + j + length] * conv_ref[j : j + 1] * same
    total_ref[...] = total
    active = total * jax.nn.sigmoid(total)
    query, keys, values = active[:, :head], active[:, head : 2 * head], active[:, 2 * head :]
    query = query * lax.rsqrt(jnp.sum(query * query, axis=1, keepdims=True) + 1e-6)
    keys = keys * lax.rsqrt(jnp.sum(keys * keys, axis=1, keepdims=True) + 1e-6)
    low = gates_ref[:, :head].astype(BF16)
    rates = jnp.dot(low, gate_up_ref[...], preferred_element_type=F32)
    log_decay = -rate_ref[...] * softplus(rates)
    beta = jax.nn.sigmoid(gates_ref[:, head : head + 1])
    row, col, inside, inclusive, strict = masks(docs_ref, doc_row_ref)
    carried = carried_of(docs_ref)
    summed = mm(inside.astype(F32), log_decay)
    ends = jnp.concatenate(
        [jnp.broadcast_to(summed[b * BLOCK + BLOCK - 1 : (b + 1) * BLOCK], (BLOCK, head)) for b in range(count)]
    )
    grow = jnp.exp(summed)
    shrink = jnp.exp(-summed)
    tail = jnp.exp(ends - summed) * (docs_ref[:, 3:4] == docs_ref[:, 5:6]).astype(F32)
    grow_ref[:, :head] = grow
    grow_ref[:, head : 2 * head] = shrink
    grow_ref[:, 2 * head :] = tail
    key_grow, key_shrink, query_grow, key_tail = keys * grow, keys * shrink, query * grow, keys * tail
    both = mm_nt(jnp.concatenate([key_grow, query_grow]), key_shrink)
    lower = jnp.where(strict, both[:length], 0.0) * beta
    scores = jnp.where(inclusive, both[length:], 0.0)
    score_ref[...] = scores
    inverse = (row == col).astype(F32) - jnp.where(row // 2 == col // 2, lower, 0.0)
    size = 2
    while size < BLOCK:
        corner = jnp.where((row // (2 * size) == col // (2 * size)) & (row // size != col // size), lower, 0.0)
        inverse = inverse - mm(inverse, mm(corner, inverse))
        size *= 2
    inv_ref[...] = inverse
    wu = mm(inverse, jnp.concatenate([beta * carried * key_grow, beta * values], axis=1))
    wu_ref[...] = wu
    mixed = mm(scores, wu)
    qo_ref[:, :head] = carried * query_grow - mixed[:, :head]
    qo_ref[:, head:] = mixed[:, head:]
    eye = lax.broadcasted_iota(jnp.int32, (head, head), 0) == lax.broadcasted_iota(jnp.int32, (head, head), 1)
    pairs = []
    for b in range(count):
        rows = slice(b * BLOCK, (b + 1) * BLOCK)
        last = (b + 1) * BLOCK - 1
        keep = grow[last : last + 1] * carried[last : last + 1]
        update = mm_tn(key_tail[rows], wu[rows])
        moved = jnp.where(eye, keep, 0.0) - update[:, :head]
        maps_ref[b, :, :head] = moved
        maps_ref[b, :, head:] = update[:, head:]
        pairs.append((moved, update[:, head:]))

    def after(second, first):
        made = mm(second[0], jnp.concatenate(first, axis=1))
        return (made[:, :head], made[:, head:] + second[1])

    while len(pairs) > 1:
        pairs = [after(pairs[i + 1], pairs[i]) for i in range(0, len(pairs), 2)]
    device_map_ref[:, :head] = pairs[0][0]
    device_map_ref[:, head:] = pairs[0][1]


def mid_kernel(
    near_ref, far_ref, maps_ref, wu_ref, qo_ref, d_hidden_ref, gain_ref,
    hidden_ref, d_out_ref, pseudo_ref, states_ref, from_out_ref, d_enter_ref,
):
    length, head = d_hidden_ref.shape
    count = length // BLOCK
    state = near_ref[:, head:] + mm(near_ref[:, :head], far_ref[...])
    states = []
    for b in range(count):
        states.append(state)
        states_ref[b] = state
        if b < count - 1:
            state = mm(maps_ref[b, :, :head], state) + maps_ref[b, :, head:]
    outs, pseudos = [], []
    for b in range(count):
        rows = slice(b * BLOCK, (b + 1) * BLOCK)
        made = mm(jnp.concatenate([qo_ref[rows, :head], wu_ref[rows, :head]]), states[b])
        outs.append(qo_ref[rows, head:] + made[:BLOCK])
        pseudos.append(wu_ref[rows, head:] - made[BLOCK:])
    out = jnp.concatenate(outs)
    pseudo_ref[...] = jnp.concatenate(pseudos)
    scale = lax.rsqrt(jnp.mean(out * out, axis=1, keepdims=True) + 1e-5)
    hidden_ref[...] = (out * scale * gain_ref[...]).astype(BF16)
    lifted = d_hidden_ref[...] * gain_ref[...]
    d_out = scale * lifted - out * (scale * scale * scale) * jnp.mean(lifted * out, axis=1, keepdims=True)
    d_out_ref[...] = d_out
    d_state = None
    for b in reversed(range(count)):
        rows = slice(b * BLOCK, (b + 1) * BLOCK)
        part = mm_tn(qo_ref[rows, :head], d_out[rows])
        from_out_ref[b] = part
        d_state = part if d_state is None else part + mm_tn(maps_ref[b, :, :head], d_state)
    d_enter_ref[...] = d_state


def share_kernel(place_ref, hidden_ref, upstream_ref, *refs):
    pieces, (share_ref, last_ref) = refs[:-2], refs[-2:]
    size, here = upstream_ref.shape[1], upstream_ref.shape[3]
    head = hidden_ref.shape[1]
    for k, piece in enumerate(pieces):
        index = lax.rem(place_ref[0] + offset_of(k) + size, size)
        weights = piece[:, 3 * head :]
        total = jnp.zeros((piece.shape[0], head), F32)
        for c in range(2):
            part = hidden_ref[c * here : (c + 1) * here]
            share_ref[c, index] = lax.dot_general(
                weights, part, (((1,), (1,)), ((), ())), preferred_element_type=F32
            )
            total = total + jnp.dot(upstream_ref[c, k], part, preferred_element_type=F32)
        last_ref[k] = total


def post_kernel(
    near_ref, far_ref, far_map_ref, maps_ref, from_out_ref, states_ref, pseudo_ref, d_out_ref, inv_ref, score_ref,
    grow_ref, total_ref, gates_ref, docs_ref, doc_row_ref, conv_ref,
    d_proj_ref, power_ref,
    d_ext_ref,
):
    length, head = d_out_ref.shape
    count = length // BLOCK
    d_state = near_ref[...] + mm_tn(far_map_ref[...], far_ref[...])
    d_after = [None] * count
    for b in reversed(range(count)):
        d_after[b] = d_state
        if b > 0:
            d_state = from_out_ref[b] + mm_tn(maps_ref[b, :, :head], d_state)
    total = total_ref[...]
    gate = jax.nn.sigmoid(total)
    active = total * gate
    raw_q, raw_k = active[:, :head], active[:, head : 2 * head]
    inv_q = lax.rsqrt(jnp.sum(raw_q * raw_q, axis=1, keepdims=True) + 1e-6)
    inv_k = lax.rsqrt(jnp.sum(raw_k * raw_k, axis=1, keepdims=True) + 1e-6)
    query, keys = raw_q * inv_q, raw_k * inv_k
    grow, shrink, tail = grow_ref[:, :head], grow_ref[:, head : 2 * head], grow_ref[:, 2 * head :]
    key_grow, key_shrink, query_grow, key_tail = keys * grow, keys * shrink, query * grow, keys * tail
    beta = jax.nn.sigmoid(gates_ref[:, head : head + 1])
    _, _, _, inclusive, strict = masks(docs_ref, doc_row_ref)
    carried = carried_of(docs_ref)
    d_out, pseudo = d_out_ref[...], pseudo_ref[...]

    def each(function):
        return jnp.concatenate([function(b, slice(b * BLOCK, (b + 1) * BLOCK)) for b in range(count)])

    d_pseudo = mm_tn(score_ref[...], d_out) + each(lambda b, rows: mm(key_tail[rows], d_after[b]))
    d_target = mm_tn(inv_ref[...], d_pseudo)
    both = mm_nt(jnp.concatenate([d_out, d_target]), pseudo)
    d_scores = jnp.where(inclusive, both[:length], 0.0)
    d_lower = jnp.where(strict, both[length:], 0.0) * (-beta)
    d_values = beta * d_target
    d_from_keys = -carried * d_values
    lifted_out = carried * d_out
    d_query_grow = each(lambda b, rows: mm_nt(lifted_out[rows], states_ref[b])) + mm(d_scores, key_shrink)
    d_key_grow = each(lambda b, rows: mm_nt(d_from_keys[rows], states_ref[b])) + mm(d_lower, key_shrink)
    d_key_shrink = mm_tn(d_scores, query_grow) + mm_tn(d_lower, key_grow)
    d_key_tail = each(lambda b, rows: mm_nt(pseudo[rows], d_after[b]))
    d_query = d_query_grow * grow
    d_keys = d_key_grow * grow + d_key_shrink * shrink + d_key_tail * tail
    d_query = inv_q * d_query - query * (inv_q * jnp.sum(d_query * query, axis=1, keepdims=True))
    d_keys = inv_k * d_keys - keys * (inv_k * jnp.sum(d_keys * keys, axis=1, keepdims=True))
    d_total = jnp.concatenate([d_query, d_keys, d_values], axis=1) * (gate * (1.0 + total * (1.0 - gate)))
    d_ext_ref[...] = jnp.zeros_like(d_ext_ref)
    for j in range(TAPS):
        same = (docs_ref[:, j : j + 1] == docs_ref[:, 3:4]).astype(F32)
        spot = slice(HALO - 3 + j, HALO - 3 + j + length)
        d_ext_ref[spot] = d_ext_ref[spot] + d_total * conv_ref[j : j + 1] * same
    d_proj_ref[:length] = d_ext_ref[HALO:].astype(BF16)
    d_proj_ref[length:] = d_ext_ref[:HALO].astype(BF16)
    most = jnp.max(jnp.abs(d_ext_ref[...]), axis=0, keepdims=True) * (TOKEN_MOST * 1.01 * (length + HALO))
    power = jnp.ceil(jnp.log(jnp.maximum(most, 1e-30)) * 1.4426950408889634 + 0.01)
    power_ref[:, : 3 * head] = jnp.broadcast_to(power, (8, 3 * head))
    power_ref[:, 3 * head :] = jnp.full((8, head), LAST_POWER, F32)


def call(kernel, outs, *args, scratch=()):
    def spec(arg):
        return pl.BlockSpec(memory_space=pltpu.SMEM if arg.dtype == jnp.int32 else pltpu.VMEM)

    return pl.pallas_call(
        kernel,
        out_shape=tuple(jax.ShapeDtypeStruct(shape, dtype) for shape, dtype in outs),
        in_specs=[spec(arg) for arg in args],
        out_specs=tuple(pl.BlockSpec(memory_space=pltpu.VMEM) for _ in outs),
        scratch_shapes=list(scratch),
        compiler_params=pltpu.CompilerParams(vmem_limit_bytes=VMEM_LIMIT),
    )(*args)


def pack(total, power):
    scaled = (total * jnp.exp2(TOP - power)).astype(F16)
    return jnp.concatenate([scaled, jnp.broadcast_to(power, (16, total.shape[1])).astype(F16)])


def unpack(packed):
    power = packed[-16:-15].astype(F32)
    return packed[:-16].astype(F32) * jnp.exp2(power - TOP), power


def swap(array, axis):
    return lax.ppermute(array, axis, [(0, 1), (1, 0)])


def turn(array, axis, by):
    size = lax.axis_size(axis)
    return lax.ppermute(array, axis, [(i, (i + by) % size) for i in range(size)])


def shift(array, axis, by):
    size = lax.axis_size(axis)
    return lax.ppermute(array, axis, [(i, i + by) for i in range(size) if 0 <= i + by < size])


def ordered(mine, other, index):
    return jnp.where(index == 0, jnp.stack([mine, other]), jnp.stack([other, mine]))


def pick(array, index):
    return lax.dynamic_index_in_dim(array, index, 0, keepdims=False)


def put(array, piece, index):
    return lax.dynamic_update_index_in_dim(array, piece, index, 0)


def outer(a, b):
    return lax.dot_general(a, b, (((0,), (0,)), ((), ())), preferred_element_type=F32)


def per_device(
    tokens, cotangent, doc_ids, projections, conv_weight, gate_down, gate_up, decay_log, beta_weight, norm_gain
):
    z, core, x, ylo, roll = (lax.axis_index(a) for a in ("z", "core", "x", "ylo", "roll"))
    nz, nx = lax.axis_size("z"), lax.axis_size("x")
    here, width = tokens.shape[1], tokens.shape[2]
    head = norm_gain.shape[0]
    rows = projections.shape[0]
    length = 2 * here
    span = 4 * rows

    split = projections.reshape(rows, 4, 2, head)
    mine = lax.dynamic_index_in_dim(split, core, 2, keepdims=False).reshape(rows, 4 * head)
    theirs = lax.dynamic_index_in_dim(split, 1 - core, 2, keepdims=False).reshape(rows, 4 * head)
    chip_rows = ordered(mine, swap(theirs, "core"), core)
    piece = jnp.swapaxes(ordered(chip_rows, swap(chip_rows, "roll"), roll), 0, 1).reshape(span, 4 * head)

    def gather_mp(block):
        pair = ordered(block, swap(block, "ylo"), ylo)
        full = jnp.zeros((nx,) + pair.shape, pair.dtype)
        full = put(full, pair, x)
        for by in (1, -1, 2):
            full = put(full, turn(pair, "x", by), (x - by) % nx)
        return full.reshape(-1, block.shape[1])

    features = gather_mp(tokens[0].T)
    model = features.shape[0]
    doc_row = jnp.broadcast_to((doc_ids + 1).astype(BF16), (16, here))
    own = jnp.concatenate([features, doc_row])
    both_cores = ordered(own, swap(own, "core"), core)
    chip = jnp.concatenate([both_cores[0], both_cores[1]], axis=1)
    halo = shift(chip[:, length - HALO :].T, "z", 1)
    features = chip[:model]
    upstream = lax.all_gather(cotangent[0].T, ("core", "x", "ylo"), axis=0).reshape(2, nz, span, here)
    docs = chip[model].astype(F32)
    doc_ext = jnp.concatenate([halo[HALO - 3 :, model].astype(F32), docs])
    prior = jnp.repeat(doc_ext[2 : 2 + length : BLOCK], BLOCK)
    last = jnp.repeat(docs[BLOCK - 1 :: BLOCK], BLOCK)
    doc_columns = jnp.stack([doc_ext[j : j + length] for j in range(TAPS)] + [prior, last, docs, docs], axis=1)
    extended = jnp.concatenate([features, halo[:, :model].T], axis=1)

    beta_column = lax.dynamic_index_in_dim(beta_weight, core, 1)
    gate_weights = jnp.concatenate([gate_down, jnp.pad(beta_column, ((0, 0), (0, head - 1)))], axis=1)
    gate_up = lax.dynamic_index_in_dim(gate_up.reshape(-1, 2, head), core, 1, keepdims=False)
    rate = jnp.broadcast_to(jnp.exp(pick(decay_log, core)), (1, head))
    conv = lax.dynamic_index_in_dim(conv_weight.reshape(3, TAPS, 2, head), core, 2, keepdims=False)
    conv = jnp.swapaxes(conv, 0, 1).reshape(TAPS, 3 * head)

    place = z.astype(jnp.int32).reshape(1)
    blocks = extended.reshape(nz, span, length + HALO)
    arrived = [piece]
    right = left = piece
    for k in range(1, nz // 2 + 1):
        right = turn(right, "z", 1)
        arrived.append(right)
        if k < nz // 2:
            left = turn(left, "z", -1)
            arrived.append(left)
    projected, d_hidden, gates = call(
        gather_kernel,
        [((length + HALO, 3 * head), F32), ((length, head), F32), ((length, 2 * head), F32)],
        place, blocks, upstream, gate_weights.reshape(nz, span, 2 * head), *arrived[:-1],
    )
    total, grow, inverse, scores, wu, qo, maps, device_map, d_hidden = call(
        pre_kernel,
        [
            ((length, 3 * head), F32), ((length, 3 * head), F32), ((length, length), F32), ((length, length), F32),
            ((length, 2 * head), F32), ((length, 2 * head), F32), ((length // BLOCK, head, 2 * head), F32),
            ((head, 2 * head), F32), ((length, head), F32),
        ],
        place, blocks, upstream, arrived[-1], projected, d_hidden, gates, gate_up, rate, conv, doc_columns, docs[None],
        scratch=[pltpu.VMEM((length + HALO, 3 * head), F32)],
    )

    one, two = shift(device_map, "z", 1), shift(device_map, "z", 2)
    joined = mm(one[:, :head], two)
    near = jnp.concatenate([joined[:, :head], joined[:, head:] + one[:, head:]], axis=1)
    far = shift(near[:, head:], "z", 2)
    far_map = shift(near[:, :head], "z", -3)
    hidden, d_out, pseudo, states, from_out, d_enter = call(
        mid_kernel,
        [
            ((length, head), BF16), ((length, head), F32), ((length, head), F32), ((length // BLOCK, head, head), F32),
            ((length // BLOCK, head, head), F32), ((head, head), F32),
        ],
        near, far, maps, wu, qo, d_hidden, norm_gain[None],
    )
    share, last = call(
        share_kernel,
        [((2, nz, span, here), F32), ((nz, span, head), F32)],
        place, hidden, upstream, *arrived,
    )
    layer_out = lax.psum_scatter(
        share.reshape(-1, span, here), ("core", "x", "ylo"), scatter_dimension=0, tiled=True
    )[0].T.astype(BF16)[None]

    d_two = d_enter + lax.dot_general(
        device_map[:, :head], shift(d_enter, "z", -1), (((0,), (0,)), ((), ())), precision=HIGH
    )
    d_near, d_far = shift(d_two, "z", -1), shift(d_two, "z", -3)
    d_projected, power = call(
        post_kernel,
        [((length + HALO, 3 * head), BF16), ((8, 4 * head), F32)],
        d_near, d_far, far_map, maps, from_out, states, pseudo, d_out, inverse, scores, grow, total, gates, doc_columns,
        docs[None], conv,
        scratch=[pltpu.VMEM((length + HALO, 3 * head), F32)],
    )

    own_power = power[:1]

    def part(by):
        index = (z + by) % nz
        first = jnp.dot(pick(blocks, index), d_projected, preferred_element_type=F32)
        return jnp.concatenate([first, pick(last, index)], axis=1)

    def add(packed, by):
        total, power = unpack(packed)
        return total + part(by), jnp.maximum(power, own_power) + 1.0

    half = nz // 2
    right = turn(pack(part(half), own_power), "z", 1)
    left = turn(pack(part(1 - half), own_power), "z", -1)
    for k in range(1, half):
        right = turn(pack(*add(right, half - k)), "z", 1)
        if k < half - 1:
            left = turn(pack(*add(left, 1 - half + k)), "z", -1)
    total, power = add(right, 0)
    more, more_power = unpack(left)
    packed = pack(total + more, jnp.maximum(power, more_power) + 1.0)
    grad = unpack(packed)[0] + unpack(swap(packed, "roll"))[0]
    fresh = (piece.astype(F32) - RATE * grad).astype(BF16).reshape(2, span // 2, 4 * head)
    kept, sent = pick(fresh, core), pick(fresh, 1 - core)
    heads = ordered(kept, swap(sent, "core"), core).reshape(2, span // 2, 4, head)
    engine_tiles = jnp.moveaxis(heads, 0, 2).reshape(span // 2, 4, 2 * head)
    return (layer_out, engine_tiles)


def solution(mesh):
    fine = Mesh(mesh.devices.reshape(8, 2, 4, 2, 2), ("z", "core", "x", "ylo", "roll"))
    seq, mp = ("z", "core"), ("x", "ylo")
    in_specs = (
        P("roll", seq, mp),
        P("roll", seq, mp),
        P("roll", seq),
        P(("z", "core", "roll"), None, mp),
        P(None, None, mp),
        P(),
        P(None, mp),
        P(mp),
        P(None, mp),
        P(),
    )
    out_specs = (P("roll", seq, mp), P(seq, None, mp))
    return jax.shard_map(per_device, mesh=fine, in_specs=in_specs, out_specs=out_specs, check_vma=False)
```

```python
import jax
import jax.numpy as jnp
from jax import lax
from jax.experimental import pallas as pl
from jax.experimental.pallas import tpu as pltpu
from jax.sharding import Mesh
from jax.sharding import PartitionSpec as P

BLOCK = 64
TAPS = 4
HALO = 16
RATE = 0.01
TOKEN_MOST = 6.0
LAST_POWER = 16.0
TOP = 15.0
LIFT = 8.0
F32 = jnp.float32
F16 = jnp.float16
BF16 = jnp.bfloat16
HIGH = lax.Precision.HIGHEST
VMEM_LIMIT = 56 * 1024 * 1024


def product(a, b, dims, precision=None):
    return lax.dot_general(a, b, ((dims[:1], dims[1:]), ((), ())), precision=precision, preferred_element_type=F32)


def halves(a):
    high = a.astype(BF16)
    return high, (a - high.astype(F32)).astype(BF16)


def split_product(a, b, dims):
    (a_high, a_low), (b_high, b_low) = halves(a), halves(b)
    return product(a_high, b_high, dims) + (product(a_high, b_low, dims) + product(a_low, b_high, dims))


def mm(a, b):
    return split_product(a, b, (1, 0))


def mm_nt(a, b):
    return split_product(a, b, (1, 1))


def mm_tn(a, b):
    return mm(a.T, b)


def softplus(x):
    return jnp.maximum(x, 0.0) + jnp.log1p(jnp.exp(-jnp.abs(x)))


def masks(docs_ref, doc_row_ref):
    length = docs_ref.shape[0]
    row = lax.broadcasted_iota(jnp.int32, (length, length), 0)
    col = lax.broadcasted_iota(jnp.int32, (length, length), 1)
    inside = (row // BLOCK == col // BLOCK) & (row >= col)
    paired = docs_ref[:, 3:4] == doc_row_ref[...]
    inclusive = inside & paired
    strict = inclusive & (row > col)
    return row, col, inside, inclusive, strict


def carried_of(docs_ref):
    return (docs_ref[:, 3:4] == docs_ref[:, 4:5]).astype(F32)


def gather_kernel(
    place_ref, features_ref, upstream_ref, gate_weights_ref, *refs
):
    pieces, (proj_ref, d_hidden_ref, gates_ref) = refs[:-3], refs[-3:]
    size = features_ref.shape[0]
    head = d_hidden_ref.shape[1]
    here = upstream_ref.shape[3]
    length = 2 * here
    proj = jnp.zeros(proj_ref.shape, F32)
    d_hidden = jnp.zeros(d_hidden_ref.shape, F32)
    gates = jnp.zeros(gates_ref.shape, F32)
    for k, piece in enumerate(pieces):
        index = lax.rem(place_ref[0] + offset_of(k) + size, size)
        proj = proj + jnp.dot(features_ref[index].T, piece[:, : 3 * head], preferred_element_type=F32)
        both = jnp.concatenate([upstream_ref[0, index].T, upstream_ref[1, index].T])
        d_hidden = d_hidden + jnp.dot(both, piece[:, 3 * head :], preferred_element_type=F32)
    for k in range(size):
        gates = gates + jnp.dot(
            features_ref[k, :, :length].T, gate_weights_ref[k], preferred_element_type=F32
        )
    proj_ref[...] = proj
    d_hidden_ref[...] = d_hidden
    gates_ref[...] = gates


def offset_of(k):
    return ((k + 1) // 2) * (-1 if k % 2 else 1)


def pre_kernel(
    place_ref, features_ref, upstream_ref, piece_ref, proj_in_ref, d_hidden_in_ref,
    gates_ref, gate_up_ref, rate_ref, conv_ref, docs_ref, doc_row_ref,
    total_ref, grow_ref, inv_ref, score_ref, wu_ref, qo_ref, maps_ref, device_map_ref, d_hidden_ref,
    ext_ref,
):
    length, head = d_hidden_ref.shape
    count = length // BLOCK
    size = features_ref.shape[0]
    index = lax.rem(place_ref[0] + size // 2, size)
    proj = proj_in_ref[...] + jnp.dot(features_ref[index].T, piece_ref[:, : 3 * head], preferred_element_type=F32)
    both = jnp.concatenate([upstream_ref[0, index].T, upstream_ref[1, index].T])
    d_hidden_ref[...] = d_hidden_in_ref[...] + jnp.dot(both, piece_ref[:, 3 * head :], preferred_element_type=F32)
    ext_ref[:HALO] = proj[length:]
    ext_ref[HALO:] = proj[:length]
    total = jnp.zeros((length, 3 * head), F32)
    for j in range(TAPS):
        same = (docs_ref[:, j : j + 1] == docs_ref[:, 3:4]).astype(F32)
        total = total + ext_ref[HALO - 3 + j : HALO - 3 + j + length] * conv_ref[j : j + 1] * same
    total_ref[...] = total
    active = total * jax.nn.sigmoid(total)
    query, keys, values = active[:, :head], active[:, head : 2 * head], active[:, 2 * head :]
    query = query * lax.rsqrt(jnp.sum(query * query, axis=1, keepdims=True) + 1e-6)
    keys = keys * lax.rsqrt(jnp.sum(keys * keys, axis=1, keepdims=True) + 1e-6)
    low = gates_ref[:, :head].astype(BF16)
    rates = jnp.dot(low, gate_up_ref[...], preferred_element_type=F32)
    log_decay = -rate_ref[...] * softplus(rates)
    beta = jax.nn.sigmoid(gates_ref[:, head : head + 1])
    row, col, inside, inclusive, strict = masks(docs_ref, doc_row_ref)
    carried = carried_of(docs_ref)
    summed = product(inside.astype(F32), log_decay, (1, 0), HIGH)
    ends = jnp.concatenate(
        [jnp.broadcast_to(summed[b * BLOCK + BLOCK - 1 : (b + 1) * BLOCK], (BLOCK, head)) for b in range(count)]
    )
    grow = jnp.exp(summed)
    shrink = jnp.exp(-summed)
    tail = jnp.exp(ends - summed) * (docs_ref[:, 3:4] == docs_ref[:, 5:6]).astype(F32)
    grow_ref[:, :head] = grow
    grow_ref[:, head : 2 * head] = shrink
    grow_ref[:, 2 * head :] = tail
    key_grow, key_shrink, query_grow, key_tail = keys * grow, keys * shrink, query * grow, keys * tail
    both = mm_nt(jnp.concatenate([key_grow, query_grow]), key_shrink)
    lower = jnp.where(strict, both[:length], 0.0) * beta
    scores = jnp.where(inclusive, both[length:], 0.0)
    score_ref[...] = scores
    inverse = (row == col).astype(F32) - jnp.where(row // 2 == col // 2, lower, 0.0)
    size = 2
    while size < BLOCK:
        corner = jnp.where((row // (2 * size) == col // (2 * size)) & (row // size != col // size), lower, 0.0)
        inverse = inverse - mm(inverse, mm(corner, inverse))
        size *= 2
    inv_ref[...] = inverse
    wu = mm(inverse, jnp.concatenate([beta * carried * key_grow, beta * values], axis=1))
    wu_ref[...] = wu
    mixed = mm(scores, wu)
    qo_ref[:, :head] = carried * query_grow - mixed[:, :head]
    qo_ref[:, head:] = mixed[:, head:]
    eye = lax.broadcasted_iota(jnp.int32, (head, head), 0) == lax.broadcasted_iota(jnp.int32, (head, head), 1)
    pairs = []
    for b in range(count):
        rows = slice(b * BLOCK, (b + 1) * BLOCK)
        last = (b + 1) * BLOCK - 1
        keep = grow[last : last + 1] * carried[last : last + 1]
        update = mm_tn(key_tail[rows], wu[rows])
        moved = jnp.where(eye, keep, 0.0) - update[:, :head]
        maps_ref[b, :, :head] = moved
        maps_ref[b, :, head:] = update[:, head:]
        pairs.append((moved, update[:, head:]))

    def after(second, first):
        made = mm(second[0], jnp.concatenate(first, axis=1))
        return (made[:, :head], made[:, head:] + second[1])

    while len(pairs) > 1:
        pairs = [after(pairs[i + 1], pairs[i]) for i in range(0, len(pairs), 2)]
    device_map_ref[:, :head] = pairs[0][0]
    device_map_ref[:, head:] = pairs[0][1]


def mid_kernel(
    near_ref, far_ref, maps_ref, wu_ref, qo_ref, d_hidden_ref, gain_ref,
    hidden_ref, d_out_ref, pseudo_ref, states_ref, from_out_ref, d_enter_ref,
):
    length, head = d_hidden_ref.shape
    count = length // BLOCK
    state = near_ref[:, head:] + mm(near_ref[:, :head], far_ref[...])
    states = []
    for b in range(count):
        states.append(state)
        states_ref[b] = state
        if b < count - 1:
            state = mm(maps_ref[b, :, :head], state) + maps_ref[b, :, head:]
    outs, pseudos = [], []
    for b in range(count):
        rows = slice(b * BLOCK, (b + 1) * BLOCK)
        made = mm(jnp.concatenate([qo_ref[rows, :head], wu_ref[rows, :head]]), states[b])
        outs.append(qo_ref[rows, head:] + made[:BLOCK])
        pseudos.append(wu_ref[rows, head:] - made[BLOCK:])
    out = jnp.concatenate(outs)
    pseudo_ref[...] = jnp.concatenate(pseudos)
    scale = lax.rsqrt(jnp.mean(out * out, axis=1, keepdims=True) + 1e-5)
    hidden_ref[...] = (out * scale * gain_ref[...]).astype(BF16)
    lifted = d_hidden_ref[...] * gain_ref[...]
    d_out = scale * lifted - out * (scale * scale * scale) * jnp.mean(lifted * out, axis=1, keepdims=True)
    d_out_ref[...] = d_out
    d_state = None
    for b in reversed(range(count)):
        rows = slice(b * BLOCK, (b + 1) * BLOCK)
        part = mm_tn(qo_ref[rows, :head], d_out[rows])
        from_out_ref[b] = part
        d_state = part if d_state is None else part + mm_tn(maps_ref[b, :, :head], d_state)
    d_enter_ref[...] = d_state


def share_kernel(place_ref, hidden_ref, upstream_ref, *refs):
    pieces, (share_ref, last_ref) = refs[:-2], refs[-2:]
    size, here = upstream_ref.shape[1], upstream_ref.shape[3]
    head = hidden_ref.shape[1]
    for k, piece in enumerate(pieces):
        index = lax.rem(place_ref[0] + offset_of(k) + size, size)
        weights = piece[:, 3 * head :]
        total = jnp.zeros((piece.shape[0], head), F32)
        for c in range(2):
            part = hidden_ref[c * here : (c + 1) * here]
            share_ref[c, index] = lax.dot_general(
                weights, part, (((1,), (1,)), ((), ())), preferred_element_type=F32
            )
            total = total + jnp.dot(upstream_ref[c, k], part, preferred_element_type=F32)
        last_ref[k] = total


def post_kernel(
    near_ref, far_ref, far_map_ref, maps_ref, from_out_ref, states_ref, pseudo_ref, d_out_ref, inv_ref, score_ref,
    grow_ref, total_ref, gates_ref, docs_ref, doc_row_ref, conv_ref,
    d_proj_ref, power_ref,
    d_ext_ref,
):
    length, head = d_out_ref.shape
    count = length // BLOCK
    d_state = near_ref[...] + mm_tn(far_map_ref[...], far_ref[...])
    d_after = [None] * count
    for b in reversed(range(count)):
        d_after[b] = d_state
        if b > 0:
            d_state = from_out_ref[b] + mm_tn(maps_ref[b, :, :head], d_state)
    total = total_ref[...]
    gate = jax.nn.sigmoid(total)
    active = total * gate
    raw_q, raw_k = active[:, :head], active[:, head : 2 * head]
    inv_q = lax.rsqrt(jnp.sum(raw_q * raw_q, axis=1, keepdims=True) + 1e-6)
    inv_k = lax.rsqrt(jnp.sum(raw_k * raw_k, axis=1, keepdims=True) + 1e-6)
    query, keys = raw_q * inv_q, raw_k * inv_k
    grow, shrink, tail = grow_ref[:, :head], grow_ref[:, head : 2 * head], grow_ref[:, 2 * head :]
    key_grow, key_shrink, query_grow, key_tail = keys * grow, keys * shrink, query * grow, keys * tail
    beta = jax.nn.sigmoid(gates_ref[:, head : head + 1])
    _, _, _, inclusive, strict = masks(docs_ref, doc_row_ref)
    carried = carried_of(docs_ref)
    d_out, pseudo = d_out_ref[...], pseudo_ref[...]

    def each(function):
        return jnp.concatenate([function(b, slice(b * BLOCK, (b + 1) * BLOCK)) for b in range(count)])

    d_pseudo = mm_tn(score_ref[...], d_out) + each(lambda b, rows: mm(key_tail[rows], d_after[b]))
    d_target = mm_tn(inv_ref[...], d_pseudo)
    both = mm_nt(jnp.concatenate([d_out, d_target]), pseudo)
    d_scores = jnp.where(inclusive, both[:length], 0.0)
    d_lower = jnp.where(strict, both[length:], 0.0) * (-beta)
    d_values = beta * d_target
    d_from_keys = -carried * d_values
    lifted_out = carried * d_out
    d_query_grow = each(lambda b, rows: mm_nt(lifted_out[rows], states_ref[b])) + mm(d_scores, key_shrink)
    d_key_grow = each(lambda b, rows: mm_nt(d_from_keys[rows], states_ref[b])) + mm(d_lower, key_shrink)
    d_key_shrink = mm_tn(d_scores, query_grow) + mm_tn(d_lower, key_grow)
    d_key_tail = each(lambda b, rows: mm_nt(pseudo[rows], d_after[b]))
    d_query = d_query_grow * grow
    d_keys = d_key_grow * grow + d_key_shrink * shrink + d_key_tail * tail
    d_query = inv_q * d_query - query * (inv_q * jnp.sum(d_query * query, axis=1, keepdims=True))
    d_keys = inv_k * d_keys - keys * (inv_k * jnp.sum(d_keys * keys, axis=1, keepdims=True))
    d_total = jnp.concatenate([d_query, d_keys, d_values], axis=1) * (gate * (1.0 + total * (1.0 - gate)))
    d_ext_ref[...] = jnp.zeros_like(d_ext_ref)
    for j in range(TAPS):
        same = (docs_ref[:, j : j + 1] == docs_ref[:, 3:4]).astype(F32)
        spot = slice(HALO - 3 + j, HALO - 3 + j + length)
        d_ext_ref[spot] = d_ext_ref[spot] + d_total * conv_ref[j : j + 1] * same
    d_proj_ref[:length] = d_ext_ref[HALO:].astype(BF16)
    d_proj_ref[length:] = d_ext_ref[:HALO].astype(BF16)
    most = jnp.max(jnp.abs(d_ext_ref[...]), axis=0, keepdims=True) * (TOKEN_MOST * 1.01 * (length + HALO))
    power = jnp.ceil(jnp.log(jnp.maximum(most, 1e-30)) * 1.4426950408889634 + 0.01)
    power_ref[:, : 3 * head] = jnp.broadcast_to(power, (8, 3 * head))
    power_ref[:, 3 * head :] = jnp.full((8, head), LAST_POWER, F32)


def call(kernel, outs, *args, scratch=()):
    def spec(arg):
        return pl.BlockSpec(memory_space=pltpu.SMEM if arg.dtype == jnp.int32 else pltpu.VMEM)

    return pl.pallas_call(
        kernel,
        out_shape=tuple(jax.ShapeDtypeStruct(shape, dtype) for shape, dtype in outs),
        in_specs=[spec(arg) for arg in args],
        out_specs=tuple(pl.BlockSpec(memory_space=pltpu.VMEM) for _ in outs),
        scratch_shapes=list(scratch),
        compiler_params=pltpu.CompilerParams(vmem_limit_bytes=VMEM_LIMIT),
    )(*args)


def pack(total, power):
    scaled = (total * jnp.exp2(TOP - power)).astype(F16)
    return jnp.concatenate([scaled, jnp.broadcast_to(power, (16, total.shape[1])).astype(F16)])


def unpack(packed):
    power = packed[-16:-15].astype(F32)
    return packed[:-16].astype(F32) * jnp.exp2(power - TOP), power


def swap(array, axis):
    return lax.ppermute(array, axis, [(0, 1), (1, 0)])


def turn(array, axis, by):
    size = lax.axis_size(axis)
    return lax.ppermute(array, axis, [(i, (i + by) % size) for i in range(size)])


def shift(array, axis, by):
    size = lax.axis_size(axis)
    return lax.ppermute(array, axis, [(i, i + by) for i in range(size) if 0 <= i + by < size])


def ordered(mine, other, index):
    return jnp.where(index == 0, jnp.stack([mine, other]), jnp.stack([other, mine]))


def pick(array, index):
    return lax.dynamic_index_in_dim(array, index, 0, keepdims=False)


def put(array, piece, index):
    return lax.dynamic_update_index_in_dim(array, piece, index, 0)


def outer(a, b):
    return lax.dot_general(a, b, (((0,), (0,)), ((), ())), preferred_element_type=F32)


def per_device(
    tokens, cotangent, doc_ids, projections, conv_weight, gate_down, gate_up, decay_log, beta_weight, norm_gain
):
    z, core, x, ylo, roll = (lax.axis_index(a) for a in ("z", "core", "x", "ylo", "roll"))
    nz, nx = lax.axis_size("z"), lax.axis_size("x")
    here, width = tokens.shape[1], tokens.shape[2]
    head = norm_gain.shape[0]
    rows = projections.shape[0]
    length = 2 * here
    span = 4 * rows

    split = projections.reshape(rows, 4, 2, head)
    mine = lax.dynamic_index_in_dim(split, core, 2, keepdims=False).reshape(rows, 4 * head)
    theirs = lax.dynamic_index_in_dim(split, 1 - core, 2, keepdims=False).reshape(rows, 4 * head)
    chip_rows = ordered(mine, swap(theirs, "core"), core)
    piece = jnp.swapaxes(ordered(chip_rows, swap(chip_rows, "roll"), roll), 0, 1).reshape(span, 4 * head)

    block = jnp.stack([tokens[0].T, cotangent[0].T])
    pair = ordered(block, swap(block, "ylo"), ylo)
    full = jnp.zeros((nx,) + pair.shape, pair.dtype)
    full = put(full, pair, x)
    for by in (1, -1, 2):
        full = put(full, turn(pair, "x", by), (x - by) % nx)
    features, upstream = (full[:, :, i].reshape(-1, here) for i in range(2))
    model = features.shape[0]
    doc_row = jnp.broadcast_to((doc_ids + 1).astype(BF16), (16, here))
    own = jnp.concatenate([features, doc_row])
    both_cores = ordered(own, swap(own, "core"), core)
    chip = jnp.concatenate([both_cores[0], both_cores[1]], axis=1)
    halo = shift(chip[:, length - HALO :].T, "z", 1)
    features = chip[:model]
    upstream = ordered(upstream, swap(upstream, "core"), core).reshape(2, nz, span, here)
    docs = chip[model].astype(F32)
    doc_ext = jnp.concatenate([halo[HALO - 3 :, model].astype(F32), docs])
    prior = jnp.repeat(doc_ext[2 : 2 + length : BLOCK], BLOCK)
    last = jnp.repeat(docs[BLOCK - 1 :: BLOCK], BLOCK)
    doc_columns = jnp.stack([doc_ext[j : j + length] for j in range(TAPS)] + [prior, last, docs, docs], axis=1)
    extended = jnp.concatenate([features, halo[:, :model].T], axis=1)

    beta_column = lax.dynamic_index_in_dim(beta_weight, core, 1)
    gate_weights = jnp.concatenate([gate_down, jnp.pad(beta_column, ((0, 0), (0, head - 1)))], axis=1)
    gate_up = lax.dynamic_index_in_dim(gate_up.reshape(-1, 2, head), core, 1, keepdims=False)
    rate = jnp.broadcast_to(jnp.exp(pick(decay_log, core)), (1, head))
    conv = lax.dynamic_index_in_dim(conv_weight.reshape(3, TAPS, 2, head), core, 2, keepdims=False)
    conv = jnp.swapaxes(conv, 0, 1).reshape(TAPS, 3 * head)

    place = z.astype(jnp.int32).reshape(1)
    blocks = extended.reshape(nz, span, length + HALO)
    arrived = [piece]
    right = left = piece
    for k in range(1, nz // 2 + 1):
        right = turn(right, "z", 1)
        arrived.append(right)
        if k < nz // 2:
            left = turn(left, "z", -1)
            arrived.append(left)
    projected, d_hidden, gates = call(
        gather_kernel,
        [((length + HALO, 3 * head), F32), ((length, head), F32), ((length, 2 * head), F32)],
        place, blocks, upstream, gate_weights.reshape(nz, span, 2 * head), *arrived[:-1],
    )
    total, grow, inverse, scores, wu, qo, maps, device_map, d_hidden = call(
        pre_kernel,
        [
            ((length, 3 * head), F32), ((length, 3 * head), F32), ((length, length), F32), ((length, length), F32),
            ((length, 2 * head), F32), ((length, 2 * head), F32), ((length // BLOCK, head, 2 * head), F32),
            ((head, 2 * head), F32), ((length, head), F32),
        ],
        place, blocks, upstream, arrived[-1], projected, d_hidden, gates, gate_up, rate, conv, doc_columns, docs[None],
        scratch=[pltpu.VMEM((length + HALO, 3 * head), F32)],
    )

    one, two = shift(device_map, "z", 1), shift(device_map, "z", 2)
    joined = product(one[:, :head], two, (1, 0), HIGH)
    near = jnp.concatenate([joined[:, :head], joined[:, head:] + one[:, head:]], axis=1)
    far = shift(near[:, head:], "z", 2)
    far_map = shift(near[:, :head], "z", -3)
    hidden, d_out, pseudo, states, from_out, d_enter = call(
        mid_kernel,
        [
            ((length, head), BF16), ((length, head), F32), ((length, head), F32), ((length // BLOCK, head, head), F32),
            ((length // BLOCK, head, head), F32), ((head, head), F32),
        ],
        near, far, maps, wu, qo, d_hidden, norm_gain[None],
    )
    share, last = call(
        share_kernel,
        [((2, nz, span, here), F32), ((nz, span, head), F32)],
        place, hidden, upstream, *arrived,
    )
    from_core = swap((pick(share, 1 - core) * LIFT).astype(F16), "core")

    d_two = d_enter + lax.dot_general(
        device_map[:, :head], shift(d_enter, "z", -1), (((0,), (0,)), ((), ())), precision=HIGH
    )
    d_near, d_far = shift(d_two, "z", -1), shift(d_two, "z", -3)
    d_projected, power = call(
        post_kernel,
        [((length + HALO, 3 * head), BF16), ((8, 4 * head), F32)],
        d_near, d_far, far_map, maps, from_out, states, pseudo, d_out, inverse, scores, grow, total, gates, doc_columns,
        docs[None], conv,
        scratch=[pltpu.VMEM((length + HALO, 3 * head), F32)],
    )

    own_power = power[:1]

    def part(by):
        index = (z + by) % nz
        first = jnp.dot(pick(blocks, index), d_projected, preferred_element_type=F32)
        return jnp.concatenate([first, pick(last, index)], axis=1)

    def add(packed, by):
        total, power = unpack(packed)
        return total + part(by), jnp.maximum(power, own_power) + 1.0

    half = nz // 2
    right = turn(pack(part(half), own_power), "z", 1)
    left = turn(pack(part(1 - half), own_power), "z", -1)
    right, left, from_core = lax.optimization_barrier((right, left, from_core))
    right = turn(pack(*add(right, half - 1)), "z", 1)
    left = turn(pack(*add(left, 2 - half)), "z", -1)
    shared = (pick(share, core) * LIFT + from_core.astype(F32)).reshape(nx, 2, span, here)
    from_ylo = swap(lax.dynamic_index_in_dim(shared, 1 - ylo, 1, keepdims=False).astype(F16), "ylo")
    right, left, from_ylo = lax.optimization_barrier((right, left, from_ylo))
    for k in range(2, half):
        right = turn(pack(*add(right, half - k)), "z", 1)
        if k < half - 1:
            left = turn(pack(*add(left, 1 - half + k)), "z", -1)
        if k == 2:
            shared = lax.dynamic_index_in_dim(shared, ylo, 1, keepdims=False) + from_ylo.astype(F32)
            from_x = [turn(pick(shared, (x + by) % nx).astype(F16), "x", by) for by in (1, -1, 2)]
        right, left, *from_x = lax.optimization_barrier((right, left, *from_x))
    layer_out = ((pick(shared, x) + sum(f.astype(F32) for f in from_x)) * (1.0 / LIFT)).T.astype(BF16)[None]
    total, power = add(right, 0)
    more, more_power = unpack(left)
    packed = pack(total + more, jnp.maximum(power, more_power) + 1.0)
    grad = unpack(packed)[0] + unpack(swap(packed, "roll"))[0]
    fresh = (piece.astype(F32) - RATE * grad).astype(BF16).reshape(2, span // 2, 4 * head)
    kept, sent = pick(fresh, core), pick(fresh, 1 - core)
    heads = ordered(kept, swap(sent, "core"), core).reshape(2, span // 2, 4, head)
    engine_tiles = jnp.moveaxis(heads, 0, 2).reshape(span // 2, 4, 2 * head)
    return (layer_out, engine_tiles)


def solution(mesh):
    fine = Mesh(mesh.devices.reshape(8, 2, 4, 2, 2), ("z", "core", "x", "ylo", "roll"))
    seq, mp = ("z", "core"), ("x", "ylo")
    in_specs = (
        P("roll", seq, mp),
        P("roll", seq, mp),
        P("roll", seq),
        P(("z", "core", "roll"), None, mp),
        P(None, None, mp),
        P(),
        P(None, mp),
        P(mp),
        P(None, mp),
        P(),
    )
    out_specs = (P("roll", seq, mp), P(seq, None, mp))
    return jax.shard_map(per_device, mesh=fine, in_specs=in_specs, out_specs=out_specs, check_vma=False)
```

```python
import jax
import jax.numpy as jnp
from jax import lax
from jax.experimental import pallas as pl
from jax.experimental.pallas import tpu as pltpu
from jax.sharding import Mesh
from jax.sharding import PartitionSpec as P

BLOCK = 64
TAPS = 4
HALO = 16
RATE = 0.01
TOKEN_MOST = 6.0
LAST_POWER = 16.0
TOP = 15.0
LIFT = 8.0
F32 = jnp.float32
F16 = jnp.float16
BF16 = jnp.bfloat16
HIGH = lax.Precision.HIGHEST
VMEM_LIMIT = 56 * 1024 * 1024


def product(a, b, dims, precision=None):
    return lax.dot_general(a, b, ((dims[:1], dims[1:]), ((), ())), precision=precision, preferred_element_type=F32)


def halves(a):
    high = a.astype(BF16)
    return high, (a - high.astype(F32)).astype(BF16)


def split_product(a, b, dims):
    (a_high, a_low), (b_high, b_low) = halves(a), halves(b)
    return product(a_high, b_high, dims) + (product(a_high, b_low, dims) + product(a_low, b_high, dims))


def mm(a, b):
    return split_product(a, b, (1, 0))


def mm_nt(a, b):
    return split_product(a, b, (1, 1))


def mm_tn(a, b):
    return mm(a.T, b)


def softplus(x):
    return jnp.maximum(x, 0.0) + jnp.log1p(jnp.exp(-jnp.abs(x)))


def masks(docs_ref, doc_row_ref):
    length = docs_ref.shape[0]
    row = lax.broadcasted_iota(jnp.int32, (length, length), 0)
    col = lax.broadcasted_iota(jnp.int32, (length, length), 1)
    inside = (row // BLOCK == col // BLOCK) & (row >= col)
    paired = docs_ref[:, 3:4] == doc_row_ref[...]
    inclusive = inside & paired
    strict = inclusive & (row > col)
    return row, col, inside, inclusive, strict


def carried_of(docs_ref):
    return (docs_ref[:, 3:4] == docs_ref[:, 4:5]).astype(F32)


def own_rows(core, here, skip=0):
    return pl.ds(pl.multiple_of(skip + core * here, 16), here)


def offset_of(k):
    return ((k + 1) // 2) * (-1 if k % 2 else 1)


def index_of(place_ref, k, size):
    return lax.rem(place_ref[0] + offset_of(k) + size, size)


def gather_kernel(
    place_ref, features_ref, up_ref, up_other_ref, gate_weights_ref, gate_up_ref, rate_ref, docs_ref, *refs
):
    pieces, (proj_ref, d_hidden_ref, grow_ref, beta_ref, decay_ref) = refs[:-5], refs[-5:]
    size, here, head = features_ref.shape[0], up_ref.shape[2], d_hidden_ref.shape[1]
    length, count = 2 * here, 2 * here // BLOCK
    proj = jnp.zeros(proj_ref.shape, F32)
    d_hidden = jnp.zeros(d_hidden_ref.shape, F32)
    gates = jnp.zeros((length, 2 * head), F32)
    for k in range(size):
        index = index_of(place_ref, k, size)
        rows = features_ref[index].T
        gates = gates + jnp.dot(rows[:length], gate_weights_ref[index], preferred_element_type=F32)
        if k < len(pieces):
            both = jnp.concatenate([up_ref[index].T, up_other_ref[index].T])
            proj = proj + jnp.dot(rows, pieces[k][:, : 3 * head], preferred_element_type=F32)
            d_hidden = d_hidden + jnp.dot(both, pieces[k][:, 3 * head :], preferred_element_type=F32)
    proj_ref[...] = proj
    d_hidden_ref[...] = d_hidden
    low = gates[:, :head].astype(BF16)
    rates = jnp.dot(low, gate_up_ref[...], preferred_element_type=F32)
    log_decay = -rate_ref[...] * softplus(rates)
    beta = jnp.broadcast_to(jax.nn.sigmoid(gates[:, head : head + 1]), (length, head))
    core = place_ref[1]
    for ref, array in ((decay_ref, log_decay), (beta_ref, beta)):
        ref[own_rows(core, here)] = array[:here]
        ref[own_rows(1 - core, here)] = array[here:]
    row = lax.broadcasted_iota(jnp.int32, (length, length), 0)
    col = lax.broadcasted_iota(jnp.int32, (length, length), 1)
    inside = (row // BLOCK == col // BLOCK) & (row >= col)
    summed = product(inside.astype(F32), decay_ref[...], (1, 0), HIGH)
    ends = jnp.concatenate(
        [jnp.broadcast_to(summed[b * BLOCK + BLOCK - 1 : (b + 1) * BLOCK], (BLOCK, head)) for b in range(count)]
    )
    grow_ref[:, :head] = jnp.exp(summed)
    grow_ref[:, head : 2 * head] = jnp.exp(-summed)
    same = (docs_ref[:, 3:4] == docs_ref[:, 5:6]).astype(F32)
    grow_ref[:, 2 * head :] = jnp.exp(ends - summed) * same


def pre_kernel(
    place_ref, features_ref, up_ref, up_other_ref, piece_ref, proj_in_ref, d_hidden_in_ref,
    grow_ref, beta_ref, conv_ref, docs_ref, doc_row_ref,
    total_ref, inv_ref, score_ref, wu_ref, qo_ref, maps_ref, device_map_ref, device_map16_ref, d_hidden_ref,
    ext_ref,
):
    length, head = d_hidden_ref.shape
    here, count = length // 2, length // BLOCK
    size, core = features_ref.shape[0], place_ref[1]
    index = index_of(place_ref, size - 1, size)
    proj = proj_in_ref[...] + jnp.dot(features_ref[index].T, piece_ref[:, : 3 * head], preferred_element_type=F32)
    both = jnp.concatenate([up_ref[index].T, up_other_ref[index].T])
    d_hidden = d_hidden_in_ref[...] + jnp.dot(both, piece_ref[:, 3 * head :], preferred_element_type=F32)
    d_hidden_ref[own_rows(core, here)] = d_hidden[:here]
    d_hidden_ref[own_rows(1 - core, here)] = d_hidden[here:]
    ext_ref[:HALO] = proj[length:]
    ext_ref[own_rows(core, here, HALO)] = proj[:here]
    ext_ref[own_rows(1 - core, here, HALO)] = proj[here:length]
    total = jnp.zeros((length, 3 * head), F32)
    for j in range(TAPS):
        same = (docs_ref[:, j : j + 1] == docs_ref[:, 3:4]).astype(F32)
        total = total + ext_ref[HALO - 3 + j : HALO - 3 + j + length] * conv_ref[j : j + 1] * same
    total_ref[...] = total
    active = total * jax.nn.sigmoid(total)
    query, keys, values = active[:, :head], active[:, head : 2 * head], active[:, 2 * head :]
    query = query * lax.rsqrt(jnp.sum(query * query, axis=1, keepdims=True) + 1e-6)
    keys = keys * lax.rsqrt(jnp.sum(keys * keys, axis=1, keepdims=True) + 1e-6)
    beta = beta_ref[:, :1]
    row, col, _, inclusive, strict = masks(docs_ref, doc_row_ref)
    carried = carried_of(docs_ref)
    grow, shrink, tail = grow_ref[:, :head], grow_ref[:, head : 2 * head], grow_ref[:, 2 * head :]
    key_grow, key_shrink, query_grow, key_tail = keys * grow, keys * shrink, query * grow, keys * tail
    both = mm_nt(jnp.concatenate([key_grow, query_grow]), key_shrink)
    lower = jnp.where(strict, both[:length], 0.0) * beta
    scores = jnp.where(inclusive, both[length:], 0.0)
    score_ref[...] = scores
    inverse = (row == col).astype(F32) - jnp.where(row // 2 == col // 2, lower, 0.0)
    size = 2
    while size < BLOCK:
        corner = jnp.where((row // (2 * size) == col // (2 * size)) & (row // size != col // size), lower, 0.0)
        inverse = inverse - mm(inverse, mm(corner, inverse))
        size *= 2
    inv_ref[...] = inverse
    wu = mm(inverse, jnp.concatenate([beta * carried * key_grow, beta * values], axis=1))
    wu_ref[...] = wu
    mixed = mm(scores, wu)
    qo_ref[:, :head] = carried * query_grow - mixed[:, :head]
    qo_ref[:, head:] = mixed[:, head:]
    eye = lax.broadcasted_iota(jnp.int32, (head, head), 0) == lax.broadcasted_iota(jnp.int32, (head, head), 1)
    pairs = []
    for b in range(count):
        rows = slice(b * BLOCK, (b + 1) * BLOCK)
        last = (b + 1) * BLOCK - 1
        keep = grow[last : last + 1] * carried[last : last + 1]
        update = mm_tn(key_tail[rows], wu[rows])
        moved = jnp.where(eye, keep, 0.0) - update[:, :head]
        maps_ref[b, :, :head] = moved
        maps_ref[b, :, head:] = update[:, head:]
        pairs.append((moved, update[:, head:]))

    def after(second, first):
        made = mm(second[0], jnp.concatenate(first, axis=1))
        return (made[:, :head], made[:, head:] + second[1])

    while len(pairs) > 1:
        pairs = [after(pairs[i + 1], pairs[i]) for i in range(0, len(pairs), 2)]
    device_map_ref[:, :head] = pairs[0][0]
    device_map_ref[:, head:] = pairs[0][1]
    device_map16_ref[:, :head] = pairs[0][0].astype(BF16)
    device_map16_ref[:, head:] = pairs[0][1].astype(BF16)


def mid_kernel(
    near_ref, far_ref, maps_ref, wu_ref, qo_ref, d_hidden_ref, gain_ref,
    hidden_ref, d_out_ref, pseudo_ref, states_ref, from_out_ref, d_enter_ref,
):
    length, head = d_hidden_ref.shape
    count = length // BLOCK
    state = near_ref[:, head:] + mm(near_ref[:, :head], far_ref[...].astype(F32))
    states = []
    for b in range(count):
        states.append(state)
        states_ref[b] = state
        if b < count - 1:
            state = mm(maps_ref[b, :, :head], state) + maps_ref[b, :, head:]
    outs, pseudos = [], []
    for b in range(count):
        rows = slice(b * BLOCK, (b + 1) * BLOCK)
        made = mm(jnp.concatenate([qo_ref[rows, :head], wu_ref[rows, :head]]), states[b])
        outs.append(qo_ref[rows, head:] + made[:BLOCK])
        pseudos.append(wu_ref[rows, head:] - made[BLOCK:])
    out = jnp.concatenate(outs)
    pseudo_ref[...] = jnp.concatenate(pseudos)
    scale = lax.rsqrt(jnp.mean(out * out, axis=1, keepdims=True) + 1e-5)
    hidden_ref[...] = (out * scale * gain_ref[...]).astype(BF16)
    lifted = d_hidden_ref[...] * gain_ref[...]
    d_out = scale * lifted - out * (scale * scale * scale) * jnp.mean(lifted * out, axis=1, keepdims=True)
    d_out_ref[...] = d_out
    d_state = None
    for b in reversed(range(count)):
        rows = slice(b * BLOCK, (b + 1) * BLOCK)
        part = mm_tn(qo_ref[rows, :head], d_out[rows])
        from_out_ref[b] = part
        d_state = part if d_state is None else part + mm_tn(maps_ref[b, :, :head], d_state)
    d_enter_ref[...] = d_state


def share_kernel(place_ref, hidden_ref, up_ref, up_other_ref, *refs):
    pieces, (share_ref, last_ref) = refs[:-2], refs[-2:]
    size, here, head = up_ref.shape[0], up_ref.shape[2], hidden_ref.shape[1]
    core = place_ref[1]
    own, other = hidden_ref[own_rows(core, here)], hidden_ref[own_rows(1 - core, here)]
    for k, piece in enumerate(pieces):
        index = index_of(place_ref, k, size)
        for c in range(2):
            share_ref[c, index] = lax.dot_general(
                piece[:, 3 * head :], hidden_ref[c * here : (c + 1) * here], (((1,), (1,)), ((), ())),
                preferred_element_type=F32,
            )
        last_ref[k] = jnp.dot(up_ref[k], own, preferred_element_type=F32) + jnp.dot(
            up_other_ref[k], other, preferred_element_type=F32
        )


def post_kernel(
    place_ref, near_ref, far_ref, far_map_ref, maps_ref, from_out_ref, states_ref, pseudo_ref, d_out_ref, inv_ref,
    score_ref, grow_ref, total_ref, beta_ref, docs_ref, doc_row_ref, conv_ref,
    d_proj_ref, power_ref,
    d_ext_ref,
):
    length, head = d_out_ref.shape
    count = length // BLOCK
    core, here = place_ref[1], length // 2
    d_state = near_ref[...] + lax.dot_general(
        far_map_ref[...].T, far_ref[...], (((1,), (0,)), ((), ())), preferred_element_type=F32
    )
    d_after = [None] * count
    for b in reversed(range(count)):
        d_after[b] = d_state
        if b > 0:
            d_state = from_out_ref[b] + mm_tn(maps_ref[b, :, :head], d_state)
    total = total_ref[...]
    gate = jax.nn.sigmoid(total)
    active = total * gate
    raw_q, raw_k = active[:, :head], active[:, head : 2 * head]
    inv_q = lax.rsqrt(jnp.sum(raw_q * raw_q, axis=1, keepdims=True) + 1e-6)
    inv_k = lax.rsqrt(jnp.sum(raw_k * raw_k, axis=1, keepdims=True) + 1e-6)
    query, keys = raw_q * inv_q, raw_k * inv_k
    grow, shrink, tail = grow_ref[:, :head], grow_ref[:, head : 2 * head], grow_ref[:, 2 * head :]
    key_grow, key_shrink, query_grow, key_tail = keys * grow, keys * shrink, query * grow, keys * tail
    beta = beta_ref[:, :1]
    _, _, _, inclusive, strict = masks(docs_ref, doc_row_ref)
    carried = carried_of(docs_ref)
    d_out, pseudo = d_out_ref[...], pseudo_ref[...]

    def each(function):
        return jnp.concatenate([function(b, slice(b * BLOCK, (b + 1) * BLOCK)) for b in range(count)])

    d_pseudo = mm_tn(score_ref[...], d_out) + each(lambda b, rows: mm(key_tail[rows], d_after[b]))
    d_target = mm_tn(inv_ref[...], d_pseudo)
    both = mm_nt(jnp.concatenate([d_out, d_target]), pseudo)
    d_scores = jnp.where(inclusive, both[:length], 0.0)
    d_lower = jnp.where(strict, both[length:], 0.0) * (-beta)
    d_values = beta * d_target
    d_from_keys = -carried * d_values
    lifted_out = carried * d_out
    d_query_grow = each(lambda b, rows: mm_nt(lifted_out[rows], states_ref[b])) + mm(d_scores, key_shrink)
    d_key_grow = each(lambda b, rows: mm_nt(d_from_keys[rows], states_ref[b])) + mm(d_lower, key_shrink)
    d_key_shrink = mm_tn(d_scores, query_grow) + mm_tn(d_lower, key_grow)
    d_key_tail = each(lambda b, rows: mm_nt(pseudo[rows], d_after[b]))
    d_query = d_query_grow * grow
    d_keys = d_key_grow * grow + d_key_shrink * shrink + d_key_tail * tail
    d_query = inv_q * d_query - query * (inv_q * jnp.sum(d_query * query, axis=1, keepdims=True))
    d_keys = inv_k * d_keys - keys * (inv_k * jnp.sum(d_keys * keys, axis=1, keepdims=True))
    d_total = jnp.concatenate([d_query, d_keys, d_values], axis=1) * (gate * (1.0 + total * (1.0 - gate)))
    d_ext_ref[...] = jnp.zeros_like(d_ext_ref)
    for j in range(TAPS):
        same = (docs_ref[:, j : j + 1] == docs_ref[:, 3:4]).astype(F32)
        spot = slice(HALO - 3 + j, HALO - 3 + j + length)
        d_ext_ref[spot] = d_ext_ref[spot] + d_total * conv_ref[j : j + 1] * same
    d_proj_ref[:here] = d_ext_ref[own_rows(core, here, HALO)].astype(BF16)
    d_proj_ref[here:length] = d_ext_ref[own_rows(1 - core, here, HALO)].astype(BF16)
    d_proj_ref[length:] = d_ext_ref[:HALO].astype(BF16)
    most = jnp.max(jnp.abs(d_ext_ref[...]), axis=0, keepdims=True) * (TOKEN_MOST * 1.01 * (length + HALO))
    power = jnp.ceil(jnp.log(jnp.maximum(most, 1e-30)) * 1.4426950408889634 + 0.01)
    power_ref[:, : 3 * head] = jnp.broadcast_to(power, (8, 3 * head))
    power_ref[:, 3 * head :] = jnp.full((8, head), LAST_POWER, F32)


def call(kernel, outs, *args, scratch=()):
    def spec(arg):
        return pl.BlockSpec(memory_space=pltpu.SMEM if arg.dtype == jnp.int32 else pltpu.VMEM)

    return pl.pallas_call(
        kernel,
        out_shape=tuple(jax.ShapeDtypeStruct(shape, dtype) for shape, dtype in outs),
        in_specs=[spec(arg) for arg in args],
        out_specs=tuple(pl.BlockSpec(memory_space=pltpu.VMEM) for _ in outs),
        scratch_shapes=list(scratch),
        compiler_params=pltpu.CompilerParams(vmem_limit_bytes=VMEM_LIMIT),
    )(*args)


def pack(total, power):
    scaled = (total * jnp.exp2(TOP - power)).astype(F16)
    return jnp.concatenate([scaled, jnp.broadcast_to(power, (16, total.shape[1])).astype(F16)])


def unpack(packed):
    power = packed[-16:-15].astype(F32)
    return packed[:-16].astype(F32) * jnp.exp2(power - TOP), power


def swap(array, axis):
    return lax.ppermute(array, axis, [(0, 1), (1, 0)])


def turn(array, axis, by):
    size = lax.axis_size(axis)
    return lax.ppermute(array, axis, [(i, (i + by) % size) for i in range(size)])


def shift(array, axis, by):
    size = lax.axis_size(axis)
    return lax.ppermute(array, axis, [(i, i + by) for i in range(size) if 0 <= i + by < size])


def ordered(mine, other, index):
    return jnp.where(index == 0, jnp.stack([mine, other]), jnp.stack([other, mine]))


def pick(array, index):
    return lax.dynamic_index_in_dim(array, index, 0, keepdims=False)


def put(array, piece, index):
    return lax.dynamic_update_index_in_dim(array, piece, index, 0)


def outer(a, b):
    return lax.dot_general(a, b, (((0,), (0,)), ((), ())), preferred_element_type=F32)


def per_device(
    tokens, cotangent, doc_ids, projections, conv_weight, gate_down, gate_up, decay_log, beta_weight, norm_gain
):
    z, core, x, ylo, roll = (lax.axis_index(a) for a in ("z", "core", "x", "ylo", "roll"))
    nz, nx = lax.axis_size("z"), lax.axis_size("x")
    here, width = tokens.shape[1], tokens.shape[2]
    head = norm_gain.shape[0]
    rows = projections.shape[0]
    length = 2 * here
    span = 4 * rows

    split = projections.reshape(rows, 4, 2, head)
    mine = lax.dynamic_index_in_dim(split, core, 2, keepdims=False).reshape(rows, 4 * head)
    theirs = lax.dynamic_index_in_dim(split, 1 - core, 2, keepdims=False).reshape(rows, 4 * head)
    chip_rows = ordered(mine, swap(theirs, "core"), core)
    piece = jnp.swapaxes(ordered(chip_rows, swap(chip_rows, "roll"), roll), 0, 1).reshape(span, 4 * head)

    block = jnp.stack([tokens[0].T, cotangent[0].T])
    pair = ordered(block, swap(block, "ylo"), ylo)
    full = jnp.zeros((nx,) + pair.shape, pair.dtype)
    full = put(full, pair, x)
    for by in (1, -1, 2):
        full = put(full, turn(pair, "x", by), (x - by) % nx)
    features, upstream = (full[:, :, i].reshape(-1, here) for i in range(2))
    model = features.shape[0]
    doc_row = jnp.broadcast_to((doc_ids + 1).astype(BF16), (16, here))
    own = jnp.concatenate([features, doc_row])
    other = swap(own, "core")
    up_other = swap(upstream, "core")
    halo = shift(jnp.where(core == 1, own[:, here - HALO :], other[:, here - HALO :]).T, "z", 1)
    docs = ordered(own[model], other[model], core).reshape(length).astype(F32)
    upstream, up_other = upstream.reshape(nz, span, here), up_other.reshape(nz, span, here)
    doc_ext = jnp.concatenate([halo[HALO - 3 :, model].astype(F32), docs])
    prior = jnp.repeat(doc_ext[2 : 2 + length : BLOCK], BLOCK)
    last = jnp.repeat(docs[BLOCK - 1 :: BLOCK], BLOCK)
    doc_columns = jnp.stack([doc_ext[j : j + length] for j in range(TAPS)] + [prior, last, docs, docs], axis=1)
    extended = jnp.concatenate([features, other[:model], halo[:, :model].T], axis=1)

    beta_column = lax.dynamic_index_in_dim(beta_weight, core, 1)
    gate_weights = jnp.concatenate([gate_down, jnp.pad(beta_column, ((0, 0), (0, head - 1)))], axis=1)
    gate_up = lax.dynamic_index_in_dim(gate_up.reshape(-1, 2, head), core, 1, keepdims=False)
    rate = jnp.broadcast_to(jnp.exp(pick(decay_log, core)), (1, head))
    conv = lax.dynamic_index_in_dim(conv_weight.reshape(3, TAPS, 2, head), core, 2, keepdims=False)
    conv = jnp.swapaxes(conv, 0, 1).reshape(TAPS, 3 * head)

    place = jnp.stack([z, core]).astype(jnp.int32)
    blocks = extended.reshape(nz, span, length + HALO)
    arrived = [piece]
    right = left = piece
    for k in range(1, nz // 2 + 1):
        right = turn(right, "z", 1)
        arrived.append(right)
        if k < nz // 2:
            left = turn(left, "z", -1)
            arrived.append(left)
    projected, d_hidden, grow, beta, _ = call(
        gather_kernel,
        [((length + HALO, 3 * head), F32), ((length, head), F32), ((length, 3 * head), F32)]
        + [((length, head), F32)] * 2,
        place, blocks, upstream, up_other, gate_weights.reshape(nz, span, 2 * head), gate_up, rate, doc_columns,
        *arrived[:-1],
    )
    total, inverse, scores, wu, qo, maps, device_map, device_map16, d_hidden = call(
        pre_kernel,
        [
            ((length, 3 * head), F32), ((length, length), F32), ((length, length), F32), ((length, 2 * head), F32),
            ((length, 2 * head), F32), ((length // BLOCK, head, 2 * head), F32), ((head, 2 * head), F32),
            ((head, 2 * head), BF16), ((length, head), F32),
        ],
        place, blocks, upstream, up_other, arrived[-1], projected, d_hidden, grow, beta, conv, doc_columns, docs[None],
        scratch=[pltpu.VMEM((length + HALO, 3 * head), F32)],
    )

    one, two = shift(device_map, "z", 1), shift(device_map16, "z", 2).astype(F32)
    joined = product(one[:, :head], two, (1, 0), HIGH)
    near = jnp.concatenate([joined[:, :head], joined[:, head:] + one[:, head:]], axis=1)
    far = shift(near[:, head:].astype(BF16), "z", 2)
    far_map = shift(near[:, :head].astype(BF16), "z", -3)
    hidden, d_out, pseudo, states, from_out, d_enter = call(
        mid_kernel,
        [
            ((length, head), BF16), ((length, head), F32), ((length, head), F32), ((length // BLOCK, head, head), F32),
            ((length // BLOCK, head, head), F32), ((head, head), F32),
        ],
        near, far, maps, wu, qo, d_hidden, norm_gain[None],
    )
    d_two = d_enter + lax.dot_general(
        device_map[:, :head], shift(d_enter, "z", -1), (((0,), (0,)), ((), ())), precision=HIGH
    )
    d_two, late = lax.optimization_barrier((d_two, hidden))
    d_near, d_far = shift(d_two, "z", -1), shift(d_two.astype(BF16), "z", -3)
    share, last = call(
        share_kernel,
        [((2, nz, span, here), F32), ((nz, span, head), F32)],
        place, late, upstream, up_other, *arrived,
    )
    from_core = swap((pick(share, 1 - core) * LIFT).astype(F16), "core")

    d_projected, power = call(
        post_kernel,
        [((length + HALO, 3 * head), BF16), ((8, 4 * head), F32)],
        place, d_near, d_far, far_map, maps, from_out, states, pseudo, d_out, inverse, scores, grow, total, beta,
        doc_columns, docs[None], conv,
        scratch=[pltpu.VMEM((length + HALO, 3 * head), F32)],
    )

    own_power = power[:1]

    def part(by):
        index = (z + by) % nz
        first = jnp.dot(pick(blocks, index), d_projected, preferred_element_type=F32)
        return jnp.concatenate([first, pick(last, index)], axis=1)

    def add(packed, by):
        total, power = unpack(packed)
        return total + part(by), jnp.maximum(power, own_power) + 1.0

    half = nz // 2
    right = turn(pack(part(half), own_power), "z", 1)
    left = turn(pack(part(1 - half), own_power), "z", -1)
    right, left, from_core = lax.optimization_barrier((right, left, from_core))
    right = turn(pack(*add(right, half - 1)), "z", 1)
    left = turn(pack(*add(left, 2 - half)), "z", -1)
    shared = (pick(share, core) * LIFT + from_core.astype(F32)).reshape(nx, 2, span, here)
    from_ylo = swap(lax.dynamic_index_in_dim(shared, 1 - ylo, 1, keepdims=False).astype(F16), "ylo")
    right, left, from_ylo = lax.optimization_barrier((right, left, from_ylo))
    for k in range(2, half):
        right = turn(pack(*add(right, half - k)), "z", 1)
        if k < half - 1:
            left = turn(pack(*add(left, 1 - half + k)), "z", -1)
        if k == 2:
            shared = lax.dynamic_index_in_dim(shared, ylo, 1, keepdims=False) + from_ylo.astype(F32)
            from_x = [turn(pick(shared, (x + by) % nx).astype(F16), "x", by) for by in (1, -1, 2)]
        right, left = lax.optimization_barrier((right, left))
    layer_out = ((pick(shared, x) + sum(f.astype(F32) for f in from_x)) * (1.0 / LIFT)).T.astype(BF16)[None]
    total, power = add(right, 0)
    more, more_power = unpack(left)
    packed = pack(total + more, jnp.maximum(power, more_power) + 1.0)
    grad = unpack(packed)[0] + unpack(swap(packed, "roll"))[0]
    fresh = (piece.astype(F32) - RATE * grad).astype(BF16).reshape(2, span // 2, 4 * head)
    kept, sent = pick(fresh, core), pick(fresh, 1 - core)
    heads = ordered(kept, swap(sent, "core"), core).reshape(2, span // 2, 4, head)
    engine_tiles = jnp.moveaxis(heads, 0, 2).reshape(span // 2, 4, 2 * head)
    return (layer_out, engine_tiles)


def solution(mesh):
    fine = Mesh(mesh.devices.reshape(8, 2, 4, 2, 2), ("z", "core", "x", "ylo", "roll"))
    seq, mp = ("z", "core"), ("x", "ylo")
    in_specs = (
        P("roll", seq, mp),
        P("roll", seq, mp),
        P("roll", seq),
        P(("z", "core", "roll"), None, mp),
        P(None, None, mp),
        P(),
        P(None, mp),
        P(mp),
        P(None, mp),
        P(),
    )
    out_specs = (P("roll", seq, mp), P(seq, None, mp))
    return jax.shard_map(per_device, mesh=fine, in_specs=in_specs, out_specs=out_specs, check_vma=False)
```

```python
import jax
import jax.numpy as jnp
from jax import lax
from jax.experimental import pallas as pl
from jax.experimental.pallas import tpu as pltpu
from jax.sharding import Mesh
from jax.sharding import PartitionSpec as P

BLOCK = 64
TAPS = 4
HALO = 16
RATE = 0.01
TOKEN_MOST = 6.0
LAST_POWER = 16.0
TOP = 15.0
LIFT = 8.0
F32 = jnp.float32
F16 = jnp.float16
BF16 = jnp.bfloat16
HIGH = lax.Precision.HIGHEST
VMEM_LIMIT = 56 * 1024 * 1024


def product(a, b, dims, precision=None):
    return lax.dot_general(a, b, ((dims[:1], dims[1:]), ((), ())), precision=precision, preferred_element_type=F32)


def halves(a):
    high = a.astype(BF16)
    return high, (a - high.astype(F32)).astype(BF16)


def split_product(a, b, dims):
    (a_high, a_low), (b_high, b_low) = halves(a), halves(b)
    return product(a_high, b_high, dims) + (product(a_high, b_low, dims) + product(a_low, b_high, dims))


def mm(a, b):
    return split_product(a, b, (1, 0))


def mm_nt(a, b):
    return split_product(a, b, (1, 1))


def mm_tn(a, b):
    return mm(a.T, b)


def softplus(x):
    return jnp.maximum(x, 0.0) + jnp.log1p(jnp.exp(-jnp.abs(x)))


def masks(docs_ref, doc_row_ref):
    length = docs_ref.shape[0]
    row = lax.broadcasted_iota(jnp.int32, (length, length), 0)
    col = lax.broadcasted_iota(jnp.int32, (length, length), 1)
    inside = (row // BLOCK == col // BLOCK) & (row >= col)
    paired = docs_ref[:, 3:4] == doc_row_ref[...]
    inclusive = inside & paired
    strict = inclusive & (row > col)
    return row, col, inside, inclusive, strict


def carried_of(docs_ref):
    return (docs_ref[:, 3:4] == docs_ref[:, 4:5]).astype(F32)


def own_rows(core, here, skip=0):
    return pl.ds(pl.multiple_of(skip + core * here, 16), here)


def offset_of(k):
    return ((k + 1) // 2) * (-1 if k % 2 else 1)


def index_of(place_ref, k, size):
    return lax.rem(place_ref[0] + offset_of(k) + size, size)


def gather_kernel(
    place_ref, features_ref, gate_weights_ref, gate_up_ref, rate_ref, docs_ref, *refs
):
    pieces, (proj_ref, grow_ref, beta_ref, decay_ref) = refs[:-4], refs[-4:]
    size, (length, head) = features_ref.shape[0], decay_ref.shape
    here, count = length // 2, length // BLOCK
    proj = jnp.zeros(proj_ref.shape, F32)
    gates = jnp.zeros((length, 2 * head), F32)
    for k in range(size):
        index = index_of(place_ref, k, size)
        rows = features_ref[index].T
        gates = gates + jnp.dot(rows[:length], gate_weights_ref[index], preferred_element_type=F32)
        if k < len(pieces):
            proj = proj + jnp.dot(rows, pieces[k][:, : 3 * head], preferred_element_type=F32)
    proj_ref[...] = proj
    low = gates[:, :head].astype(BF16)
    rates = jnp.dot(low, gate_up_ref[...], preferred_element_type=F32)
    log_decay = -rate_ref[...] * softplus(rates)
    beta = jnp.broadcast_to(jax.nn.sigmoid(gates[:, head : head + 1]), (length, head))
    core = place_ref[1]
    for ref, array in ((decay_ref, log_decay), (beta_ref, beta)):
        ref[own_rows(core, here)] = array[:here]
        ref[own_rows(1 - core, here)] = array[here:]
    row = lax.broadcasted_iota(jnp.int32, (length, length), 0)
    col = lax.broadcasted_iota(jnp.int32, (length, length), 1)
    inside = (row // BLOCK == col // BLOCK) & (row >= col)
    summed = product(inside.astype(F32), decay_ref[...], (1, 0), HIGH)
    ends = jnp.concatenate(
        [jnp.broadcast_to(summed[b * BLOCK + BLOCK - 1 : (b + 1) * BLOCK], (BLOCK, head)) for b in range(count)]
    )
    grow_ref[:, :head] = jnp.exp(summed)
    grow_ref[:, head : 2 * head] = jnp.exp(-summed)
    same = (docs_ref[:, 3:4] == docs_ref[:, 5:6]).astype(F32)
    grow_ref[:, 2 * head :] = jnp.exp(ends - summed) * same


def hidden_grad_kernel(place_ref, up_ref, up_other_ref, *refs):
    pieces, d_hidden_ref = refs[:-1], refs[-1]
    size, here, (length, head) = up_ref.shape[0], up_ref.shape[2], d_hidden_ref.shape
    d_hidden = jnp.zeros((length, head), F32)
    for k, piece in enumerate(pieces):
        index = index_of(place_ref, k, size)
        both = jnp.concatenate([up_ref[index].T, up_other_ref[index].T])
        d_hidden = d_hidden + jnp.dot(both, piece[:, 3 * head :], preferred_element_type=F32)
    d_hidden_ref[own_rows(place_ref[1], here)] = d_hidden[:here]
    d_hidden_ref[own_rows(1 - place_ref[1], here)] = d_hidden[here:]


def pre_kernel(
    place_ref, features_ref, piece_ref, proj_in_ref,
    grow_ref, beta_ref, conv_ref, docs_ref, doc_row_ref,
    total_ref, inv_ref, score_ref, wu_ref, qo_ref, maps_ref, device_map_ref, device_map16_ref,
    ext_ref,
):
    length, head = beta_ref.shape
    here, count = length // 2, length // BLOCK
    size, core = features_ref.shape[0], place_ref[1]
    index = index_of(place_ref, size - 1, size)
    proj = proj_in_ref[...] + jnp.dot(features_ref[index].T, piece_ref[:, : 3 * head], preferred_element_type=F32)
    ext_ref[:HALO] = proj[length:]
    ext_ref[own_rows(core, here, HALO)] = proj[:here]
    ext_ref[own_rows(1 - core, here, HALO)] = proj[here:length]
    total = jnp.zeros((length, 3 * head), F32)
    for j in range(TAPS):
        same = (docs_ref[:, j : j + 1] == docs_ref[:, 3:4]).astype(F32)
        total = total + ext_ref[HALO - 3 + j : HALO - 3 + j + length] * conv_ref[j : j + 1] * same
    total_ref[...] = total
    active = total * jax.nn.sigmoid(total)
    query, keys, values = active[:, :head], active[:, head : 2 * head], active[:, 2 * head :]
    query = query * lax.rsqrt(jnp.sum(query * query, axis=1, keepdims=True) + 1e-6)
    keys = keys * lax.rsqrt(jnp.sum(keys * keys, axis=1, keepdims=True) + 1e-6)
    beta = beta_ref[:, :1]
    row, col, _, inclusive, strict = masks(docs_ref, doc_row_ref)
    carried = carried_of(docs_ref)
    grow, shrink, tail = grow_ref[:, :head], grow_ref[:, head : 2 * head], grow_ref[:, 2 * head :]
    key_grow, key_shrink, query_grow, key_tail = keys * grow, keys * shrink, query * grow, keys * tail
    both = mm_nt(jnp.concatenate([key_grow, query_grow]), key_shrink)
    lower = jnp.where(strict, both[:length], 0.0) * beta
    scores = jnp.where(inclusive, both[length:], 0.0)
    score_ref[...] = scores
    inverse = (row == col).astype(F32) - jnp.where(row // 2 == col // 2, lower, 0.0)
    size = 2
    while size < BLOCK:
        corner = jnp.where((row // (2 * size) == col // (2 * size)) & (row // size != col // size), lower, 0.0)
        inverse = inverse - mm(inverse, mm(corner, inverse))
        size *= 2
    inv_ref[...] = inverse
    wu = mm(inverse, jnp.concatenate([beta * carried * key_grow, beta * values], axis=1))
    wu_ref[...] = wu
    mixed = mm(scores, wu)
    qo_ref[:, :head] = carried * query_grow - mixed[:, :head]
    qo_ref[:, head:] = mixed[:, head:]
    eye = lax.broadcasted_iota(jnp.int32, (head, head), 0) == lax.broadcasted_iota(jnp.int32, (head, head), 1)
    pairs = []
    for b in range(count):
        rows = slice(b * BLOCK, (b + 1) * BLOCK)
        last = (b + 1) * BLOCK - 1
        keep = grow[last : last + 1] * carried[last : last + 1]
        update = mm_tn(key_tail[rows], wu[rows])
        moved = jnp.where(eye, keep, 0.0) - update[:, :head]
        maps_ref[b, :, :head] = moved
        maps_ref[b, :, head:] = update[:, head:]
        pairs.append((moved, update[:, head:]))

    def after(second, first):
        made = mm(second[0], jnp.concatenate(first, axis=1))
        return (made[:, :head], made[:, head:] + second[1])

    while len(pairs) > 1:
        pairs = [after(pairs[i + 1], pairs[i]) for i in range(0, len(pairs), 2)]
    device_map_ref[:, :head] = pairs[0][0]
    device_map_ref[:, head:] = pairs[0][1]
    device_map16_ref[:, :head] = pairs[0][0].astype(BF16)
    device_map16_ref[:, head:] = pairs[0][1].astype(BF16)


def mid_kernel(
    near_ref, far_ref, maps_ref, wu_ref, qo_ref, d_hidden_ref, gain_ref,
    hidden_ref, d_out_ref, pseudo_ref, states_ref, from_out_ref, d_enter_ref,
):
    length, head = d_hidden_ref.shape
    count = length // BLOCK
    state = near_ref[:, head:] + mm(near_ref[:, :head], far_ref[...].astype(F32))
    states = []
    for b in range(count):
        states.append(state)
        states_ref[b] = state
        if b < count - 1:
            state = mm(maps_ref[b, :, :head], state) + maps_ref[b, :, head:]
    outs, pseudos = [], []
    for b in range(count):
        rows = slice(b * BLOCK, (b + 1) * BLOCK)
        made = mm(jnp.concatenate([qo_ref[rows, :head], wu_ref[rows, :head]]), states[b])
        outs.append(qo_ref[rows, head:] + made[:BLOCK])
        pseudos.append(wu_ref[rows, head:] - made[BLOCK:])
    out = jnp.concatenate(outs)
    pseudo_ref[...] = jnp.concatenate(pseudos)
    scale = lax.rsqrt(jnp.mean(out * out, axis=1, keepdims=True) + 1e-5)
    hidden_ref[...] = (out * scale * gain_ref[...]).astype(BF16)
    lifted = d_hidden_ref[...] * gain_ref[...]
    d_out = scale * lifted - out * (scale * scale * scale) * jnp.mean(lifted * out, axis=1, keepdims=True)
    d_out_ref[...] = d_out
    d_state = None
    for b in reversed(range(count)):
        rows = slice(b * BLOCK, (b + 1) * BLOCK)
        part = mm_tn(qo_ref[rows, :head], d_out[rows])
        from_out_ref[b] = part
        d_state = part if d_state is None else part + mm_tn(maps_ref[b, :, :head], d_state)
    d_enter_ref[...] = d_state


def share_kernel(place_ref, hidden_ref, *refs):
    pieces, share_ref = refs[:-1], refs[-1]
    size, here, head = share_ref.shape[1], share_ref.shape[3], hidden_ref.shape[1]
    for k, piece in enumerate(pieces):
        index = index_of(place_ref, k, size)
        for c in range(2):
            share_ref[c, index] = lax.dot_general(
                piece[:, 3 * head :], hidden_ref[c * here : (c + 1) * here], (((1,), (1,)), ((), ())),
                preferred_element_type=F32,
            )


def last_kernel(place_ref, hidden_ref, up_ref, up_other_ref, last_ref):
    here, core = up_ref.shape[2], place_ref[1]
    own, other = hidden_ref[own_rows(core, here)], hidden_ref[own_rows(1 - core, here)]
    for k in range(up_ref.shape[0]):
        last_ref[k] = jnp.dot(up_ref[k], own, preferred_element_type=F32) + jnp.dot(
            up_other_ref[k], other, preferred_element_type=F32
        )


def post_kernel(
    place_ref, near_ref, far_ref, far_map_ref, maps_ref, from_out_ref, states_ref, pseudo_ref, d_out_ref, inv_ref,
    score_ref, grow_ref, total_ref, beta_ref, docs_ref, doc_row_ref, conv_ref,
    d_proj_ref, power_ref,
    d_ext_ref,
):
    length, head = d_out_ref.shape
    count = length // BLOCK
    core, here = place_ref[1], length // 2
    d_state = near_ref[...] + lax.dot_general(
        far_map_ref[...].T, far_ref[...], (((1,), (0,)), ((), ())), preferred_element_type=F32
    )
    d_after = [None] * count
    for b in reversed(range(count)):
        d_after[b] = d_state
        if b > 0:
            d_state = from_out_ref[b] + mm_tn(maps_ref[b, :, :head], d_state)
    total = total_ref[...]
    gate = jax.nn.sigmoid(total)
    active = total * gate
    raw_q, raw_k = active[:, :head], active[:, head : 2 * head]
    inv_q = lax.rsqrt(jnp.sum(raw_q * raw_q, axis=1, keepdims=True) + 1e-6)
    inv_k = lax.rsqrt(jnp.sum(raw_k * raw_k, axis=1, keepdims=True) + 1e-6)
    query, keys = raw_q * inv_q, raw_k * inv_k
    grow, shrink, tail = grow_ref[:, :head], grow_ref[:, head : 2 * head], grow_ref[:, 2 * head :]
    key_grow, key_shrink, query_grow, key_tail = keys * grow, keys * shrink, query * grow, keys * tail
    beta = beta_ref[:, :1]
    _, _, _, inclusive, strict = masks(docs_ref, doc_row_ref)
    carried = carried_of(docs_ref)
    d_out, pseudo = d_out_ref[...], pseudo_ref[...]

    def each(function):
        return jnp.concatenate([function(b, slice(b * BLOCK, (b + 1) * BLOCK)) for b in range(count)])

    d_pseudo = mm_tn(score_ref[...], d_out) + each(lambda b, rows: mm(key_tail[rows], d_after[b]))
    d_target = mm_tn(inv_ref[...], d_pseudo)
    both = mm_nt(jnp.concatenate([d_out, d_target]), pseudo)
    d_scores = jnp.where(inclusive, both[:length], 0.0)
    d_lower = jnp.where(strict, both[length:], 0.0) * (-beta)
    d_values = beta * d_target
    d_from_keys = -carried * d_values
    lifted_out = carried * d_out
    d_query_grow = each(lambda b, rows: mm_nt(lifted_out[rows], states_ref[b])) + mm(d_scores, key_shrink)
    d_key_grow = each(lambda b, rows: mm_nt(d_from_keys[rows], states_ref[b])) + mm(d_lower, key_shrink)
    d_key_shrink = mm_tn(d_scores, query_grow) + mm_tn(d_lower, key_grow)
    d_key_tail = each(lambda b, rows: mm_nt(pseudo[rows], d_after[b]))
    d_query = d_query_grow * grow
    d_keys = d_key_grow * grow + d_key_shrink * shrink + d_key_tail * tail
    d_query = inv_q * d_query - query * (inv_q * jnp.sum(d_query * query, axis=1, keepdims=True))
    d_keys = inv_k * d_keys - keys * (inv_k * jnp.sum(d_keys * keys, axis=1, keepdims=True))
    d_total = jnp.concatenate([d_query, d_keys, d_values], axis=1) * (gate * (1.0 + total * (1.0 - gate)))
    d_ext_ref[...] = jnp.zeros_like(d_ext_ref)
    for j in range(TAPS):
        same = (docs_ref[:, j : j + 1] == docs_ref[:, 3:4]).astype(F32)
        spot = slice(HALO - 3 + j, HALO - 3 + j + length)
        d_ext_ref[spot] = d_ext_ref[spot] + d_total * conv_ref[j : j + 1] * same
    d_proj_ref[:here] = d_ext_ref[own_rows(core, here, HALO)].astype(BF16)
    d_proj_ref[here:length] = d_ext_ref[own_rows(1 - core, here, HALO)].astype(BF16)
    d_proj_ref[length:] = d_ext_ref[:HALO].astype(BF16)
    most = jnp.max(jnp.abs(d_ext_ref[...]), axis=0, keepdims=True) * (TOKEN_MOST * 1.01 * (length + HALO))
    power = jnp.ceil(jnp.log(jnp.maximum(most, 1e-30)) * 1.4426950408889634 + 0.01)
    power_ref[:, : 3 * head] = jnp.broadcast_to(power, (8, 3 * head))
    power_ref[:, 3 * head :] = jnp.full((8, head), LAST_POWER, F32)


def call(kernel, outs, *args, scratch=()):
    def spec(arg):
        return pl.BlockSpec(memory_space=pltpu.SMEM if arg.dtype == jnp.int32 else pltpu.VMEM)

    return pl.pallas_call(
        kernel,
        out_shape=tuple(jax.ShapeDtypeStruct(shape, dtype) for shape, dtype in outs),
        in_specs=[spec(arg) for arg in args],
        out_specs=tuple(pl.BlockSpec(memory_space=pltpu.VMEM) for _ in outs),
        scratch_shapes=list(scratch),
        compiler_params=pltpu.CompilerParams(vmem_limit_bytes=VMEM_LIMIT),
    )(*args)


def pack(total, power):
    scaled = (total * jnp.exp2(TOP - power)).astype(F16)
    return jnp.concatenate([scaled, jnp.broadcast_to(power, (16, total.shape[1])).astype(F16)])


def unpack(packed):
    power = packed[-16:-15].astype(F32)
    return packed[:-16].astype(F32) * jnp.exp2(power - TOP), power


def swap(array, axis):
    return lax.ppermute(array, axis, [(0, 1), (1, 0)])


def turn(array, axis, by):
    size = lax.axis_size(axis)
    return lax.ppermute(array, axis, [(i, (i + by) % size) for i in range(size)])


def shift(array, axis, by):
    size = lax.axis_size(axis)
    return lax.ppermute(array, axis, [(i, i + by) for i in range(size) if 0 <= i + by < size])


def ordered(mine, other, index):
    return jnp.where(index == 0, jnp.stack([mine, other]), jnp.stack([other, mine]))


def pick(array, index):
    return lax.dynamic_index_in_dim(array, index, 0, keepdims=False)


def put(array, piece, index):
    return lax.dynamic_update_index_in_dim(array, piece, index, 0)


def outer(a, b):
    return lax.dot_general(a, b, (((0,), (0,)), ((), ())), preferred_element_type=F32)


def per_device(
    tokens, cotangent, doc_ids, projections, conv_weight, gate_down, gate_up, decay_log, beta_weight, norm_gain
):
    z, core, x, ylo, roll = (lax.axis_index(a) for a in ("z", "core", "x", "ylo", "roll"))
    nz, nx = lax.axis_size("z"), lax.axis_size("x")
    here, width = tokens.shape[1], tokens.shape[2]
    head = norm_gain.shape[0]
    rows = projections.shape[0]
    length = 2 * here
    span = 4 * rows

    split = projections.reshape(rows, 4, 2, head)
    mine = lax.dynamic_index_in_dim(split, core, 2, keepdims=False).reshape(rows, 4 * head)
    theirs = lax.dynamic_index_in_dim(split, 1 - core, 2, keepdims=False).reshape(rows, 4 * head)
    chip_rows = ordered(mine, swap(theirs, "core"), core)
    piece = jnp.swapaxes(ordered(chip_rows, swap(chip_rows, "roll"), roll), 0, 1).reshape(span, 4 * head)

    block = jnp.stack([tokens[0].T, cotangent[0].T])
    pair = ordered(block, swap(block, "ylo"), ylo)
    behind, ahead = turn(pair, "x", 1), turn(pair, "x", -1)
    across = [turn(behind[:, 0], "x", 1), turn(ahead[:, 1], "x", -1)]

    def ring_order(i):
        full = jnp.zeros((nx,) + across[i].shape, across[i].dtype)
        for by, part in ((0, pair[:, i]), (1, behind[:, i]), (-1, ahead[:, i]), (2, across[i])):
            full = put(full, part, (x - by) % nx)
        return full.reshape(-1, here)

    features, upstream = ring_order(0), ring_order(1)
    model = features.shape[0]
    doc_row = jnp.broadcast_to((doc_ids + 1).astype(BF16), (16, here))
    own = jnp.concatenate([features, doc_row])
    other = swap(own, "core")
    up_other = swap(upstream, "core")
    halo = shift(jnp.where(core == 1, own[:, here - HALO :], other[:, here - HALO :]).T, "z", 1)
    docs = ordered(own[model], other[model], core).reshape(length).astype(F32)
    upstream, up_other = upstream.reshape(nz, span, here), up_other.reshape(nz, span, here)
    doc_ext = jnp.concatenate([halo[HALO - 3 :, model].astype(F32), docs])
    prior = jnp.repeat(doc_ext[2 : 2 + length : BLOCK], BLOCK)
    last = jnp.repeat(docs[BLOCK - 1 :: BLOCK], BLOCK)
    doc_columns = jnp.stack([doc_ext[j : j + length] for j in range(TAPS)] + [prior, last, docs, docs], axis=1)
    extended = jnp.concatenate([features, other[:model], halo[:, :model].T], axis=1)

    beta_column = lax.dynamic_index_in_dim(beta_weight, core, 1)
    gate_weights = jnp.concatenate([gate_down, jnp.pad(beta_column, ((0, 0), (0, head - 1)))], axis=1)
    gate_up = lax.dynamic_index_in_dim(gate_up.reshape(-1, 2, head), core, 1, keepdims=False)
    rate = jnp.broadcast_to(jnp.exp(pick(decay_log, core)), (1, head))
    conv = lax.dynamic_index_in_dim(conv_weight.reshape(3, TAPS, 2, head), core, 2, keepdims=False)
    conv = jnp.swapaxes(conv, 0, 1).reshape(TAPS, 3 * head)

    place = jnp.stack([z, core]).astype(jnp.int32)
    blocks = extended.reshape(nz, span, length + HALO)
    arrived = [piece]
    right = left = piece
    for k in range(1, nz // 2 + 1):
        right = turn(right, "z", 1)
        arrived.append(right)
        if k < nz // 2:
            left = turn(left, "z", -1)
            arrived.append(left)
    projected, grow, beta, _ = call(
        gather_kernel,
        [((length + HALO, 3 * head), F32), ((length, 3 * head), F32)] + [((length, head), F32)] * 2,
        place, blocks, gate_weights.reshape(nz, span, 2 * head), gate_up, rate, doc_columns, *arrived[:-1],
    )
    total, inverse, scores, wu, qo, maps, device_map, device_map16 = call(
        pre_kernel,
        [
            ((length, 3 * head), F32), ((length, length), F32), ((length, length), F32), ((length, 2 * head), F32),
            ((length, 2 * head), F32), ((length // BLOCK, head, 2 * head), F32), ((head, 2 * head), F32),
            ((head, 2 * head), BF16),
        ],
        place, blocks, arrived[-1], projected, grow, beta, conv, doc_columns, docs[None],
        scratch=[pltpu.VMEM((length + HALO, 3 * head), F32)],
    )
    device_map, device_map16, late = lax.optimization_barrier((device_map, device_map16, place))
    (d_hidden,) = call(hidden_grad_kernel, [((length, head), F32)], late, upstream, up_other, *arrived)

    one, two = shift(device_map, "z", 1), shift(device_map16, "z", 2).astype(F32)
    joined = product(one[:, :head], two, (1, 0), HIGH)
    near = jnp.concatenate([joined[:, :head], joined[:, head:] + one[:, head:]], axis=1)
    far = shift(near[:, head:].astype(BF16), "z", 2)
    far_map = shift(near[:, :head].astype(BF16), "z", -3)
    hidden, d_out, pseudo, states, from_out, d_enter = call(
        mid_kernel,
        [
            ((length, head), BF16), ((length, head), F32), ((length, head), F32), ((length // BLOCK, head, head), F32),
            ((length // BLOCK, head, head), F32), ((head, head), F32),
        ],
        near, far, maps, wu, qo, d_hidden, norm_gain[None],
    )
    d_two = d_enter + lax.dot_general(
        device_map[:, :head], shift(d_enter, "z", -1), (((0,), (0,)), ((), ())), precision=HIGH
    )
    d_two, late = lax.optimization_barrier((d_two, hidden))
    d_near, d_far = shift(d_two, "z", -1), shift(d_two.astype(BF16), "z", -3)
    (last,) = call(last_kernel, [((nz, span, head), F32)], place, late, upstream, up_other)
    d_projected, power = call(
        post_kernel,
        [((length + HALO, 3 * head), BF16), ((8, 4 * head), F32)],
        place, d_near, d_far, far_map, maps, from_out, states, pseudo, d_out, inverse, scores, grow, total, beta,
        doc_columns, docs[None], conv,
        scratch=[pltpu.VMEM((length + HALO, 3 * head), F32)],
    )

    own_power = power[:1]

    def part(by):
        index = (z + by) % nz
        first = jnp.dot(pick(blocks, index), d_projected, preferred_element_type=F32)
        return jnp.concatenate([first, pick(last, index)], axis=1)

    def add(packed, by):
        total, power = unpack(packed)
        return total + part(by), jnp.maximum(power, own_power) + 1.0

    half, mid = nz // 2, span // 2
    farthest = part(half)
    right = turn(pack(farthest[:mid], own_power), "z", 1)
    left = turn(pack(farthest[mid:], own_power), "z", -1)
    late, d_projected = lax.optimization_barrier((hidden, d_projected))
    (share,) = call(share_kernel, [((2, nz, span, here), F32)], place, late, *arrived)
    right, left, share = lax.optimization_barrier((right, left, share))

    def widen(packed, by, skip):
        some, power = unpack(packed)
        return part(by) + jnp.pad(some, ((skip, mid - skip), (0, 0))), jnp.maximum(power, own_power) + 1.0

    right = turn(pack(*widen(right, half - 1, 0)), "z", 1)
    left = turn(pack(*widen(left, 1 - half, mid)), "z", -1)
    from_core = swap((pick(share, 1 - core) * LIFT).astype(F16), "core")
    right, left, from_core = lax.optimization_barrier((right, left, from_core))
    right = turn(pack(*add(right, half - 2)), "z", 1)
    left = turn(pack(*add(left, 2 - half)), "z", -1)
    shared = (pick(share, core) * LIFT + from_core.astype(F32)).reshape(nx, 2, span, here)
    from_ylo = swap(lax.dynamic_index_in_dim(shared, 1 - ylo, 1, keepdims=False).astype(F16), "ylo")
    right, left, from_ylo = lax.optimization_barrier((right, left, from_ylo))
    right = turn(pack(*add(right, half - 3)), "z", 1)
    left = turn(pack(*add(left, 3 - half)), "z", -1)
    shared = lax.dynamic_index_in_dim(shared, ylo, 1, keepdims=False) + from_ylo.astype(F32)
    from_x = [turn(pick(shared, (x + by) % nx).astype(F16), "x", by) for by in (1, -1, 2)]
    layer_out = ((pick(shared, x) + sum(f.astype(F32) for f in from_x)) * (1.0 / LIFT)).T.astype(BF16)[None]
    total, power = add(right, 0)
    more, more_power = unpack(left)
    packed = pack(total + more, jnp.maximum(power, more_power) + 1.0)
    grad = unpack(packed)[0] + unpack(swap(packed, "roll"))[0]
    fresh = (piece.astype(F32) - RATE * grad).astype(BF16).reshape(2, span // 2, 4 * head)
    kept, sent = pick(fresh, core), pick(fresh, 1 - core)
    heads = ordered(kept, swap(sent, "core"), core).reshape(2, span // 2, 4, head)
    engine_tiles = jnp.moveaxis(heads, 0, 2).reshape(span // 2, 4, 2 * head)
    return (layer_out, engine_tiles)


def solution(mesh):
    fine = Mesh(mesh.devices.reshape(8, 2, 4, 2, 2), ("z", "core", "x", "ylo", "roll"))
    seq, mp = ("z", "core"), ("x", "ylo")
    in_specs = (
        P("roll", seq, mp),
        P("roll", seq, mp),
        P("roll", seq),
        P(("z", "core", "roll"), None, mp),
        P(None, None, mp),
        P(),
        P(None, mp),
        P(mp),
        P(None, mp),
        P(),
    )
    out_specs = (P("roll", seq, mp), P(seq, None, mp))
    return jax.shard_map(per_device, mesh=fine, in_specs=in_specs, out_specs=out_specs, check_vma=False)
```

```python
import jax
import jax.numpy as jnp
from jax import lax
from jax.experimental import pallas as pl
from jax.experimental.pallas import tpu as pltpu
from jax.sharding import Mesh
from jax.sharding import PartitionSpec as P

BLOCK = 64
TAPS = 4
HALO = 16
RATE = 0.01
TOKEN_MOST = 6.0
LAST_POWER = 16.0
TOP = 15.0
LIFT = 8.0
F32 = jnp.float32
F16 = jnp.float16
BF16 = jnp.bfloat16
HIGH = lax.Precision.HIGHEST
VMEM_LIMIT = 56 * 1024 * 1024


def product(a, b, dims, precision=None):
    return lax.dot_general(a, b, ((dims[:1], dims[1:]), ((), ())), precision=precision, preferred_element_type=F32)


def halves(a):
    high = a.astype(BF16)
    return high, (a - high.astype(F32)).astype(BF16)


def split_product(a, b, dims):
    (a_high, a_low), (b_high, b_low) = halves(a), halves(b)
    return product(a_high, b_high, dims) + (product(a_high, b_low, dims) + product(a_low, b_high, dims))


def mm(a, b):
    return split_product(a, b, (1, 0))


def mm_nt(a, b):
    return split_product(a, b, (1, 1))


def mm_tn(a, b):
    return mm(a.T, b)


def softplus(x):
    return jnp.maximum(x, 0.0) + jnp.log1p(jnp.exp(-jnp.abs(x)))


def masks(docs_ref, doc_row_ref):
    length = docs_ref.shape[0]
    row = lax.broadcasted_iota(jnp.int32, (length, length), 0)
    col = lax.broadcasted_iota(jnp.int32, (length, length), 1)
    inside = (row // BLOCK == col // BLOCK) & (row >= col)
    paired = docs_ref[:, 3:4] == doc_row_ref[...]
    inclusive = inside & paired
    strict = inclusive & (row > col)
    return row, col, inside, inclusive, strict


def carried_of(docs_ref):
    return (docs_ref[:, 3:4] == docs_ref[:, 4:5]).astype(F32)


def own_rows(core, here, skip=0):
    return pl.ds(pl.multiple_of(skip + core * here, 16), here)


def offset_of(k):
    return ((k + 1) // 2) * (-1 if k % 2 else 1)


def index_of(place_ref, k, size):
    return lax.rem(place_ref[0] + offset_of(k) + size, size)


def taps_of(conv_ref, core, head, j):
    here = pl.ds(pl.multiple_of(core * head, head), head)
    return jnp.concatenate([conv_ref[c, j : j + 1, here] for c in range(3)], axis=1)


def halo_kernel(place_ref, own_ref, other_ref, halo_ref):
    model, here = halo_ref.shape[1] - 128, own_ref.shape[1]
    last = jnp.where(place_ref[1] == 1, own_ref[...].astype(F32), other_ref[...].astype(F32))
    halo_ref[:, :model] = last[:model].T[here - HALO :].astype(BF16)
    row = lax.broadcasted_iota(jnp.int32, (HALO, here), 0)
    col = lax.broadcasted_iota(jnp.int32, (HALO, here), 1)
    docs = jnp.sum(jnp.where(col == row + (here - HALO), last[model : model + HALO], 0.0), axis=1, keepdims=True)
    halo_ref[:, model:] = jnp.broadcast_to(docs, (HALO, 128)).astype(BF16)


def gather_kernel(
    place_ref, decay_log_ref, own_ref, other_ref, halo_ref, gate_down_ref, beta_weight_ref, gate_up_ref, *refs
):
    pieces, (features_ref, docs_ref, doc_row_ref, proj_ref, grow_ref, beta_ref, decay_ref) = refs[:-7], refs[-7:]
    size, span, _ = features_ref.shape
    length, head = decay_ref.shape
    here, count, model = length // 2, length // BLOCK, size * span
    core = place_ref[1]
    halo = halo_ref[:, :model].T
    for k in range(size):
        rows = slice(k * span, (k + 1) * span)
        features_ref[k, :, :here] = own_ref[rows]
        features_ref[k, :, here:length] = other_ref[rows]
        features_ref[k, :, length:] = halo[rows]

    own_docs, other_docs = (ref[model : model + 16].astype(F32)[:1] for ref in (own_ref, other_ref))
    doc_row = jnp.where(
        core == 0, jnp.concatenate([own_docs, other_docs], axis=1), jnp.concatenate([other_docs, own_docs], axis=1)
    )
    doc_row_ref[...] = doc_row
    rim = halo_ref[:, model:].astype(F32)
    row = lax.broadcasted_iota(jnp.int32, (length, length), 0)
    col = lax.broadcasted_iota(jnp.int32, (length, length), 1)
    spot = lax.broadcasted_iota(jnp.int32, (length, 1), 0)

    def taken(line, target):
        return jnp.sum(jnp.where(col == target, line, 0.0), axis=1, keepdims=True)

    columns = []
    for back in (3, 2, 1, 0):
        column = taken(doc_row, row - back)
        for t in range(back):
            at = HALO + t - back
            column = jnp.where(spot == t, rim[at : at + 1, :1], column)
        columns.append(column)
    first = row // BLOCK * BLOCK
    prior = jnp.where(spot < BLOCK, rim[HALO - 1 : HALO, :1], taken(doc_row, first - 1))
    last = taken(doc_row, first + BLOCK - 1)
    docs_ref[...] = jnp.concatenate(columns + [prior, last, columns[3], columns[3]], axis=1)

    proj = jnp.zeros(proj_ref.shape, F32)
    low = jnp.zeros((length, head), F32)
    logits = jnp.zeros((beta_weight_ref.shape[0], features_ref.shape[2]), F32)
    for k in range(size):
        index = index_of(place_ref, k, size)
        rows = features_ref[index].T
        low = low + jnp.dot(rows[:length], gate_down_ref[index], preferred_element_type=F32)
        logits = logits + jnp.dot(
            beta_weight_ref[:, k * span : (k + 1) * span], features_ref[k], preferred_element_type=F32
        )
        if k < len(pieces):
            proj = proj + jnp.dot(rows, pieces[k][:, : 3 * head], preferred_element_type=F32)
    proj_ref[...] = proj
    gate_up = gate_up_ref[:, pl.ds(pl.multiple_of(core * head, head), head)]
    rates = jnp.dot(low.astype(BF16), gate_up, preferred_element_type=F32)
    log_decay = -jnp.exp(jnp.full((1, head), decay_log_ref[core])) * softplus(rates)
    logit = jnp.where(core == 0, logits[:1, :length], logits[1:2, :length])
    beta = jnp.broadcast_to(jax.nn.sigmoid(taken(logit, row)), (length, head))
    for ref, array in ((decay_ref, log_decay), (beta_ref, beta)):
        ref[own_rows(core, here)] = array[:here]
        ref[own_rows(1 - core, here)] = array[here:]
    inside = (row // BLOCK == col // BLOCK) & (row >= col)
    summed = product(inside.astype(F32), decay_ref[...], (1, 0), HIGH)
    ends = jnp.concatenate(
        [jnp.broadcast_to(summed[b * BLOCK + BLOCK - 1 : (b + 1) * BLOCK], (BLOCK, head)) for b in range(count)]
    )
    grow_ref[:, :head] = jnp.exp(summed)
    grow_ref[:, head : 2 * head] = jnp.exp(-summed)
    grow_ref[:, 2 * head :] = jnp.exp(ends - summed) * (columns[3] == last).astype(F32)


def hidden_grad_kernel(place_ref, up_ref, up_other_ref, *refs):
    pieces, d_hidden_ref = refs[:-1], refs[-1]
    size, here, (length, head) = up_ref.shape[0], up_ref.shape[2], d_hidden_ref.shape
    d_hidden = jnp.zeros((length, head), F32)
    for k, piece in enumerate(pieces):
        index = index_of(place_ref, k, size)
        both = jnp.concatenate([up_ref[index].T, up_other_ref[index].T])
        d_hidden = d_hidden + jnp.dot(both, piece[:, 3 * head :], preferred_element_type=F32)
    d_hidden_ref[own_rows(place_ref[1], here)] = d_hidden[:here]
    d_hidden_ref[own_rows(1 - place_ref[1], here)] = d_hidden[here:]


def pre_kernel(
    place_ref, features_ref, piece_ref, proj_in_ref,
    grow_ref, beta_ref, conv_ref, docs_ref, doc_row_ref,
    total_ref, inv_ref, score_ref, wu_ref, qo_ref, maps_ref, device_map_ref, device_map16_ref,
    ext_ref,
):
    length, head = beta_ref.shape
    here, count = length // 2, length // BLOCK
    size, core = features_ref.shape[0], place_ref[1]
    index = index_of(place_ref, size - 1, size)
    proj = proj_in_ref[...] + jnp.dot(features_ref[index].T, piece_ref[:, : 3 * head], preferred_element_type=F32)
    ext_ref[:HALO] = proj[length:]
    ext_ref[own_rows(core, here, HALO)] = proj[:here]
    ext_ref[own_rows(1 - core, here, HALO)] = proj[here:length]
    total = jnp.zeros((length, 3 * head), F32)
    for j in range(TAPS):
        same = (docs_ref[:, j : j + 1] == docs_ref[:, 3:4]).astype(F32)
        total = total + ext_ref[HALO - 3 + j : HALO - 3 + j + length] * taps_of(conv_ref, core, head, j) * same
    total_ref[...] = total
    active = total * jax.nn.sigmoid(total)
    query, keys, values = active[:, :head], active[:, head : 2 * head], active[:, 2 * head :]
    query = query * lax.rsqrt(jnp.sum(query * query, axis=1, keepdims=True) + 1e-6)
    keys = keys * lax.rsqrt(jnp.sum(keys * keys, axis=1, keepdims=True) + 1e-6)
    beta = beta_ref[:, :1]
    row, col, _, inclusive, strict = masks(docs_ref, doc_row_ref)
    carried = carried_of(docs_ref)
    grow, shrink, tail = grow_ref[:, :head], grow_ref[:, head : 2 * head], grow_ref[:, 2 * head :]
    key_grow, key_shrink, query_grow, key_tail = keys * grow, keys * shrink, query * grow, keys * tail
    both = mm_nt(jnp.concatenate([key_grow, query_grow]), key_shrink)
    lower = jnp.where(strict, both[:length], 0.0) * beta
    scores = jnp.where(inclusive, both[length:], 0.0)
    score_ref[...] = scores
    inverse = (row == col).astype(F32) - jnp.where(row // 2 == col // 2, lower, 0.0)
    size = 2
    while size < BLOCK:
        corner = jnp.where((row // (2 * size) == col // (2 * size)) & (row // size != col // size), lower, 0.0)
        inverse = inverse - mm(inverse, mm(corner, inverse))
        size *= 2
    inv_ref[...] = inverse
    wu = mm(inverse, jnp.concatenate([beta * carried * key_grow, beta * values], axis=1))
    wu_ref[...] = wu
    mixed = mm(scores, wu)
    qo_ref[:, :head] = carried * query_grow - mixed[:, :head]
    qo_ref[:, head:] = mixed[:, head:]
    eye = lax.broadcasted_iota(jnp.int32, (head, head), 0) == lax.broadcasted_iota(jnp.int32, (head, head), 1)
    pairs = []
    for b in range(count):
        rows = slice(b * BLOCK, (b + 1) * BLOCK)
        last = (b + 1) * BLOCK - 1
        keep = grow[last : last + 1] * carried[last : last + 1]
        update = mm_tn(key_tail[rows], wu[rows])
        moved = jnp.where(eye, keep, 0.0) - update[:, :head]
        maps_ref[b, :, :head] = moved
        maps_ref[b, :, head:] = update[:, head:]
        pairs.append((moved, update[:, head:]))

    def after(second, first):
        made = mm(second[0], jnp.concatenate(first, axis=1))
        return (made[:, :head], made[:, head:] + second[1])

    while len(pairs) > 1:
        pairs = [after(pairs[i + 1], pairs[i]) for i in range(0, len(pairs), 2)]
    device_map_ref[:, :head] = pairs[0][0]
    device_map_ref[:, head:] = pairs[0][1]
    device_map16_ref[:, :head] = pairs[0][0].astype(BF16)
    device_map16_ref[:, head:] = pairs[0][1].astype(BF16)


def mid_kernel(
    near_ref, far_ref, maps_ref, wu_ref, qo_ref, d_hidden_ref, gain_ref,
    hidden_ref, d_out_ref, pseudo_ref, states_ref, from_out_ref, d_enter_ref,
):
    length, head = d_hidden_ref.shape
    count = length // BLOCK
    state = near_ref[:, head:] + mm(near_ref[:, :head], far_ref[...].astype(F32))
    states = []
    for b in range(count):
        states.append(state)
        states_ref[b] = state
        if b < count - 1:
            state = mm(maps_ref[b, :, :head], state) + maps_ref[b, :, head:]
    outs, pseudos = [], []
    for b in range(count):
        rows = slice(b * BLOCK, (b + 1) * BLOCK)
        made = mm(jnp.concatenate([qo_ref[rows, :head], wu_ref[rows, :head]]), states[b])
        outs.append(qo_ref[rows, head:] + made[:BLOCK])
        pseudos.append(wu_ref[rows, head:] - made[BLOCK:])
    out = jnp.concatenate(outs)
    pseudo_ref[...] = jnp.concatenate(pseudos)
    scale = lax.rsqrt(jnp.mean(out * out, axis=1, keepdims=True) + 1e-5)
    hidden_ref[...] = (out * scale * gain_ref[...]).astype(BF16)
    lifted = d_hidden_ref[...] * gain_ref[...]
    d_out = scale * lifted - out * (scale * scale * scale) * jnp.mean(lifted * out, axis=1, keepdims=True)
    d_out_ref[...] = d_out
    d_state = None
    for b in reversed(range(count)):
        rows = slice(b * BLOCK, (b + 1) * BLOCK)
        part = mm_tn(qo_ref[rows, :head], d_out[rows])
        from_out_ref[b] = part
        d_state = part if d_state is None else part + mm_tn(maps_ref[b, :, :head], d_state)
    d_enter_ref[...] = d_state


def share_kernel(place_ref, hidden_ref, up_ref, up_other_ref, *refs):
    pieces, (share_ref, last_ref) = refs[:-2], refs[-2:]
    size, here, head = up_ref.shape[0], up_ref.shape[2], hidden_ref.shape[1]
    core = place_ref[1]
    own, other = hidden_ref[own_rows(core, here)], hidden_ref[own_rows(1 - core, here)]
    for k, piece in enumerate(pieces):
        index = index_of(place_ref, k, size)
        for c in range(2):
            share_ref[c, index] = lax.dot_general(
                piece[:, 3 * head :], hidden_ref[c * here : (c + 1) * here], (((1,), (1,)), ((), ())),
                preferred_element_type=F32,
            )
        last_ref[k] = jnp.dot(up_ref[k], own, preferred_element_type=F32) + jnp.dot(
            up_other_ref[k], other, preferred_element_type=F32
        )


def post_kernel(
    place_ref, near_ref, far_ref, far_map_ref, maps_ref, from_out_ref, states_ref, pseudo_ref, d_out_ref, inv_ref,
    score_ref, grow_ref, total_ref, beta_ref, docs_ref, doc_row_ref, conv_ref,
    d_proj_ref, power_ref,
    d_ext_ref,
):
    length, head = d_out_ref.shape
    count = length // BLOCK
    core, here = place_ref[1], length // 2
    d_state = near_ref[...] + lax.dot_general(
        far_map_ref[...].T, far_ref[...], (((1,), (0,)), ((), ())), preferred_element_type=F32
    )
    d_after = [None] * count
    for b in reversed(range(count)):
        d_after[b] = d_state
        if b > 0:
            d_state = from_out_ref[b] + mm_tn(maps_ref[b, :, :head], d_state)
    total = total_ref[...]
    gate = jax.nn.sigmoid(total)
    active = total * gate
    raw_q, raw_k = active[:, :head], active[:, head : 2 * head]
    inv_q = lax.rsqrt(jnp.sum(raw_q * raw_q, axis=1, keepdims=True) + 1e-6)
    inv_k = lax.rsqrt(jnp.sum(raw_k * raw_k, axis=1, keepdims=True) + 1e-6)
    query, keys = raw_q * inv_q, raw_k * inv_k
    grow, shrink, tail = grow_ref[:, :head], grow_ref[:, head : 2 * head], grow_ref[:, 2 * head :]
    key_grow, key_shrink, query_grow, key_tail = keys * grow, keys * shrink, query * grow, keys * tail
    beta = beta_ref[:, :1]
    _, _, _, inclusive, strict = masks(docs_ref, doc_row_ref)
    carried = carried_of(docs_ref)
    d_out, pseudo = d_out_ref[...], pseudo_ref[...]

    def each(function):
        return jnp.concatenate([function(b, slice(b * BLOCK, (b + 1) * BLOCK)) for b in range(count)])

    d_pseudo = mm_tn(score_ref[...], d_out) + each(lambda b, rows: mm(key_tail[rows], d_after[b]))
    d_target = mm_tn(inv_ref[...], d_pseudo)
    both = mm_nt(jnp.concatenate([d_out, d_target]), pseudo)
    d_scores = jnp.where(inclusive, both[:length], 0.0)
    d_lower = jnp.where(strict, both[length:], 0.0) * (-beta)
    d_values = beta * d_target
    d_from_keys = -carried * d_values
    lifted_out = carried * d_out
    d_query_grow = each(lambda b, rows: mm_nt(lifted_out[rows], states_ref[b])) + mm(d_scores, key_shrink)
    d_key_grow = each(lambda b, rows: mm_nt(d_from_keys[rows], states_ref[b])) + mm(d_lower, key_shrink)
    d_key_shrink = mm_tn(d_scores, query_grow) + mm_tn(d_lower, key_grow)
    d_key_tail = each(lambda b, rows: mm_nt(pseudo[rows], d_after[b]))
    d_query = d_query_grow * grow
    d_keys = d_key_grow * grow + d_key_shrink * shrink + d_key_tail * tail
    d_query = inv_q * d_query - query * (inv_q * jnp.sum(d_query * query, axis=1, keepdims=True))
    d_keys = inv_k * d_keys - keys * (inv_k * jnp.sum(d_keys * keys, axis=1, keepdims=True))
    d_total = jnp.concatenate([d_query, d_keys, d_values], axis=1) * (gate * (1.0 + total * (1.0 - gate)))
    d_ext_ref[...] = jnp.zeros_like(d_ext_ref)
    for j in range(TAPS):
        same = (docs_ref[:, j : j + 1] == docs_ref[:, 3:4]).astype(F32)
        spot = slice(HALO - 3 + j, HALO - 3 + j + length)
        d_ext_ref[spot] = d_ext_ref[spot] + d_total * taps_of(conv_ref, core, head, j) * same
    d_proj_ref[:here] = d_ext_ref[own_rows(core, here, HALO)].astype(BF16)
    d_proj_ref[here:length] = d_ext_ref[own_rows(1 - core, here, HALO)].astype(BF16)
    d_proj_ref[length:] = d_ext_ref[:HALO].astype(BF16)
    most = jnp.max(jnp.abs(d_ext_ref[...]), axis=0, keepdims=True) * (TOKEN_MOST * 1.01 * (length + HALO))
    power = jnp.ceil(jnp.log(jnp.maximum(most, 1e-30)) * 1.4426950408889634 + 0.01)
    power_ref[:, : 3 * head] = jnp.broadcast_to(power, (8, 3 * head))
    power_ref[:, 3 * head :] = jnp.full((8, head), LAST_POWER, F32)


def call(kernel, outs, *args, scratch=()):
    def spec(arg):
        return pl.BlockSpec(memory_space=pltpu.SMEM if arg.ndim == 1 else pltpu.VMEM)

    return pl.pallas_call(
        kernel,
        out_shape=tuple(jax.ShapeDtypeStruct(shape, dtype) for shape, dtype in outs),
        in_specs=[spec(arg) for arg in args],
        out_specs=tuple(pl.BlockSpec(memory_space=pltpu.VMEM) for _ in outs),
        scratch_shapes=list(scratch),
        compiler_params=pltpu.CompilerParams(vmem_limit_bytes=VMEM_LIMIT),
    )(*args)


def pack(total, power):
    scaled = (total * jnp.exp2(TOP - power)).astype(F16)
    return jnp.concatenate([scaled, jnp.broadcast_to(power, (16, total.shape[1])).astype(F16)])


def unpack(packed):
    power = packed[-16:-15].astype(F32)
    return packed[:-16].astype(F32) * jnp.exp2(power - TOP), power


def swap(array, axis):
    return lax.ppermute(array, axis, [(0, 1), (1, 0)])


def turn(array, axis, by):
    size = lax.axis_size(axis)
    return lax.ppermute(array, axis, [(i, (i + by) % size) for i in range(size)])


def shift(array, axis, by):
    size = lax.axis_size(axis)
    return lax.ppermute(array, axis, [(i, i + by) for i in range(size) if 0 <= i + by < size])


def ordered(mine, other, index):
    return jnp.where(index == 0, jnp.stack([mine, other]), jnp.stack([other, mine]))


def pick(array, index):
    return lax.dynamic_index_in_dim(array, index, 0, keepdims=False)


def put(array, piece, index):
    return lax.dynamic_update_index_in_dim(array, piece, index, 0)


def outer(a, b):
    return lax.dot_general(a, b, (((0,), (0,)), ((), ())), preferred_element_type=F32)


def per_device(
    tokens, cotangent, doc_ids, projections, conv_weight, gate_down, gate_up, decay_log, beta_weight, norm_gain
):
    z, core, x, ylo, roll = (lax.axis_index(a) for a in ("z", "core", "x", "ylo", "roll"))
    nz, nx = lax.axis_size("z"), lax.axis_size("x")
    here = tokens.shape[1]
    head = norm_gain.shape[0]
    rows = projections.shape[0]
    length = 2 * here
    span = 4 * rows

    split = projections.reshape(rows, 4, 2, head)
    mine = lax.dynamic_index_in_dim(split, core, 2, keepdims=False).reshape(rows, 4 * head)
    theirs = lax.dynamic_index_in_dim(split, 1 - core, 2, keepdims=False).reshape(rows, 4 * head)
    chip_rows = ordered(mine, swap(theirs, "core"), core)
    piece = jnp.swapaxes(ordered(chip_rows, swap(chip_rows, "roll"), roll), 0, 1).reshape(span, 4 * head)

    block = jnp.stack([tokens[0].T, cotangent[0].T])
    pair = ordered(block, swap(block, "ylo"), ylo)
    behind, ahead = turn(pair, "x", 1), turn(pair, "x", -1)
    across = [turn(behind[:, 0], "x", 1), turn(ahead[:, 1], "x", -1)]

    def ring_order(i):
        full = jnp.zeros((nx,) + across[i].shape, across[i].dtype)
        for by, part in ((0, pair[:, i]), (1, behind[:, i]), (-1, ahead[:, i]), (2, across[i])):
            full = put(full, part, (x - by) % nx)
        return full.reshape(-1, here)

    features, upstream = ring_order(0), ring_order(1)
    model = features.shape[0]
    own = jnp.concatenate([features, jnp.broadcast_to((doc_ids + 1).astype(BF16), (16, here))])
    other = swap(own, "core")
    up_other = swap(upstream, "core")
    place = jnp.stack([z, core]).astype(jnp.int32)
    (halo,) = call(halo_kernel, [((HALO, model + 128), BF16)], place, own, other)
    halo = shift(halo, "z", 1)
    upstream, up_other = upstream.reshape(nz, span, here), up_other.reshape(nz, span, here)

    arrived = [piece]
    right = left = piece
    for k in range(1, nz // 2 + 1):
        right = turn(right, "z", 1)
        arrived.append(right)
        if k < nz // 2:
            left = turn(left, "z", -1)
            arrived.append(left)
    blocks, doc_columns, doc_row, projected, grow, beta, _ = call(
        gather_kernel,
        [
            ((nz, span, length + HALO), BF16), ((length, 8), F32), ((1, length), F32),
            ((length + HALO, 3 * head), F32), ((length, 3 * head), F32), ((length, head), F32), ((length, head), F32),
        ],
        place, decay_log, own, other, halo, gate_down.reshape(nz, span, head), beta_weight.T, gate_up, *arrived[:-1],
    )
    total, inverse, scores, wu, qo, maps, device_map, device_map16 = call(
        pre_kernel,
        [
            ((length, 3 * head), F32), ((length, length), F32), ((length, length), F32), ((length, 2 * head), F32),
            ((length, 2 * head), F32), ((length // BLOCK, head, 2 * head), F32), ((head, 2 * head), F32),
            ((head, 2 * head), BF16),
        ],
        place, blocks, arrived[-1], projected, grow, beta, conv_weight, doc_columns, doc_row,
        scratch=[pltpu.VMEM((length + HALO, 3 * head), F32)],
    )
    device_map, device_map16, late = lax.optimization_barrier((device_map, device_map16, place))
    (d_hidden,) = call(hidden_grad_kernel, [((length, head), F32)], late, upstream, up_other, *arrived)

    one, two = shift(device_map, "z", 1), shift(device_map16, "z", 2).astype(F32)
    joined = product(one[:, :head], two, (1, 0), HIGH)
    near = jnp.concatenate([joined[:, :head], joined[:, head:] + one[:, head:]], axis=1)
    far = shift(near[:, head:].astype(BF16), "z", 2)
    far_map = shift(near[:, :head].astype(BF16), "z", -3)
    hidden, d_out, pseudo, states, from_out, d_enter = call(
        mid_kernel,
        [
            ((length, head), BF16), ((length, head), F32), ((length, head), F32), ((length // BLOCK, head, head), F32),
            ((length // BLOCK, head, head), F32), ((head, head), F32),
        ],
        near, far, maps, wu, qo, d_hidden, norm_gain[None],
    )
    d_two = d_enter + lax.dot_general(
        device_map[:, :head], shift(d_enter, "z", -1), (((0,), (0,)), ((), ())), precision=HIGH
    )
    d_two, late = lax.optimization_barrier((d_two, hidden))
    d_near, d_far = shift(d_two, "z", -1), shift(d_two.astype(BF16), "z", -3)
    share, last = call(
        share_kernel,
        [((2, nz, span, here), F32), ((nz, span, head), F32)],
        place, late, upstream, up_other, *arrived,
    )
    from_core = swap((pick(share, 1 - core) * LIFT).astype(F16), "core")

    d_projected, power = call(
        post_kernel,
        [((length + HALO, 3 * head), BF16), ((8, 4 * head), F32)],
        place, d_near, d_far, far_map, maps, from_out, states, pseudo, d_out, inverse, scores, grow, total, beta,
        doc_columns, doc_row, conv_weight,
        scratch=[pltpu.VMEM((length + HALO, 3 * head), F32)],
    )

    own_power = power[:1]

    def part(by):
        index = (z + by) % nz
        first = jnp.dot(pick(blocks, index), d_projected, preferred_element_type=F32)
        return jnp.concatenate([first, pick(last, index)], axis=1)

    def add(packed, by):
        total, power = unpack(packed)
        return total + part(by), jnp.maximum(power, own_power) + 1.0

    half = nz // 2
    right = turn(pack(part(half), own_power), "z", 1)
    left = turn(pack(part(1 - half), own_power), "z", -1)
    right, left, from_core = lax.optimization_barrier((right, left, from_core))
    right = turn(pack(*add(right, half - 1)), "z", 1)
    left = turn(pack(*add(left, 2 - half)), "z", -1)
    shared = (pick(share, core) * LIFT + from_core.astype(F32)).reshape(nx, 2, span, here)
    from_ylo = swap(lax.dynamic_index_in_dim(shared, 1 - ylo, 1, keepdims=False).astype(F16), "ylo")
    right, left, from_ylo = lax.optimization_barrier((right, left, from_ylo))
    for k in range(2, half):
        right = turn(pack(*add(right, half - k)), "z", 1)
        if k < half - 1:
            left = turn(pack(*add(left, 1 - half + k)), "z", -1)
        if k == 2:
            shared = lax.dynamic_index_in_dim(shared, ylo, 1, keepdims=False) + from_ylo.astype(F32)
            from_x = [turn(pick(shared, (x + by) % nx).astype(F16), "x", by) for by in (1, -1, 2)]
        right, left = lax.optimization_barrier((right, left))
    layer_out = ((pick(shared, x) + sum(f.astype(F32) for f in from_x)) * (1.0 / LIFT)).T.astype(BF16)[None]
    total, power = add(right, 0)
    more, more_power = unpack(left)
    packed = pack(total + more, jnp.maximum(power, more_power) + 1.0)
    grad = unpack(packed)[0] + unpack(swap(packed, "roll"))[0]
    fresh = (piece.astype(F32) - RATE * grad).astype(BF16).reshape(2, span // 2, 4 * head)
    kept, sent = pick(fresh, core), pick(fresh, 1 - core)
    heads = ordered(kept, swap(sent, "core"), core).reshape(2, span // 2, 4, head)
    engine_tiles = jnp.moveaxis(heads, 0, 2).reshape(span // 2, 4, 2 * head)
    return (layer_out, engine_tiles)


def solution(mesh):
    fine = Mesh(mesh.devices.reshape(8, 2, 4, 2, 2), ("z", "core", "x", "ylo", "roll"))
    seq, mp = ("z", "core"), ("x", "ylo")
    in_specs = (
        P("roll", seq, mp),
        P("roll", seq, mp),
        P("roll", seq),
        P(("z", "core", "roll"), None, mp),
        P(None, None, mp),
        P(),
        P(None, mp),
        P(mp),
        P(None, mp),
        P(),
    )
    out_specs = (P("roll", seq, mp), P(seq, None, mp))
    return jax.shard_map(per_device, mesh=fine, in_specs=in_specs, out_specs=out_specs, check_vma=False)
```

```python
import jax
import jax.numpy as jnp
from jax import lax
from jax.experimental import pallas as pl
from jax.experimental.pallas import tpu as pltpu
from jax.sharding import Mesh
from jax.sharding import PartitionSpec as P

BLOCK = 64
TAPS = 4
HALO = 16
RATE = 0.01
TOKEN_MOST = 6.0
LAST_POWER = 16.0
TOP = 15.0
LIFT = 8.0
F32 = jnp.float32
F16 = jnp.float16
BF16 = jnp.bfloat16
HIGH = lax.Precision.HIGHEST
VMEM_LIMIT = 56 * 1024 * 1024


def product(a, b, dims, precision=None):
    return lax.dot_general(a, b, ((dims[:1], dims[1:]), ((), ())), precision=precision, preferred_element_type=F32)


def halves(a):
    high = a.astype(BF16)
    return high, (a - high.astype(F32)).astype(BF16)


def split_product(a, b, dims):
    (a_high, a_low), (b_high, b_low) = halves(a), halves(b)
    return product(a_high, b_high, dims) + (product(a_high, b_low, dims) + product(a_low, b_high, dims))


def mm(a, b):
    return split_product(a, b, (1, 0))


def mm_nt(a, b):
    return split_product(a, b, (1, 1))


def mm_tn(a, b):
    return mm(a.T, b)


def softplus(x):
    return jnp.maximum(x, 0.0) + jnp.log1p(jnp.exp(-jnp.abs(x)))


def masks(docs_ref, doc_row_ref):
    length = docs_ref.shape[0]
    row = lax.broadcasted_iota(jnp.int32, (length, length), 0)
    col = lax.broadcasted_iota(jnp.int32, (length, length), 1)
    inside = (row // BLOCK == col // BLOCK) & (row >= col)
    paired = docs_ref[:, 3:4] == doc_row_ref[...]
    inclusive = inside & paired
    strict = inclusive & (row > col)
    return row, col, inside, inclusive, strict


def carried_of(docs_ref):
    return (docs_ref[:, 3:4] == docs_ref[:, 4:5]).astype(F32)


def own_rows(core, here, skip=0):
    return pl.ds(pl.multiple_of(skip + core * here, 16), here)


def offset_of(k):
    return ((k + 1) // 2) * (-1 if k % 2 else 1)


def index_of(place_ref, k, size):
    return lax.rem(place_ref[0] + offset_of(k) + size, size)


def taps_of(conv_ref, core, head, j):
    here = pl.ds(pl.multiple_of(core * head, head), head)
    return jnp.concatenate([conv_ref[c, j : j + 1, here] for c in range(3)], axis=1)


def halo_kernel(place_ref, own_ref, other_ref, halo_ref):
    model, here = halo_ref.shape[1] - 128, own_ref.shape[1]
    last = jnp.where(place_ref[1] == 1, own_ref[...].astype(F32), other_ref[...].astype(F32))
    halo_ref[:, :model] = last[:model].T[here - HALO :].astype(BF16)
    row = lax.broadcasted_iota(jnp.int32, (HALO, here), 0)
    col = lax.broadcasted_iota(jnp.int32, (HALO, here), 1)
    docs = jnp.sum(jnp.where(col == row + (here - HALO), last[model : model + HALO], 0.0), axis=1, keepdims=True)
    halo_ref[:, model:] = jnp.broadcast_to(docs, (HALO, 128)).astype(BF16)


def gather_kernel(
    place_ref, decay_log_ref, own_ref, other_ref, halo_ref, gate_down_ref, beta_weight_ref, gate_up_ref, *refs
):
    pieces, (features_ref, docs_ref, doc_row_ref, proj_ref, grow_ref, beta_ref, decay_ref) = refs[:-7], refs[-7:]
    size, span, _ = features_ref.shape
    length, head = decay_ref.shape
    here, count, model = length // 2, length // BLOCK, size * span
    core = place_ref[1]
    halo = halo_ref[:, :model].T
    for k in range(size):
        rows = slice(k * span, (k + 1) * span)
        features_ref[k, :, :here] = own_ref[rows]
        features_ref[k, :, here:length] = other_ref[rows]
        features_ref[k, :, length:] = halo[rows]

    own_docs, other_docs = (ref[model : model + 16].astype(F32)[:1] for ref in (own_ref, other_ref))
    doc_row = jnp.where(
        core == 0, jnp.concatenate([own_docs, other_docs], axis=1), jnp.concatenate([other_docs, own_docs], axis=1)
    )
    doc_row_ref[...] = doc_row
    rim = halo_ref[:, model:].astype(F32)
    row = lax.broadcasted_iota(jnp.int32, (length, length), 0)
    col = lax.broadcasted_iota(jnp.int32, (length, length), 1)
    spot = lax.broadcasted_iota(jnp.int32, (length, 1), 0)

    def taken(line, target):
        return jnp.sum(jnp.where(col == target, line, 0.0), axis=1, keepdims=True)

    columns = []
    for back in (3, 2, 1, 0):
        column = taken(doc_row, row - back)
        for t in range(back):
            at = HALO + t - back
            column = jnp.where(spot == t, rim[at : at + 1, :1], column)
        columns.append(column)
    first = row // BLOCK * BLOCK
    prior = jnp.where(spot < BLOCK, rim[HALO - 1 : HALO, :1], taken(doc_row, first - 1))
    last = taken(doc_row, first + BLOCK - 1)
    docs_ref[...] = jnp.concatenate(columns + [prior, last, columns[3], columns[3]], axis=1)

    proj = jnp.zeros(proj_ref.shape, F32)
    low = jnp.zeros((length, head), F32)
    logits = jnp.zeros((beta_weight_ref.shape[0], features_ref.shape[2]), F32)
    for k in range(size):
        index = index_of(place_ref, k, size)
        rows = features_ref[index].T
        low = low + jnp.dot(rows[:length], gate_down_ref[index], preferred_element_type=F32)
        logits = logits + jnp.dot(
            beta_weight_ref[:, k * span : (k + 1) * span], features_ref[k], preferred_element_type=F32
        )
        if k < len(pieces):
            proj = proj + jnp.dot(rows, pieces[k][:, : 3 * head], preferred_element_type=F32)
    proj_ref[...] = proj
    gate_up = gate_up_ref[:, pl.ds(pl.multiple_of(core * head, head), head)]
    rates = jnp.dot(low.astype(BF16), gate_up, preferred_element_type=F32)
    log_decay = -jnp.exp(jnp.full((1, head), decay_log_ref[core])) * softplus(rates)
    logit = jnp.where(core == 0, logits[:1, :length], logits[1:2, :length])
    beta = jnp.broadcast_to(jax.nn.sigmoid(taken(logit, row)), (length, head))
    for ref, array in ((decay_ref, log_decay), (beta_ref, beta)):
        ref[own_rows(core, here)] = array[:here]
        ref[own_rows(1 - core, here)] = array[here:]
    inside = (row // BLOCK == col // BLOCK) & (row >= col)
    summed = product(inside.astype(F32), decay_ref[...], (1, 0), HIGH)
    ends = jnp.concatenate(
        [jnp.broadcast_to(summed[b * BLOCK + BLOCK - 1 : (b + 1) * BLOCK], (BLOCK, head)) for b in range(count)]
    )
    grow_ref[:, :head] = jnp.exp(summed)
    grow_ref[:, head : 2 * head] = jnp.exp(-summed)
    grow_ref[:, 2 * head :] = jnp.exp(ends - summed) * (columns[3] == last).astype(F32)


def hidden_grad_kernel(place_ref, up_ref, up_other_ref, *refs):
    pieces, d_hidden_ref = refs[:-1], refs[-1]
    size, here, (length, head) = up_ref.shape[0], up_ref.shape[2], d_hidden_ref.shape
    d_hidden = jnp.zeros((length, head), F32)
    for k, piece in enumerate(pieces):
        index = index_of(place_ref, k, size)
        both = jnp.concatenate([up_ref[index].T, up_other_ref[index].T])
        d_hidden = d_hidden + jnp.dot(both, piece[:, 3 * head :], preferred_element_type=F32)
    d_hidden_ref[own_rows(place_ref[1], here)] = d_hidden[:here]
    d_hidden_ref[own_rows(1 - place_ref[1], here)] = d_hidden[here:]


def pre_kernel(
    place_ref, features_ref, piece_ref, proj_in_ref,
    grow_ref, beta_ref, conv_ref, docs_ref, doc_row_ref,
    total_ref, inv_ref, score_ref, wu_ref, qo_ref, maps_ref, device_map_ref, device_map16_ref,
    ext_ref,
):
    length, head = beta_ref.shape
    here, count = length // 2, length // BLOCK
    size, core = features_ref.shape[0], place_ref[1]
    index = index_of(place_ref, size - 1, size)
    proj = proj_in_ref[...] + jnp.dot(features_ref[index].T, piece_ref[:, : 3 * head], preferred_element_type=F32)
    ext_ref[:HALO] = proj[length:]
    ext_ref[own_rows(core, here, HALO)] = proj[:here]
    ext_ref[own_rows(1 - core, here, HALO)] = proj[here:length]
    total = jnp.zeros((length, 3 * head), F32)
    for j in range(TAPS):
        same = (docs_ref[:, j : j + 1] == docs_ref[:, 3:4]).astype(F32)
        total = total + ext_ref[HALO - 3 + j : HALO - 3 + j + length] * taps_of(conv_ref, core, head, j) * same
    total_ref[...] = total
    active = total * jax.nn.sigmoid(total)
    query, keys, values = active[:, :head], active[:, head : 2 * head], active[:, 2 * head :]
    query = query * lax.rsqrt(jnp.sum(query * query, axis=1, keepdims=True) + 1e-6)
    keys = keys * lax.rsqrt(jnp.sum(keys * keys, axis=1, keepdims=True) + 1e-6)
    beta = beta_ref[:, :1]
    row, col, _, inclusive, strict = masks(docs_ref, doc_row_ref)
    carried = carried_of(docs_ref)
    grow, shrink, tail = grow_ref[:, :head], grow_ref[:, head : 2 * head], grow_ref[:, 2 * head :]
    key_grow, key_shrink, query_grow, key_tail = keys * grow, keys * shrink, query * grow, keys * tail
    both = mm_nt(jnp.concatenate([key_grow, query_grow]), key_shrink)
    lower = jnp.where(strict, both[:length], 0.0) * beta
    scores = jnp.where(inclusive, both[length:], 0.0)
    score_ref[...] = scores
    inverse = (row == col).astype(F32) - jnp.where(row // 2 == col // 2, lower, 0.0)
    size = 2
    while size < BLOCK:
        corner = jnp.where((row // (2 * size) == col // (2 * size)) & (row // size != col // size), lower, 0.0)
        inverse = inverse - mm(inverse, mm(corner, inverse))
        size *= 2
    inv_ref[...] = inverse
    wu = mm(inverse, jnp.concatenate([beta * carried * key_grow, beta * values], axis=1))
    wu_ref[...] = wu
    mixed = mm(scores, wu)
    qo_ref[:, :head] = carried * query_grow - mixed[:, :head]
    qo_ref[:, head:] = mixed[:, head:]
    eye = lax.broadcasted_iota(jnp.int32, (head, head), 0) == lax.broadcasted_iota(jnp.int32, (head, head), 1)
    pairs = []
    for b in range(count):
        rows = slice(b * BLOCK, (b + 1) * BLOCK)
        last = (b + 1) * BLOCK - 1
        keep = grow[last : last + 1] * carried[last : last + 1]
        update = mm_tn(key_tail[rows], wu[rows])
        moved = jnp.where(eye, keep, 0.0) - update[:, :head]
        maps_ref[b, :, :head] = moved
        maps_ref[b, :, head:] = update[:, head:]
        pairs.append((moved, update[:, head:]))

    def after(second, first):
        made = mm(second[0], jnp.concatenate(first, axis=1))
        return (made[:, :head], made[:, head:] + second[1])

    while len(pairs) > 1:
        pairs = [after(pairs[i + 1], pairs[i]) for i in range(0, len(pairs), 2)]
    device_map_ref[:, :head] = pairs[0][0]
    device_map_ref[:, head:] = pairs[0][1]
    device_map16_ref[:, :head] = pairs[0][0].astype(BF16)
    device_map16_ref[:, head:] = pairs[0][1].astype(BF16)


def mid_kernel(
    near_ref, far_ref, maps_ref, wu_ref, qo_ref, d_hidden_ref, gain_ref,
    hidden_ref, d_out_ref, pseudo_ref, states_ref, from_out_ref, d_enter_ref,
):
    length, head = d_hidden_ref.shape
    count = length // BLOCK
    state = near_ref[:, head:] + mm(near_ref[:, :head], far_ref[...].astype(F32))
    states = []
    for b in range(count):
        states.append(state)
        states_ref[b] = state
        if b < count - 1:
            state = mm(maps_ref[b, :, :head], state) + maps_ref[b, :, head:]
    outs, pseudos = [], []
    for b in range(count):
        rows = slice(b * BLOCK, (b + 1) * BLOCK)
        made = mm(jnp.concatenate([qo_ref[rows, :head], wu_ref[rows, :head]]), states[b])
        outs.append(qo_ref[rows, head:] + made[:BLOCK])
        pseudos.append(wu_ref[rows, head:] - made[BLOCK:])
    out = jnp.concatenate(outs)
    pseudo_ref[...] = jnp.concatenate(pseudos)
    scale = lax.rsqrt(jnp.mean(out * out, axis=1, keepdims=True) + 1e-5)
    hidden_ref[...] = (out * scale * gain_ref[...]).astype(BF16)
    lifted = d_hidden_ref[...] * gain_ref[...]
    d_out = scale * lifted - out * (scale * scale * scale) * jnp.mean(lifted * out, axis=1, keepdims=True)
    d_out_ref[...] = d_out
    d_state = None
    for b in reversed(range(count)):
        rows = slice(b * BLOCK, (b + 1) * BLOCK)
        part = mm_tn(qo_ref[rows, :head], d_out[rows])
        from_out_ref[b] = part
        d_state = part if d_state is None else part + mm_tn(maps_ref[b, :, :head], d_state)
    d_enter_ref[...] = d_state


def share_kernel(place_ref, hidden_ref, *refs):
    pieces, share_ref = refs[:-1], refs[-1]
    size, here, head = share_ref.shape[1], share_ref.shape[3], hidden_ref.shape[1]
    for k, piece in enumerate(pieces):
        index = index_of(place_ref, k, size)
        for c in range(2):
            share_ref[c, index] = lax.dot_general(
                piece[:, 3 * head :], hidden_ref[c * here : (c + 1) * here], (((1,), (1,)), ((), ())),
                preferred_element_type=F32,
            )


def last_kernel(place_ref, hidden_ref, up_ref, up_other_ref, last_ref):
    here, core = up_ref.shape[2], place_ref[1]
    own, other = hidden_ref[own_rows(core, here)], hidden_ref[own_rows(1 - core, here)]
    for k in range(up_ref.shape[0]):
        last_ref[k] = jnp.dot(up_ref[k], own, preferred_element_type=F32) + jnp.dot(
            up_other_ref[k], other, preferred_element_type=F32
        )


def post_kernel(
    place_ref, near_ref, far_ref, far_map_ref, maps_ref, from_out_ref, states_ref, pseudo_ref, d_out_ref, inv_ref,
    score_ref, grow_ref, total_ref, beta_ref, docs_ref, doc_row_ref, conv_ref, features_ref, last_ref,
    d_proj_ref, power_ref, right_ref, left_ref,
    d_ext_ref,
):
    length, head = d_out_ref.shape
    count = length // BLOCK
    core, here = place_ref[1], length // 2
    d_state = near_ref[...] + lax.dot_general(
        far_map_ref[...].T, far_ref[...], (((1,), (0,)), ((), ())), preferred_element_type=F32
    )
    d_after = [None] * count
    for b in reversed(range(count)):
        d_after[b] = d_state
        if b > 0:
            d_state = from_out_ref[b] + mm_tn(maps_ref[b, :, :head], d_state)
    total = total_ref[...]
    gate = jax.nn.sigmoid(total)
    active = total * gate
    raw_q, raw_k = active[:, :head], active[:, head : 2 * head]
    inv_q = lax.rsqrt(jnp.sum(raw_q * raw_q, axis=1, keepdims=True) + 1e-6)
    inv_k = lax.rsqrt(jnp.sum(raw_k * raw_k, axis=1, keepdims=True) + 1e-6)
    query, keys = raw_q * inv_q, raw_k * inv_k
    grow, shrink, tail = grow_ref[:, :head], grow_ref[:, head : 2 * head], grow_ref[:, 2 * head :]
    key_grow, key_shrink, query_grow, key_tail = keys * grow, keys * shrink, query * grow, keys * tail
    beta = beta_ref[:, :1]
    _, _, _, inclusive, strict = masks(docs_ref, doc_row_ref)
    carried = carried_of(docs_ref)
    d_out, pseudo = d_out_ref[...], pseudo_ref[...]

    def each(function):
        return jnp.concatenate([function(b, slice(b * BLOCK, (b + 1) * BLOCK)) for b in range(count)])

    d_pseudo = mm_tn(score_ref[...], d_out) + each(lambda b, rows: mm(key_tail[rows], d_after[b]))
    d_target = mm_tn(inv_ref[...], d_pseudo)
    both = mm_nt(jnp.concatenate([d_out, d_target]), pseudo)
    d_scores = jnp.where(inclusive, both[:length], 0.0)
    d_lower = jnp.where(strict, both[length:], 0.0) * (-beta)
    d_values = beta * d_target
    d_from_keys = -carried * d_values
    lifted_out = carried * d_out
    d_query_grow = each(lambda b, rows: mm_nt(lifted_out[rows], states_ref[b])) + mm(d_scores, key_shrink)
    d_key_grow = each(lambda b, rows: mm_nt(d_from_keys[rows], states_ref[b])) + mm(d_lower, key_shrink)
    d_key_shrink = mm_tn(d_scores, query_grow) + mm_tn(d_lower, key_grow)
    d_key_tail = each(lambda b, rows: mm_nt(pseudo[rows], d_after[b]))
    d_query = d_query_grow * grow
    d_keys = d_key_grow * grow + d_key_shrink * shrink + d_key_tail * tail
    d_query = inv_q * d_query - query * (inv_q * jnp.sum(d_query * query, axis=1, keepdims=True))
    d_keys = inv_k * d_keys - keys * (inv_k * jnp.sum(d_keys * keys, axis=1, keepdims=True))
    d_total = jnp.concatenate([d_query, d_keys, d_values], axis=1) * (gate * (1.0 + total * (1.0 - gate)))
    d_ext_ref[...] = jnp.zeros_like(d_ext_ref)
    for j in range(TAPS):
        same = (docs_ref[:, j : j + 1] == docs_ref[:, 3:4]).astype(F32)
        spot = slice(HALO - 3 + j, HALO - 3 + j + length)
        d_ext_ref[spot] = d_ext_ref[spot] + d_total * taps_of(conv_ref, core, head, j) * same
    d_proj_ref[:here] = d_ext_ref[own_rows(core, here, HALO)].astype(BF16)
    d_proj_ref[here:length] = d_ext_ref[own_rows(1 - core, here, HALO)].astype(BF16)
    d_proj_ref[length:] = d_ext_ref[:HALO].astype(BF16)
    most = jnp.max(jnp.abs(d_ext_ref[...]), axis=0, keepdims=True) * (TOKEN_MOST * 1.01 * (length + HALO))
    power = jnp.ceil(jnp.log(jnp.maximum(most, 1e-30)) * 1.4426950408889634 + 0.01)
    power = jnp.concatenate([power, jnp.full((1, head), LAST_POWER, F32)], axis=1)
    power_ref[...] = jnp.broadcast_to(power, power_ref.shape)
    size, span, _ = features_ref.shape
    scale = jnp.exp2(TOP - power)
    for ref, by in ((right_ref, size // 2), (left_ref, size // 2 + 1)):
        index = lax.rem(place_ref[0] + by, size)
        first = jnp.dot(features_ref[index], d_proj_ref[...], preferred_element_type=F32)
        ref[:span, : 3 * head] = (first * scale[:, : 3 * head]).astype(ref.dtype)
        ref[:span, 3 * head :] = (last_ref[index] * scale[:, 3 * head :]).astype(ref.dtype)
        ref[span:] = jnp.broadcast_to(power, (16, 4 * head)).astype(ref.dtype)


def call(kernel, outs, *args, scratch=()):
    def spec(arg):
        return pl.BlockSpec(memory_space=pltpu.SMEM if arg.ndim == 1 else pltpu.VMEM)

    return pl.pallas_call(
        kernel,
        out_shape=tuple(jax.ShapeDtypeStruct(shape, dtype) for shape, dtype in outs),
        in_specs=[spec(arg) for arg in args],
        out_specs=tuple(pl.BlockSpec(memory_space=pltpu.VMEM) for _ in outs),
        scratch_shapes=list(scratch),
        compiler_params=pltpu.CompilerParams(vmem_limit_bytes=VMEM_LIMIT),
    )(*args)


def pack(total, power):
    scaled = (total * jnp.exp2(TOP - power)).astype(F16)
    return jnp.concatenate([scaled, jnp.broadcast_to(power, (16, total.shape[1])).astype(F16)])


def unpack(packed):
    power = packed[-16:-15].astype(F32)
    return packed[:-16].astype(F32) * jnp.exp2(power - TOP), power


def swap(array, axis):
    return lax.ppermute(array, axis, [(0, 1), (1, 0)])


def turn(array, axis, by):
    size = lax.axis_size(axis)
    return lax.ppermute(array, axis, [(i, (i + by) % size) for i in range(size)])


def shift(array, axis, by):
    size = lax.axis_size(axis)
    return lax.ppermute(array, axis, [(i, i + by) for i in range(size) if 0 <= i + by < size])


def ordered(mine, other, index):
    return jnp.where(index == 0, jnp.stack([mine, other]), jnp.stack([other, mine]))


def pick(array, index):
    return lax.dynamic_index_in_dim(array, index, 0, keepdims=False)


def put(array, piece, index):
    return lax.dynamic_update_index_in_dim(array, piece, index, 0)


def outer(a, b):
    return lax.dot_general(a, b, (((0,), (0,)), ((), ())), preferred_element_type=F32)


def per_device(
    tokens, cotangent, doc_ids, projections, conv_weight, gate_down, gate_up, decay_log, beta_weight, norm_gain
):
    z, core, x, ylo, roll = (lax.axis_index(a) for a in ("z", "core", "x", "ylo", "roll"))
    nz, nx = lax.axis_size("z"), lax.axis_size("x")
    here = tokens.shape[1]
    head = norm_gain.shape[0]
    rows = projections.shape[0]
    length = 2 * here
    span = 4 * rows

    split = projections.reshape(rows, 4, 2, head)
    mine = lax.dynamic_index_in_dim(split, core, 2, keepdims=False).reshape(rows, 4 * head)
    theirs = lax.dynamic_index_in_dim(split, 1 - core, 2, keepdims=False).reshape(rows, 4 * head)
    chip_rows = ordered(mine, swap(theirs, "core"), core)
    piece = jnp.swapaxes(ordered(chip_rows, swap(chip_rows, "roll"), roll), 0, 1).reshape(span, 4 * head)

    block = jnp.stack([tokens[0].T, cotangent[0].T])
    pair = ordered(block, swap(block, "ylo"), ylo)
    behind, ahead = turn(pair, "x", 1), turn(pair, "x", -1)
    across = [turn(behind[:, 0], "x", 1), turn(ahead[:, 1], "x", -1)]

    def ring_order(i):
        full = jnp.zeros((nx,) + across[i].shape, across[i].dtype)
        for by, part in ((0, pair[:, i]), (1, behind[:, i]), (-1, ahead[:, i]), (2, across[i])):
            full = put(full, part, (x - by) % nx)
        return full.reshape(-1, here)

    features, upstream = ring_order(0), ring_order(1)
    model = features.shape[0]
    own = jnp.concatenate([features, jnp.broadcast_to((doc_ids + 1).astype(BF16), (16, here))])
    other = swap(own, "core")
    up_other = swap(upstream, "core")
    place = jnp.stack([z, core]).astype(jnp.int32)
    (halo,) = call(halo_kernel, [((HALO, model + 128), BF16)], place, own, other)
    halo = shift(halo, "z", 1)
    upstream, up_other = upstream.reshape(nz, span, here), up_other.reshape(nz, span, here)

    arrived = [piece]
    right = left = piece
    for k in range(1, nz // 2 + 1):
        right = turn(right, "z", 1)
        arrived.append(right)
        if k < nz // 2:
            left = turn(left, "z", -1)
            arrived.append(left)
    blocks, doc_columns, doc_row, projected, grow, beta, _ = call(
        gather_kernel,
        [
            ((nz, span, length + HALO), BF16), ((length, 8), F32), ((1, length), F32),
            ((length + HALO, 3 * head), F32), ((length, 3 * head), F32), ((length, head), F32), ((length, head), F32),
        ],
        place, decay_log, own, other, halo, gate_down.reshape(nz, span, head), beta_weight.T, gate_up, *arrived[:-1],
    )
    total, inverse, scores, wu, qo, maps, device_map, device_map16 = call(
        pre_kernel,
        [
            ((length, 3 * head), F32), ((length, length), F32), ((length, length), F32), ((length, 2 * head), F32),
            ((length, 2 * head), F32), ((length // BLOCK, head, 2 * head), F32), ((head, 2 * head), F32),
            ((head, 2 * head), BF16),
        ],
        place, blocks, arrived[-1], projected, grow, beta, conv_weight, doc_columns, doc_row,
        scratch=[pltpu.VMEM((length + HALO, 3 * head), F32)],
    )
    device_map, device_map16, late = lax.optimization_barrier((device_map, device_map16, place))
    (d_hidden,) = call(hidden_grad_kernel, [((length, head), F32)], late, upstream, up_other, *arrived)

    one, two = shift(device_map, "z", 1), shift(device_map16, "z", 2).astype(F32)
    joined = product(one[:, :head], two, (1, 0), HIGH)
    near = jnp.concatenate([joined[:, :head], joined[:, head:] + one[:, head:]], axis=1)
    far = shift(near[:, head:].astype(BF16), "z", 2)
    far_map = shift(near[:, :head].astype(BF16), "z", -3)
    hidden, d_out, pseudo, states, from_out, d_enter = call(
        mid_kernel,
        [
            ((length, head), BF16), ((length, head), F32), ((length, head), F32), ((length // BLOCK, head, head), F32),
            ((length // BLOCK, head, head), F32), ((head, head), F32),
        ],
        near, far, maps, wu, qo, d_hidden, norm_gain[None],
    )
    d_two = d_enter + lax.dot_general(
        device_map[:, :head], shift(d_enter, "z", -1), (((0,), (0,)), ((), ())), precision=HIGH
    )
    d_two, late = lax.optimization_barrier((d_two, hidden))
    d_near, d_far = shift(d_two, "z", -1), shift(d_two.astype(BF16), "z", -3)
    (last,) = call(last_kernel, [((nz, span, head), F32)], place, late, upstream, up_other)
    d_projected, power, right, left = call(
        post_kernel,
        [((length + HALO, 3 * head), BF16), ((8, 4 * head), F32)] + [((span + 16, 4 * head), F32)] * 2,
        place, d_near, d_far, far_map, maps, from_out, states, pseudo, d_out, inverse, scores, grow, total, beta,
        doc_columns, doc_row, conv_weight, blocks, last,
        scratch=[pltpu.VMEM((length + HALO, 3 * head), F32)],
    )

    own_power = power[:1]

    def part(by):
        index = (z + by) % nz
        first = jnp.dot(pick(blocks, index), d_projected, preferred_element_type=F32)
        return jnp.concatenate([first, pick(last, index)], axis=1)

    def add(packed, by):
        total, power = unpack(packed)
        return total + part(by), jnp.maximum(power, own_power) + 1.0

    half = nz // 2
    late, d_projected = lax.optimization_barrier((hidden, d_projected))
    right, left = turn(right.astype(F16), "z", 1), turn(left.astype(F16), "z", -1)
    (share,) = call(share_kernel, [((2, nz, span, here), F32)], place, late, *arrived)
    from_core = swap((pick(share, 1 - core) * LIFT).astype(F16), "core")
    right, left, from_core = lax.optimization_barrier((right, left, from_core))
    right = turn(pack(*add(right, half - 1)), "z", 1)
    left = turn(pack(*add(left, 2 - half)), "z", -1)
    shared = (pick(share, core) * LIFT + from_core.astype(F32)).reshape(nx, 2, span, here)
    from_ylo = swap(lax.dynamic_index_in_dim(shared, 1 - ylo, 1, keepdims=False).astype(F16), "ylo")
    right, left, from_ylo = lax.optimization_barrier((right, left, from_ylo))
    for k in range(2, half):
        right = turn(pack(*add(right, half - k)), "z", 1)
        if k < half - 1:
            left = turn(pack(*add(left, 1 - half + k)), "z", -1)
        if k == 2:
            shared = lax.dynamic_index_in_dim(shared, ylo, 1, keepdims=False) + from_ylo.astype(F32)
            from_x = [turn(pick(shared, (x + by) % nx).astype(F16), "x", by) for by in (1, -1, 2)]
        right, left = lax.optimization_barrier((right, left))
    layer_out = ((pick(shared, x) + sum(f.astype(F32) for f in from_x)) * (1.0 / LIFT)).T.astype(BF16)[None]
    total, power = add(right, 0)
    more, more_power = unpack(left)
    packed = pack(total + more, jnp.maximum(power, more_power) + 1.0)
    grad = unpack(packed)[0] + unpack(swap(packed, "roll"))[0]
    fresh = (piece.astype(F32) - RATE * grad).astype(BF16).reshape(2, span // 2, 4 * head)
    kept, sent = pick(fresh, core), pick(fresh, 1 - core)
    heads = ordered(kept, swap(sent, "core"), core).reshape(2, span // 2, 4, head)
    engine_tiles = jnp.moveaxis(heads, 0, 2).reshape(span // 2, 4, 2 * head)
    return (layer_out, engine_tiles)


def solution(mesh):
    fine = Mesh(mesh.devices.reshape(8, 2, 4, 2, 2), ("z", "core", "x", "ylo", "roll"))
    seq, mp = ("z", "core"), ("x", "ylo")
    in_specs = (
        P("roll", seq, mp),
        P("roll", seq, mp),
        P("roll", seq),
        P(("z", "core", "roll"), None, mp),
        P(None, None, mp),
        P(),
        P(None, mp),
        P(mp),
        P(None, mp),
        P(),
    )
    out_specs = (P("roll", seq, mp), P(seq, None, mp))
    return jax.shard_map(per_device, mesh=fine, in_specs=in_specs, out_specs=out_specs, check_vma=False)
```

```python
import jax
import jax.numpy as jnp
from jax import lax
from jax.experimental import pallas as pl
from jax.experimental.pallas import tpu as pltpu
from jax.sharding import Mesh
from jax.sharding import PartitionSpec as P

BLOCK = 64
TAPS = 4
HALO = 16
RATE = 0.01
TOKEN_MOST = 6.0
LAST_POWER = 16.0
TOP = 15.0
LIFT = 8.0
F32 = jnp.float32
F16 = jnp.float16
BF16 = jnp.bfloat16
HIGH = lax.Precision.HIGHEST
VMEM_LIMIT = 56 * 1024 * 1024


def product(a, b, dims, precision=None):
    return lax.dot_general(a, b, ((dims[:1], dims[1:]), ((), ())), precision=precision, preferred_element_type=F32)


def halves(a):
    high = a.astype(BF16)
    return high, (a - high.astype(F32)).astype(BF16)


def split_product(a, b, dims):
    (a_high, a_low), (b_high, b_low) = halves(a), halves(b)
    return product(a_high, b_high, dims) + (product(a_high, b_low, dims) + product(a_low, b_high, dims))


def mm(a, b):
    return split_product(a, b, (1, 0))


def mm_nt(a, b):
    return split_product(a, b, (1, 1))


def mm_tn(a, b):
    return mm(a.T, b)


def softplus(x):
    return jnp.maximum(x, 0.0) + jnp.log1p(jnp.exp(-jnp.abs(x)))


def masks(docs_ref, doc_row_ref):
    length = docs_ref.shape[0]
    row = lax.broadcasted_iota(jnp.int32, (length, length), 0)
    col = lax.broadcasted_iota(jnp.int32, (length, length), 1)
    inside = (row // BLOCK == col // BLOCK) & (row >= col)
    paired = docs_ref[:, 3:4] == doc_row_ref[...]
    inclusive = inside & paired
    strict = inclusive & (row > col)
    return row, col, inside, inclusive, strict


def carried_of(docs_ref):
    return (docs_ref[:, 3:4] == docs_ref[:, 4:5]).astype(F32)


def own_rows(core, here, skip=0):
    return pl.ds(pl.multiple_of(skip + core * here, 16), here)


def offset_of(k):
    return ((k + 1) // 2) * (-1 if k % 2 else 1)


def index_of(place_ref, k, size):
    return lax.rem(place_ref[0] + offset_of(k) + size, size)


def taps_of(conv_ref, core, head, j):
    here = pl.ds(pl.multiple_of(core * head, head), head)
    return jnp.concatenate([conv_ref[c, j : j + 1, here] for c in range(3)], axis=1)


def halo_kernel(place_ref, own_ref, other_ref, halo_ref):
    model, here = halo_ref.shape[1] - 128, own_ref.shape[1]
    last = jnp.where(place_ref[1] == 1, own_ref[...].astype(F32), other_ref[...].astype(F32))
    halo_ref[:, :model] = last[:model].T[here - HALO :].astype(BF16)
    row = lax.broadcasted_iota(jnp.int32, (HALO, here), 0)
    col = lax.broadcasted_iota(jnp.int32, (HALO, here), 1)
    docs = jnp.sum(jnp.where(col == row + (here - HALO), last[model : model + HALO], 0.0), axis=1, keepdims=True)
    halo_ref[:, model:] = jnp.broadcast_to(docs, (HALO, 128)).astype(BF16)


def gather_kernel(
    place_ref, decay_log_ref, own_ref, other_ref, halo_ref, gate_down_ref, beta_weight_ref, gate_up_ref, *refs
):
    pieces, (features_ref, docs_ref, doc_row_ref, proj_ref, grow_ref, beta_ref, decay_ref) = refs[:-7], refs[-7:]
    size, span, _ = features_ref.shape
    length, head = decay_ref.shape
    here, count, model = length // 2, length // BLOCK, size * span
    core = place_ref[1]
    halo = halo_ref[:, :model].T
    for k in range(size):
        rows = slice(k * span, (k + 1) * span)
        features_ref[k, :, :here] = own_ref[rows]
        features_ref[k, :, here:length] = other_ref[rows]
        features_ref[k, :, length:] = halo[rows]

    own_docs, other_docs = (ref[model : model + 16].astype(F32)[:1] for ref in (own_ref, other_ref))
    doc_row = jnp.where(
        core == 0, jnp.concatenate([own_docs, other_docs], axis=1), jnp.concatenate([other_docs, own_docs], axis=1)
    )
    doc_row_ref[...] = doc_row
    rim = halo_ref[:, model:].astype(F32)
    row = lax.broadcasted_iota(jnp.int32, (length, length), 0)
    col = lax.broadcasted_iota(jnp.int32, (length, length), 1)
    spot = lax.broadcasted_iota(jnp.int32, (length, 1), 0)

    def taken(line, target):
        return jnp.sum(jnp.where(col == target, line, 0.0), axis=1, keepdims=True)

    columns = []
    for back in (3, 2, 1, 0):
        column = taken(doc_row, row - back)
        for t in range(back):
            at = HALO + t - back
            column = jnp.where(spot == t, rim[at : at + 1, :1], column)
        columns.append(column)
    first = row // BLOCK * BLOCK
    prior = jnp.where(spot < BLOCK, rim[HALO - 1 : HALO, :1], taken(doc_row, first - 1))
    last = taken(doc_row, first + BLOCK - 1)
    docs_ref[...] = jnp.concatenate(columns + [prior, last, columns[3], columns[3]], axis=1)

    proj = jnp.zeros(proj_ref.shape, F32)
    low = jnp.zeros((length, head), F32)
    logits = jnp.zeros((beta_weight_ref.shape[0], features_ref.shape[2]), F32)
    for k in range(size):
        index = index_of(place_ref, k, size)
        rows = features_ref[index].T
        low = low + jnp.dot(rows[:length], gate_down_ref[index], preferred_element_type=F32)
        logits = logits + jnp.dot(
            beta_weight_ref[:, k * span : (k + 1) * span], features_ref[k], preferred_element_type=F32
        )
        if k < len(pieces):
            proj = proj + jnp.dot(rows, pieces[k][:, : 3 * head], preferred_element_type=F32)
    proj_ref[...] = proj
    gate_up = gate_up_ref[:, pl.ds(pl.multiple_of(core * head, head), head)]
    rates = jnp.dot(low.astype(BF16), gate_up, preferred_element_type=F32)
    log_decay = -jnp.exp(jnp.full((1, head), decay_log_ref[core])) * softplus(rates)
    logit = jnp.where(core == 0, logits[:1, :length], logits[1:2, :length])
    beta = jnp.broadcast_to(jax.nn.sigmoid(taken(logit, row)), (length, head))
    for ref, array in ((decay_ref, log_decay), (beta_ref, beta)):
        ref[own_rows(core, here)] = array[:here]
        ref[own_rows(1 - core, here)] = array[here:]
    inside = (row // BLOCK == col // BLOCK) & (row >= col)
    summed = product(inside.astype(F32), decay_ref[...], (1, 0), HIGH)
    ends = jnp.concatenate(
        [jnp.broadcast_to(summed[b * BLOCK + BLOCK - 1 : (b + 1) * BLOCK], (BLOCK, head)) for b in range(count)]
    )
    grow_ref[:, :head] = jnp.exp(summed)
    grow_ref[:, head : 2 * head] = jnp.exp(-summed)
    grow_ref[:, 2 * head :] = jnp.exp(ends - summed) * (columns[3] == last).astype(F32)


def hidden_grad_kernel(place_ref, up_ref, up_other_ref, *refs):
    pieces, d_hidden_ref = refs[:-1], refs[-1]
    size, here, (length, head) = up_ref.shape[0], up_ref.shape[2], d_hidden_ref.shape
    d_hidden = jnp.zeros((length, head), F32)
    for k, piece in enumerate(pieces):
        index = index_of(place_ref, k, size)
        both = jnp.concatenate([up_ref[index].T, up_other_ref[index].T])
        d_hidden = d_hidden + jnp.dot(both, piece[:, 3 * head :], preferred_element_type=F32)
    d_hidden_ref[own_rows(place_ref[1], here)] = d_hidden[:here]
    d_hidden_ref[own_rows(1 - place_ref[1], here)] = d_hidden[here:]


def pre_kernel(
    place_ref, features_ref, piece_ref, proj_in_ref,
    grow_ref, beta_ref, conv_ref, docs_ref, doc_row_ref,
    total_ref, inv_ref, score_ref, wu_ref, qo_ref, maps_ref, device_map_ref, device_map16_ref,
    ext_ref,
):
    length, head = beta_ref.shape
    here, count = length // 2, length // BLOCK
    size, core = features_ref.shape[0], place_ref[1]
    index = index_of(place_ref, size - 1, size)
    proj = proj_in_ref[...] + jnp.dot(features_ref[index].T, piece_ref[:, : 3 * head], preferred_element_type=F32)
    ext_ref[:HALO] = proj[length:]
    ext_ref[own_rows(core, here, HALO)] = proj[:here]
    ext_ref[own_rows(1 - core, here, HALO)] = proj[here:length]
    total = jnp.zeros((length, 3 * head), F32)
    for j in range(TAPS):
        same = (docs_ref[:, j : j + 1] == docs_ref[:, 3:4]).astype(F32)
        total = total + ext_ref[HALO - 3 + j : HALO - 3 + j + length] * taps_of(conv_ref, core, head, j) * same
    total_ref[...] = total
    active = total * jax.nn.sigmoid(total)
    query, keys, values = active[:, :head], active[:, head : 2 * head], active[:, 2 * head :]
    query = query * lax.rsqrt(jnp.sum(query * query, axis=1, keepdims=True) + 1e-6)
    keys = keys * lax.rsqrt(jnp.sum(keys * keys, axis=1, keepdims=True) + 1e-6)
    beta = beta_ref[:, :1]
    row, col, _, inclusive, strict = masks(docs_ref, doc_row_ref)
    carried = carried_of(docs_ref)
    grow, shrink, tail = grow_ref[:, :head], grow_ref[:, head : 2 * head], grow_ref[:, 2 * head :]
    key_grow, key_shrink, query_grow, key_tail = keys * grow, keys * shrink, query * grow, keys * tail
    both = mm_nt(jnp.concatenate([key_grow, query_grow]), key_shrink)
    lower = jnp.where(strict, both[:length], 0.0) * beta
    scores = jnp.where(inclusive, both[length:], 0.0)
    score_ref[...] = scores
    inverse = (row == col).astype(F32) - jnp.where(row // 2 == col // 2, lower, 0.0)
    size = 2
    while size < BLOCK:
        corner = jnp.where((row // (2 * size) == col // (2 * size)) & (row // size != col // size), lower, 0.0)
        inverse = inverse - mm(inverse, mm(corner, inverse))
        size *= 2
    inv_ref[...] = inverse
    wu = mm(inverse, jnp.concatenate([beta * carried * key_grow, beta * values], axis=1))
    wu_ref[...] = wu
    mixed = mm(scores, wu)
    qo_ref[:, :head] = carried * query_grow - mixed[:, :head]
    qo_ref[:, head:] = mixed[:, head:]
    eye = lax.broadcasted_iota(jnp.int32, (head, head), 0) == lax.broadcasted_iota(jnp.int32, (head, head), 1)
    pairs = []
    for b in range(count):
        rows = slice(b * BLOCK, (b + 1) * BLOCK)
        last = (b + 1) * BLOCK - 1
        keep = grow[last : last + 1] * carried[last : last + 1]
        update = mm_tn(key_tail[rows], wu[rows])
        moved = jnp.where(eye, keep, 0.0) - update[:, :head]
        maps_ref[b, :, :head] = moved
        maps_ref[b, :, head:] = update[:, head:]
        pairs.append((moved, update[:, head:]))

    def after(second, first):
        made = mm(second[0], jnp.concatenate(first, axis=1))
        return (made[:, :head], made[:, head:] + second[1])

    while len(pairs) > 1:
        pairs = [after(pairs[i + 1], pairs[i]) for i in range(0, len(pairs), 2)]
    device_map_ref[:, :head] = pairs[0][0]
    device_map_ref[:, head:] = pairs[0][1]
    device_map16_ref[:, :head] = pairs[0][0].astype(BF16)
    device_map16_ref[:, head:] = pairs[0][1].astype(BF16)


def mid_kernel(
    near_ref, far_ref, maps_ref, wu_ref, qo_ref, d_hidden_ref, gain_ref,
    hidden_ref, d_out_ref, pseudo_ref, states_ref, from_out_ref, d_enter_ref,
):
    length, head = d_hidden_ref.shape
    count = length // BLOCK
    state = near_ref[:, head:] + mm(near_ref[:, :head], far_ref[...].astype(F32))
    states = []
    for b in range(count):
        states.append(state)
        states_ref[b] = state
        if b < count - 1:
            state = mm(maps_ref[b, :, :head], state) + maps_ref[b, :, head:]
    outs, pseudos = [], []
    for b in range(count):
        rows = slice(b * BLOCK, (b + 1) * BLOCK)
        made = mm(jnp.concatenate([qo_ref[rows, :head], wu_ref[rows, :head]]), states[b])
        outs.append(qo_ref[rows, head:] + made[:BLOCK])
        pseudos.append(wu_ref[rows, head:] - made[BLOCK:])
    out = jnp.concatenate(outs)
    pseudo_ref[...] = jnp.concatenate(pseudos)
    scale = lax.rsqrt(jnp.mean(out * out, axis=1, keepdims=True) + 1e-5)
    hidden_ref[...] = (out * scale * gain_ref[...]).astype(BF16)
    lifted = d_hidden_ref[...] * gain_ref[...]
    d_out = scale * lifted - out * (scale * scale * scale) * jnp.mean(lifted * out, axis=1, keepdims=True)
    d_out_ref[...] = d_out
    d_state = None
    for b in reversed(range(count)):
        rows = slice(b * BLOCK, (b + 1) * BLOCK)
        part = mm_tn(qo_ref[rows, :head], d_out[rows])
        from_out_ref[b] = part
        d_state = part if d_state is None else part + mm_tn(maps_ref[b, :, :head], d_state)
    d_enter_ref[...] = d_state


def share_kernel(place_ref, hidden_ref, *refs):
    pieces, share_ref = refs[:-1], refs[-1]
    size, here, head = share_ref.shape[1], share_ref.shape[3], hidden_ref.shape[1]
    for k, piece in enumerate(pieces):
        index = index_of(place_ref, k, size)
        for c in range(2):
            share_ref[c, index] = lax.dot_general(
                piece[:, 3 * head :], hidden_ref[c * here : (c + 1) * here], (((1,), (1,)), ((), ())),
                preferred_element_type=F32,
            )


def last_kernel(place_ref, hidden_ref, up_ref, up_other_ref, last_ref):
    here, core = up_ref.shape[2], place_ref[1]
    own, other = hidden_ref[own_rows(core, here)], hidden_ref[own_rows(1 - core, here)]
    for k in range(up_ref.shape[0]):
        last_ref[k] = jnp.dot(up_ref[k], own, preferred_element_type=F32) + jnp.dot(
            up_other_ref[k], other, preferred_element_type=F32
        )


def post_kernel(
    place_ref, near_ref, far_ref, far_map_ref, maps_ref, from_out_ref, states_ref, pseudo_ref, d_out_ref, inv_ref,
    score_ref, grow_ref, total_ref, beta_ref, docs_ref, doc_row_ref, conv_ref, features_ref, last_ref,
    d_proj_ref, power_ref, right_ref, left_ref,
    d_ext_ref,
):
    length, head = d_out_ref.shape
    count = length // BLOCK
    core, here = place_ref[1], length // 2
    d_state = near_ref[...] + lax.dot_general(
        far_map_ref[...].T, far_ref[...], (((1,), (0,)), ((), ())), preferred_element_type=F32
    )
    d_after = [None] * count
    for b in reversed(range(count)):
        d_after[b] = d_state
        if b > 0:
            d_state = from_out_ref[b] + mm_tn(maps_ref[b, :, :head], d_state)
    total = total_ref[...]
    gate = jax.nn.sigmoid(total)
    active = total * gate
    raw_q, raw_k = active[:, :head], active[:, head : 2 * head]
    inv_q = lax.rsqrt(jnp.sum(raw_q * raw_q, axis=1, keepdims=True) + 1e-6)
    inv_k = lax.rsqrt(jnp.sum(raw_k * raw_k, axis=1, keepdims=True) + 1e-6)
    query, keys = raw_q * inv_q, raw_k * inv_k
    grow, shrink, tail = grow_ref[:, :head], grow_ref[:, head : 2 * head], grow_ref[:, 2 * head :]
    key_grow, key_shrink, query_grow, key_tail = keys * grow, keys * shrink, query * grow, keys * tail
    beta = beta_ref[:, :1]
    _, _, _, inclusive, strict = masks(docs_ref, doc_row_ref)
    carried = carried_of(docs_ref)
    d_out, pseudo = d_out_ref[...], pseudo_ref[...]

    def each(function):
        return jnp.concatenate([function(b, slice(b * BLOCK, (b + 1) * BLOCK)) for b in range(count)])

    d_pseudo = mm_tn(score_ref[...], d_out) + each(lambda b, rows: mm(key_tail[rows], d_after[b]))
    d_target = mm_tn(inv_ref[...], d_pseudo)
    both = mm_nt(jnp.concatenate([d_out, d_target]), pseudo)
    d_scores = jnp.where(inclusive, both[:length], 0.0)
    d_lower = jnp.where(strict, both[length:], 0.0) * (-beta)
    d_values = beta * d_target
    d_from_keys = -carried * d_values
    lifted_out = carried * d_out
    d_query_grow = each(lambda b, rows: mm_nt(lifted_out[rows], states_ref[b])) + mm(d_scores, key_shrink)
    d_key_grow = each(lambda b, rows: mm_nt(d_from_keys[rows], states_ref[b])) + mm(d_lower, key_shrink)
    d_key_shrink = mm_tn(d_scores, query_grow) + mm_tn(d_lower, key_grow)
    d_key_tail = each(lambda b, rows: mm_nt(pseudo[rows], d_after[b]))
    d_query = d_query_grow * grow
    d_keys = d_key_grow * grow + d_key_shrink * shrink + d_key_tail * tail
    d_query = inv_q * d_query - query * (inv_q * jnp.sum(d_query * query, axis=1, keepdims=True))
    d_keys = inv_k * d_keys - keys * (inv_k * jnp.sum(d_keys * keys, axis=1, keepdims=True))
    d_total = jnp.concatenate([d_query, d_keys, d_values], axis=1) * (gate * (1.0 + total * (1.0 - gate)))
    d_ext_ref[...] = jnp.zeros_like(d_ext_ref)
    for j in range(TAPS):
        same = (docs_ref[:, j : j + 1] == docs_ref[:, 3:4]).astype(F32)
        spot = slice(HALO - 3 + j, HALO - 3 + j + length)
        d_ext_ref[spot] = d_ext_ref[spot] + d_total * taps_of(conv_ref, core, head, j) * same
    d_proj_ref[:here] = d_ext_ref[own_rows(core, here, HALO)].astype(BF16)
    d_proj_ref[here:length] = d_ext_ref[own_rows(1 - core, here, HALO)].astype(BF16)
    d_proj_ref[length:] = d_ext_ref[:HALO].astype(BF16)
    most = jnp.max(jnp.abs(d_ext_ref[...]), axis=0, keepdims=True) * (TOKEN_MOST * 1.01 * (length + HALO))
    power = jnp.ceil(jnp.log(jnp.maximum(most, 1e-30)) * 1.4426950408889634 + 0.01)
    power = jnp.concatenate([power, jnp.full((1, head), LAST_POWER, F32)], axis=1)
    power_ref[...] = jnp.broadcast_to(power, power_ref.shape)
    size, span, _ = features_ref.shape
    scale = jnp.exp2(TOP - power)
    for ref, by in ((right_ref, size // 2), (left_ref, size // 2 + 1)):
        index = lax.rem(place_ref[0] + by, size)
        first = jnp.dot(features_ref[index], d_proj_ref[...], preferred_element_type=F32)
        ref[:span, : 3 * head] = (first * scale[:, : 3 * head]).astype(ref.dtype)
        ref[:span, 3 * head :] = (last_ref[index] * scale[:, 3 * head :]).astype(ref.dtype)
        ref[span:] = jnp.broadcast_to(power, (16, 4 * head)).astype(ref.dtype)


def call(kernel, outs, *args, scratch=()):
    def spec(arg):
        return pl.BlockSpec(memory_space=pltpu.SMEM if arg.ndim == 1 else pltpu.VMEM)

    return pl.pallas_call(
        kernel,
        out_shape=tuple(jax.ShapeDtypeStruct(shape, dtype) for shape, dtype in outs),
        in_specs=[spec(arg) for arg in args],
        out_specs=tuple(pl.BlockSpec(memory_space=pltpu.VMEM) for _ in outs),
        scratch_shapes=list(scratch),
        compiler_params=pltpu.CompilerParams(vmem_limit_bytes=VMEM_LIMIT),
    )(*args)


def pack(total, power):
    scaled = (total * jnp.exp2(TOP - power)).astype(F16)
    return jnp.concatenate([scaled, jnp.broadcast_to(power, (16, total.shape[1])).astype(F16)])


def unpack(packed):
    power = packed[-16:-15].astype(F32)
    return packed[:-16].astype(F32) * jnp.exp2(power - TOP), power


def swap(array, axis):
    return lax.ppermute(array, axis, [(0, 1), (1, 0)])


def turn(array, axis, by):
    size = lax.axis_size(axis)
    return lax.ppermute(array, axis, [(i, (i + by) % size) for i in range(size)])


def shift(array, axis, by):
    size = lax.axis_size(axis)
    return lax.ppermute(array, axis, [(i, i + by) for i in range(size) if 0 <= i + by < size])


def ordered(mine, other, index):
    return jnp.where(index == 0, jnp.stack([mine, other]), jnp.stack([other, mine]))


def pick(array, index):
    return lax.dynamic_index_in_dim(array, index, 0, keepdims=False)


def put(array, piece, index):
    return lax.dynamic_update_index_in_dim(array, piece, index, 0)


def outer(a, b):
    return lax.dot_general(a, b, (((0,), (0,)), ((), ())), preferred_element_type=F32)


def per_device(
    tokens, cotangent, doc_ids, projections, conv_weight, gate_down, gate_up, decay_log, beta_weight, norm_gain
):
    z, core, x, ylo, roll = (lax.axis_index(a) for a in ("z", "core", "x", "ylo", "roll"))
    nz, nx = lax.axis_size("z"), lax.axis_size("x")
    here = tokens.shape[1]
    head = norm_gain.shape[0]
    rows = projections.shape[0]
    length = 2 * here
    span = 4 * rows

    split = projections.reshape(rows, 4, 2, head)
    mine = lax.dynamic_index_in_dim(split, core, 2, keepdims=False).reshape(rows, 4 * head)
    theirs = lax.dynamic_index_in_dim(split, 1 - core, 2, keepdims=False).reshape(rows, 4 * head)
    chip_rows = ordered(mine, swap(theirs, "core"), core)
    piece = jnp.swapaxes(ordered(chip_rows, swap(chip_rows, "roll"), roll), 0, 1).reshape(span, 4 * head)

    block = jnp.stack([tokens[0].T, cotangent[0].T])
    pair = ordered(block, swap(block, "ylo"), ylo)
    behind, ahead = turn(pair, "x", 1), turn(pair, "x", -1)
    across = [turn(behind[:, 0], "x", 1), turn(ahead[:, 1], "x", -1)]

    def ring_order(i):
        full = jnp.zeros((nx,) + across[i].shape, across[i].dtype)
        for by, part in ((0, pair[:, i]), (1, behind[:, i]), (-1, ahead[:, i]), (2, across[i])):
            full = put(full, part, (x - by) % nx)
        return full.reshape(-1, here)

    features, upstream = ring_order(0), ring_order(1)
    model = features.shape[0]
    own = jnp.concatenate([features, jnp.broadcast_to((doc_ids + 1).astype(BF16), (16, here))])
    other = swap(own, "core")
    up_other = swap(upstream, "core")
    place = jnp.stack([z, core]).astype(jnp.int32)
    (halo,) = call(halo_kernel, [((HALO, model + 128), BF16)], place, own, other)
    halo = shift(halo, "z", 1)
    upstream, up_other = upstream.reshape(nz, span, here), up_other.reshape(nz, span, here)

    arrived = [piece]
    right = left = piece
    for k in range(1, nz // 2 + 1):
        right = turn(right, "z", 1)
        arrived.append(right)
        if k < nz // 2:
            left = turn(left, "z", -1)
            arrived.append(left)
    blocks, doc_columns, doc_row, projected, grow, beta, _ = call(
        gather_kernel,
        [
            ((nz, span, length + HALO), BF16), ((length, 8), F32), ((1, length), F32),
            ((length + HALO, 3 * head), F32), ((length, 3 * head), F32), ((length, head), F32), ((length, head), F32),
        ],
        place, decay_log, own, other, halo, gate_down.reshape(nz, span, head), beta_weight.T, gate_up, *arrived[:-1],
    )
    total, inverse, scores, wu, qo, maps, device_map, device_map16 = call(
        pre_kernel,
        [
            ((length, 3 * head), F32), ((length, length), F32), ((length, length), F32), ((length, 2 * head), F32),
            ((length, 2 * head), F32), ((length // BLOCK, head, 2 * head), F32), ((head, 2 * head), F32),
            ((head, 2 * head), BF16),
        ],
        place, blocks, arrived[-1], projected, grow, beta, conv_weight, doc_columns, doc_row,
        scratch=[pltpu.VMEM((length + HALO, 3 * head), F32)],
    )
    device_map, device_map16, late = lax.optimization_barrier((device_map, device_map16, place))
    (d_hidden,) = call(hidden_grad_kernel, [((length, head), F32)], late, upstream, up_other, *arrived)

    one, two = shift(device_map, "z", 1), shift(device_map16, "z", 2).astype(F32)
    joined = product(one[:, :head], two, (1, 0), HIGH)
    near = jnp.concatenate([joined[:, :head], joined[:, head:] + one[:, head:]], axis=1)
    far = shift(near[:, head:].astype(BF16), "z", 2)
    far_map = shift(near[:, :head].astype(BF16), "z", -3)
    hidden, d_out, pseudo, states, from_out, d_enter = call(
        mid_kernel,
        [
            ((length, head), BF16), ((length, head), F32), ((length, head), F32), ((length // BLOCK, head, head), F32),
            ((length // BLOCK, head, head), F32), ((head, head), F32),
        ],
        near, far, maps, wu, qo, d_hidden, norm_gain[None],
    )
    d_two = d_enter + lax.dot_general(
        device_map[:, :head], shift(d_enter, "z", -1), (((0,), (0,)), ((), ())), precision=HIGH
    )
    d_two, late, far_map = lax.optimization_barrier((d_two, hidden, far_map))
    d_near, d_far = shift(d_two, "z", -1), shift(d_two.astype(BF16), "z", -3)
    (last,) = call(last_kernel, [((nz, span, head), F32)], place, late, upstream, up_other)
    d_projected, power, right, left = call(
        post_kernel,
        [((length + HALO, 3 * head), BF16), ((8, 4 * head), F32)] + [((span + 16, 4 * head), F32)] * 2,
        place, d_near, d_far, far_map, maps, from_out, states, pseudo, d_out, inverse, scores, grow, total, beta,
        doc_columns, doc_row, conv_weight, blocks, last,
        scratch=[pltpu.VMEM((length + HALO, 3 * head), F32)],
    )

    own_power = power[:1]

    def part(by):
        index = (z + by) % nz
        first = jnp.dot(pick(blocks, index), d_projected, preferred_element_type=F32)
        return jnp.concatenate([first, pick(last, index)], axis=1)

    def add(packed, by):
        total, power = unpack(packed)
        return total + part(by), jnp.maximum(power, own_power) + 1.0

    half = nz // 2
    late, d_projected = lax.optimization_barrier((hidden, d_projected))
    right, left = turn(right.astype(F16), "z", 1), turn(left.astype(F16), "z", -1)
    (share,) = call(share_kernel, [((2, nz, span, here), F32)], place, late, *arrived)
    right, left, share = lax.optimization_barrier((right, left, share))
    right = turn(pack(*add(right, half - 1)), "z", 1)
    left = turn(pack(*add(left, 2 - half)), "z", -1)
    from_core = swap((pick(share, 1 - core) * LIFT).astype(F16), "core")
    right, left, from_core = lax.optimization_barrier((right, left, from_core))
    right = turn(pack(*add(right, half - 2)), "z", 1)
    left = turn(pack(*add(left, 3 - half)), "z", -1)
    shared = (pick(share, core) * LIFT + from_core.astype(F32)).reshape(nx, 2, span, here)
    from_ylo = swap(lax.dynamic_index_in_dim(shared, 1 - ylo, 1, keepdims=False).astype(F16), "ylo")
    right, left, from_ylo = lax.optimization_barrier((right, left, from_ylo))
    right = turn(pack(*add(right, half - 3)), "z", 1)
    shared = lax.dynamic_index_in_dim(shared, ylo, 1, keepdims=False) + from_ylo.astype(F32)
    from_x = [turn(pick(shared, (x + by) % nx).astype(F16), "x", by) for by in (1, -1, 2)]
    layer_out = ((pick(shared, x) + sum(f.astype(F32) for f in from_x)) * (1.0 / LIFT)).T.astype(BF16)[None]
    total, power = add(right, 0)
    more, more_power = unpack(left)
    packed = pack(total + more, jnp.maximum(power, more_power) + 1.0)
    grad = unpack(packed)[0] + unpack(swap(packed, "roll"))[0]
    fresh = (piece.astype(F32) - RATE * grad).astype(BF16).reshape(2, span // 2, 4 * head)
    kept, sent = pick(fresh, core), pick(fresh, 1 - core)
    heads = ordered(kept, swap(sent, "core"), core).reshape(2, span // 2, 4, head)
    engine_tiles = jnp.moveaxis(heads, 0, 2).reshape(span // 2, 4, 2 * head)
    return (layer_out, engine_tiles)


def solution(mesh):
    fine = Mesh(mesh.devices.reshape(8, 2, 4, 2, 2), ("z", "core", "x", "ylo", "roll"))
    seq, mp = ("z", "core"), ("x", "ylo")
    in_specs = (
        P("roll", seq, mp),
        P("roll", seq, mp),
        P("roll", seq),
        P(("z", "core", "roll"), None, mp),
        P(None, None, mp),
        P(),
        P(None, mp),
        P(mp),
        P(None, mp),
        P(),
    )
    out_specs = (P("roll", seq, mp), P(seq, None, mp))
    return jax.shard_map(per_device, mesh=fine, in_specs=in_specs, out_specs=out_specs, check_vma=False)
```

```python
import jax
import jax.numpy as jnp
from jax import lax
from jax.experimental import pallas as pl
from jax.experimental.pallas import tpu as pltpu
from jax.sharding import Mesh
from jax.sharding import PartitionSpec as P

BLOCK = 64
TAPS = 4
HALO = 16
RATE = 0.01
TOKEN_MOST = 6.0
LAST_POWER = 16.0
TOP = 15.0
LIFT = 8.0
F32 = jnp.float32
F16 = jnp.float16
BF16 = jnp.bfloat16
HIGH = lax.Precision.HIGHEST
VMEM_LIMIT = 56 * 1024 * 1024


def product(a, b, dims, precision=None):
    return lax.dot_general(a, b, ((dims[:1], dims[1:]), ((), ())), precision=precision, preferred_element_type=F32)


def halves(a):
    high = a.astype(BF16)
    return high, (a - high.astype(F32)).astype(BF16)


def split_product(a, b, dims):
    (a_high, a_low), (b_high, b_low) = halves(a), halves(b)
    return product(a_high, b_high, dims) + (product(a_high, b_low, dims) + product(a_low, b_high, dims))


def mm(a, b):
    return split_product(a, b, (1, 0))


def mm_nt(a, b):
    return split_product(a, b, (1, 1))


def mm_tn(a, b):
    return mm(a.T, b)


def softplus(x):
    return jnp.maximum(x, 0.0) + jnp.log1p(jnp.exp(-jnp.abs(x)))


def masks(docs_ref, doc_row_ref):
    length = docs_ref.shape[0]
    row = lax.broadcasted_iota(jnp.int32, (length, length), 0)
    col = lax.broadcasted_iota(jnp.int32, (length, length), 1)
    inside = (row // BLOCK == col // BLOCK) & (row >= col)
    paired = docs_ref[:, 3:4] == doc_row_ref[...]
    inclusive = inside & paired
    strict = inclusive & (row > col)
    return row, col, inside, inclusive, strict


def carried_of(docs_ref):
    return (docs_ref[:, 3:4] == docs_ref[:, 4:5]).astype(F32)


def own_rows(core, here, skip=0):
    return pl.ds(pl.multiple_of(skip + core * here, 16), here)


def offset_of(k):
    return ((k + 1) // 2) * (-1 if k % 2 else 1)


def index_of(place_ref, k, size):
    return lax.rem(place_ref[0] + offset_of(k) + size, size)


def taps_of(conv_ref, core, head, j):
    here = pl.ds(pl.multiple_of(core * head, head), head)
    return jnp.concatenate([conv_ref[c, j : j + 1, here] for c in range(3)], axis=1)


def halo_kernel(place_ref, own_ref, other_ref, halo_ref):
    model, here = halo_ref.shape[1] - 128, own_ref.shape[1]
    last = jnp.where(place_ref[1] == 1, own_ref[...].astype(F32), other_ref[...].astype(F32))
    halo_ref[:, :model] = last[:model].T[here - HALO :].astype(BF16)
    row = lax.broadcasted_iota(jnp.int32, (HALO, here), 0)
    col = lax.broadcasted_iota(jnp.int32, (HALO, here), 1)
    docs = jnp.sum(jnp.where(col == row + (here - HALO), last[model : model + HALO], 0.0), axis=1, keepdims=True)
    halo_ref[:, model:] = jnp.broadcast_to(docs, (HALO, 128)).astype(BF16)


def gather_kernel(
    place_ref, decay_log_ref, own_ref, other_ref, halo_ref, gate_down_ref, beta_weight_ref, gate_up_ref, *refs
):
    pieces, (features_ref, docs_ref, doc_row_ref, proj_ref, grow_ref, beta_ref, decay_ref) = refs[:-7], refs[-7:]
    size, span, _ = features_ref.shape
    length, head = decay_ref.shape
    here, count, model = length // 2, length // BLOCK, size * span
    core = place_ref[1]
    halo = halo_ref[:, :model].T
    for k in range(size):
        rows = slice(k * span, (k + 1) * span)
        features_ref[k, :, :here] = own_ref[rows]
        features_ref[k, :, here:length] = other_ref[rows]
        features_ref[k, :, length:] = halo[rows]

    own_docs, other_docs = (ref[model : model + 16].astype(F32)[:1] for ref in (own_ref, other_ref))
    doc_row = jnp.where(
        core == 0, jnp.concatenate([own_docs, other_docs], axis=1), jnp.concatenate([other_docs, own_docs], axis=1)
    )
    doc_row_ref[...] = doc_row
    rim = halo_ref[:, model:].astype(F32)
    row = lax.broadcasted_iota(jnp.int32, (length, length), 0)
    col = lax.broadcasted_iota(jnp.int32, (length, length), 1)
    spot = lax.broadcasted_iota(jnp.int32, (length, 1), 0)

    def taken(line, target):
        return jnp.sum(jnp.where(col == target, line, 0.0), axis=1, keepdims=True)

    columns = []
    for back in (3, 2, 1, 0):
        column = taken(doc_row, row - back)
        for t in range(back):
            at = HALO + t - back
            column = jnp.where(spot == t, rim[at : at + 1, :1], column)
        columns.append(column)
    first = row // BLOCK * BLOCK
    prior = jnp.where(spot < BLOCK, rim[HALO - 1 : HALO, :1], taken(doc_row, first - 1))
    last = taken(doc_row, first + BLOCK - 1)
    docs_ref[...] = jnp.concatenate(columns + [prior, last, columns[3], columns[3]], axis=1)

    proj = jnp.zeros(proj_ref.shape, F32)
    low = jnp.zeros((length, head), F32)
    logits = jnp.zeros((beta_weight_ref.shape[0], features_ref.shape[2]), F32)
    for k in range(size):
        index = index_of(place_ref, k, size)
        rows = features_ref[index].T
        low = low + jnp.dot(rows[:length], gate_down_ref[index], preferred_element_type=F32)
        logits = logits + jnp.dot(
            beta_weight_ref[:, k * span : (k + 1) * span], features_ref[k], preferred_element_type=F32
        )
        if k < len(pieces):
            proj = proj + jnp.dot(rows, pieces[k][:, : 3 * head], preferred_element_type=F32)
    proj_ref[...] = proj
    gate_up = gate_up_ref[:, pl.ds(pl.multiple_of(core * head, head), head)]
    rates = jnp.dot(low.astype(BF16), gate_up, preferred_element_type=F32)
    log_decay = -jnp.exp(jnp.full((1, head), decay_log_ref[core])) * softplus(rates)
    logit = jnp.where(core == 0, logits[:1, :length], logits[1:2, :length])
    beta = jnp.broadcast_to(jax.nn.sigmoid(taken(logit, row)), (length, head))
    for ref, array in ((decay_ref, log_decay), (beta_ref, beta)):
        ref[own_rows(core, here)] = array[:here]
        ref[own_rows(1 - core, here)] = array[here:]
    inside = (row // BLOCK == col // BLOCK) & (row >= col)
    summed = product(inside.astype(F32), decay_ref[...], (1, 0), HIGH)
    ends = jnp.concatenate(
        [jnp.broadcast_to(summed[b * BLOCK + BLOCK - 1 : (b + 1) * BLOCK], (BLOCK, head)) for b in range(count)]
    )
    grow_ref[:, :head] = jnp.exp(summed)
    grow_ref[:, head : 2 * head] = jnp.exp(-summed)
    grow_ref[:, 2 * head :] = jnp.exp(ends - summed) * (columns[3] == last).astype(F32)


def hidden_grad_kernel(place_ref, up_ref, up_other_ref, *refs):
    pieces, d_hidden_ref = refs[:-1], refs[-1]
    size, here, (length, head) = up_ref.shape[0], up_ref.shape[2], d_hidden_ref.shape
    d_hidden = jnp.zeros((length, head), F32)
    for k, piece in enumerate(pieces):
        index = index_of(place_ref, k, size)
        both = jnp.concatenate([up_ref[index].T, up_other_ref[index].T])
        d_hidden = d_hidden + jnp.dot(both, piece[:, 3 * head :], preferred_element_type=F32)
    d_hidden_ref[own_rows(place_ref[1], here)] = d_hidden[:here]
    d_hidden_ref[own_rows(1 - place_ref[1], here)] = d_hidden[here:]


def pre_kernel(
    place_ref, features_ref, piece_ref, proj_in_ref,
    grow_ref, beta_ref, conv_ref, docs_ref, doc_row_ref,
    total_ref, inv_ref, score_ref, wu_ref, qo_ref, maps_ref, device_map_ref, device_map16_ref,
    ext_ref,
):
    length, head = beta_ref.shape
    here, count = length // 2, length // BLOCK
    size, core = features_ref.shape[0], place_ref[1]
    index = index_of(place_ref, size - 1, size)
    proj = proj_in_ref[...] + jnp.dot(features_ref[index].T, piece_ref[:, : 3 * head], preferred_element_type=F32)
    ext_ref[:HALO] = proj[length:]
    ext_ref[own_rows(core, here, HALO)] = proj[:here]
    ext_ref[own_rows(1 - core, here, HALO)] = proj[here:length]
    total = jnp.zeros((length, 3 * head), F32)
    for j in range(TAPS):
        same = (docs_ref[:, j : j + 1] == docs_ref[:, 3:4]).astype(F32)
        total = total + ext_ref[HALO - 3 + j : HALO - 3 + j + length] * taps_of(conv_ref, core, head, j) * same
    total_ref[...] = total
    active = total * jax.nn.sigmoid(total)
    query, keys, values = active[:, :head], active[:, head : 2 * head], active[:, 2 * head :]
    query = query * lax.rsqrt(jnp.sum(query * query, axis=1, keepdims=True) + 1e-6)
    keys = keys * lax.rsqrt(jnp.sum(keys * keys, axis=1, keepdims=True) + 1e-6)
    beta = beta_ref[:, :1]
    row, col, _, inclusive, strict = masks(docs_ref, doc_row_ref)
    carried = carried_of(docs_ref)
    grow, shrink, tail = grow_ref[:, :head], grow_ref[:, head : 2 * head], grow_ref[:, 2 * head :]
    key_grow, key_shrink, query_grow, key_tail = keys * grow, keys * shrink, query * grow, keys * tail
    both = mm_nt(jnp.concatenate([key_grow, query_grow]), key_shrink)
    lower = jnp.where(strict, both[:length], 0.0) * beta
    scores = jnp.where(inclusive, both[length:], 0.0)
    score_ref[...] = scores
    inverse = (row == col).astype(F32) - jnp.where(row // 2 == col // 2, lower, 0.0)
    size = 2
    while size < BLOCK:
        corner = jnp.where((row // (2 * size) == col // (2 * size)) & (row // size != col // size), lower, 0.0)
        inverse = inverse - mm(inverse, mm(corner, inverse))
        size *= 2
    inv_ref[...] = inverse
    wu = mm(inverse, jnp.concatenate([beta * carried * key_grow, beta * values], axis=1))
    wu_ref[...] = wu
    mixed = mm(scores, wu)
    qo_ref[:, :head] = carried * query_grow - mixed[:, :head]
    qo_ref[:, head:] = mixed[:, head:]
    eye = lax.broadcasted_iota(jnp.int32, (head, head), 0) == lax.broadcasted_iota(jnp.int32, (head, head), 1)
    pairs = []
    for b in range(count):
        rows = slice(b * BLOCK, (b + 1) * BLOCK)
        last = (b + 1) * BLOCK - 1
        keep = grow[last : last + 1] * carried[last : last + 1]
        update = mm_tn(key_tail[rows], wu[rows])
        moved = jnp.where(eye, keep, 0.0) - update[:, :head]
        maps_ref[b, :, :head] = moved
        maps_ref[b, :, head:] = update[:, head:]
        pairs.append((moved, update[:, head:]))

    def after(second, first):
        made = mm(second[0], jnp.concatenate(first, axis=1))
        return (made[:, :head], made[:, head:] + second[1])

    while len(pairs) > 1:
        pairs = [after(pairs[i + 1], pairs[i]) for i in range(0, len(pairs), 2)]
    device_map_ref[:, :head] = pairs[0][0]
    device_map_ref[:, head:] = pairs[0][1]
    device_map16_ref[:, :head] = pairs[0][0].astype(BF16)
    device_map16_ref[:, head:] = pairs[0][1].astype(BF16)


def mid_kernel(
    near_ref, far_ref, maps_ref, wu_ref, qo_ref, d_hidden_ref, gain_ref,
    hidden_ref, d_out_ref, pseudo_ref, states_ref, from_out_ref, d_enter_ref,
):
    length, head = d_hidden_ref.shape
    count = length // BLOCK
    state = near_ref[:, head:] + mm(near_ref[:, :head], far_ref[...].astype(F32))
    states = []
    for b in range(count):
        states.append(state)
        states_ref[b] = state
        if b < count - 1:
            state = mm(maps_ref[b, :, :head], state) + maps_ref[b, :, head:]
    outs, pseudos = [], []
    for b in range(count):
        rows = slice(b * BLOCK, (b + 1) * BLOCK)
        made = mm(jnp.concatenate([qo_ref[rows, :head], wu_ref[rows, :head]]), states[b])
        outs.append(qo_ref[rows, head:] + made[:BLOCK])
        pseudos.append(wu_ref[rows, head:] - made[BLOCK:])
    out = jnp.concatenate(outs)
    pseudo_ref[...] = jnp.concatenate(pseudos)
    scale = lax.rsqrt(jnp.mean(out * out, axis=1, keepdims=True) + 1e-5)
    hidden_ref[...] = (out * scale * gain_ref[...]).astype(BF16)
    lifted = d_hidden_ref[...] * gain_ref[...]
    d_out = scale * lifted - out * (scale * scale * scale) * jnp.mean(lifted * out, axis=1, keepdims=True)
    d_out_ref[...] = d_out
    d_state = None
    for b in reversed(range(count)):
        rows = slice(b * BLOCK, (b + 1) * BLOCK)
        part = mm_tn(qo_ref[rows, :head], d_out[rows])
        from_out_ref[b] = part
        d_state = part if d_state is None else part + mm_tn(maps_ref[b, :, :head], d_state)
    d_enter_ref[...] = d_state


def share_kernel(place_ref, hidden_ref, *refs):
    pieces, share_ref = refs[:-1], refs[-1]
    size, here, head = share_ref.shape[1], share_ref.shape[3], hidden_ref.shape[1]
    for k, piece in enumerate(pieces):
        index = index_of(place_ref, k, size)
        for c in range(2):
            share_ref[c, index] = lax.dot_general(
                piece[:, 3 * head :], hidden_ref[c * here : (c + 1) * here], (((1,), (1,)), ((), ())),
                preferred_element_type=F32,
            )


def last_kernel(place_ref, hidden_ref, up_ref, up_other_ref, last_ref):
    here, core = up_ref.shape[2], place_ref[1]
    own, other = hidden_ref[own_rows(core, here)], hidden_ref[own_rows(1 - core, here)]
    for k in range(up_ref.shape[0]):
        last_ref[k] = jnp.dot(up_ref[k], own, preferred_element_type=F32) + jnp.dot(
            up_other_ref[k], other, preferred_element_type=F32
        )


def post_kernel(
    place_ref, near_ref, far_ref, far_map_ref, maps_ref, from_out_ref, states_ref, pseudo_ref, d_out_ref, inv_ref,
    score_ref, grow_ref, total_ref, beta_ref, docs_ref, doc_row_ref, conv_ref, features_ref, last_ref,
    d_proj_ref, power_ref, right_ref, left_ref,
    d_ext_ref,
):
    length, head = d_out_ref.shape
    count = length // BLOCK
    core, here = place_ref[1], length // 2
    d_state = near_ref[...] + lax.dot_general(
        far_map_ref[...].T, far_ref[...], (((1,), (0,)), ((), ())), preferred_element_type=F32
    )
    d_after = [None] * count
    for b in reversed(range(count)):
        d_after[b] = d_state
        if b > 0:
            d_state = from_out_ref[b] + mm_tn(maps_ref[b, :, :head], d_state)
    total = total_ref[...]
    gate = jax.nn.sigmoid(total)
    active = total * gate
    raw_q, raw_k = active[:, :head], active[:, head : 2 * head]
    inv_q = lax.rsqrt(jnp.sum(raw_q * raw_q, axis=1, keepdims=True) + 1e-6)
    inv_k = lax.rsqrt(jnp.sum(raw_k * raw_k, axis=1, keepdims=True) + 1e-6)
    query, keys = raw_q * inv_q, raw_k * inv_k
    grow, shrink, tail = grow_ref[:, :head], grow_ref[:, head : 2 * head], grow_ref[:, 2 * head :]
    key_grow, key_shrink, query_grow, key_tail = keys * grow, keys * shrink, query * grow, keys * tail
    beta = beta_ref[:, :1]
    _, _, _, inclusive, strict = masks(docs_ref, doc_row_ref)
    carried = carried_of(docs_ref)
    d_out, pseudo = d_out_ref[...], pseudo_ref[...]

    def each(function):
        return jnp.concatenate([function(b, slice(b * BLOCK, (b + 1) * BLOCK)) for b in range(count)])

    d_pseudo = mm_tn(score_ref[...], d_out) + each(lambda b, rows: mm(key_tail[rows], d_after[b]))
    d_target = mm_tn(inv_ref[...], d_pseudo)
    both = mm_nt(jnp.concatenate([d_out, d_target]), pseudo)
    d_scores = jnp.where(inclusive, both[:length], 0.0)
    d_lower = jnp.where(strict, both[length:], 0.0) * (-beta)
    d_values = beta * d_target
    d_from_keys = -carried * d_values
    lifted_out = carried * d_out
    d_query_grow = each(lambda b, rows: mm_nt(lifted_out[rows], states_ref[b])) + mm(d_scores, key_shrink)
    d_key_grow = each(lambda b, rows: mm_nt(d_from_keys[rows], states_ref[b])) + mm(d_lower, key_shrink)
    d_key_shrink = mm_tn(d_scores, query_grow) + mm_tn(d_lower, key_grow)
    d_key_tail = each(lambda b, rows: mm_nt(pseudo[rows], d_after[b]))
    d_query = d_query_grow * grow
    d_keys = d_key_grow * grow + d_key_shrink * shrink + d_key_tail * tail
    d_query = inv_q * d_query - query * (inv_q * jnp.sum(d_query * query, axis=1, keepdims=True))
    d_keys = inv_k * d_keys - keys * (inv_k * jnp.sum(d_keys * keys, axis=1, keepdims=True))
    d_total = jnp.concatenate([d_query, d_keys, d_values], axis=1) * (gate * (1.0 + total * (1.0 - gate)))
    d_ext_ref[...] = jnp.zeros_like(d_ext_ref)
    for j in range(TAPS):
        same = (docs_ref[:, j : j + 1] == docs_ref[:, 3:4]).astype(F32)
        spot = slice(HALO - 3 + j, HALO - 3 + j + length)
        d_ext_ref[spot] = d_ext_ref[spot] + d_total * taps_of(conv_ref, core, head, j) * same
    d_proj_ref[:here] = d_ext_ref[own_rows(core, here, HALO)].astype(BF16)
    d_proj_ref[here:length] = d_ext_ref[own_rows(1 - core, here, HALO)].astype(BF16)
    d_proj_ref[length:] = d_ext_ref[:HALO].astype(BF16)
    most = jnp.max(jnp.abs(d_ext_ref[...]), axis=0, keepdims=True) * (TOKEN_MOST * 1.01 * (length + HALO))
    power = jnp.ceil(jnp.log(jnp.maximum(most, 1e-30)) * 1.4426950408889634 + 0.01)
    power = jnp.concatenate([power, jnp.full((1, head), LAST_POWER, F32)], axis=1)
    power_ref[...] = jnp.broadcast_to(power, power_ref.shape)
    size, span, _ = features_ref.shape
    scale = jnp.exp2(TOP - power)
    for ref, by in ((right_ref, size // 2), (left_ref, size // 2 + 1)):
        index = lax.rem(place_ref[0] + by, size)
        first = jnp.dot(features_ref[index], d_proj_ref[...], preferred_element_type=F32)
        ref[:span, : 3 * head] = (first * scale[:, : 3 * head]).astype(ref.dtype)
        ref[:span, 3 * head :] = (last_ref[index] * scale[:, 3 * head :]).astype(ref.dtype)
        ref[span:] = jnp.broadcast_to(power, (16, 4 * head)).astype(ref.dtype)


def call(kernel, outs, *args, scratch=()):
    def spec(arg):
        return pl.BlockSpec(memory_space=pltpu.SMEM if arg.ndim == 1 else pltpu.VMEM)

    return pl.pallas_call(
        kernel,
        out_shape=tuple(jax.ShapeDtypeStruct(shape, dtype) for shape, dtype in outs),
        in_specs=[spec(arg) for arg in args],
        out_specs=tuple(pl.BlockSpec(memory_space=pltpu.VMEM) for _ in outs),
        scratch_shapes=list(scratch),
        compiler_params=pltpu.CompilerParams(vmem_limit_bytes=VMEM_LIMIT),
    )(*args)


def pack(total, power):
    scaled = (total * jnp.exp2(TOP - power)).astype(F16)
    return jnp.concatenate([scaled, jnp.broadcast_to(power, (16, total.shape[1])).astype(F16)])


def unpack(packed):
    power = packed[-16:-15].astype(F32)
    return packed[:-16].astype(F32) * jnp.exp2(power - TOP), power


def swap(array, axis):
    return lax.ppermute(array, axis, [(0, 1), (1, 0)])


def turn(array, axis, by):
    size = lax.axis_size(axis)
    return lax.ppermute(array, axis, [(i, (i + by) % size) for i in range(size)])


def shift(array, axis, by):
    size = lax.axis_size(axis)
    return lax.ppermute(array, axis, [(i, i + by) for i in range(size) if 0 <= i + by < size])


def ordered(mine, other, index):
    return jnp.where(index == 0, jnp.stack([mine, other]), jnp.stack([other, mine]))


def pick(array, index):
    return lax.dynamic_index_in_dim(array, index, 0, keepdims=False)


def put(array, piece, index):
    return lax.dynamic_update_index_in_dim(array, piece, index, 0)


def outer(a, b):
    return lax.dot_general(a, b, (((0,), (0,)), ((), ())), preferred_element_type=F32)


def per_device(
    tokens, cotangent, doc_ids, projections, conv_weight, gate_down, gate_up, decay_log, beta_weight, norm_gain
):
    z, core, x, ylo, roll = (lax.axis_index(a) for a in ("z", "core", "x", "ylo", "roll"))
    nz, nx = lax.axis_size("z"), lax.axis_size("x")
    here = tokens.shape[1]
    head = norm_gain.shape[0]
    rows = projections.shape[0]
    length = 2 * here
    span = 4 * rows

    split = projections.reshape(rows, 4, 2, head)
    mine = lax.dynamic_index_in_dim(split, core, 2, keepdims=False).reshape(rows, 4 * head)
    theirs = lax.dynamic_index_in_dim(split, 1 - core, 2, keepdims=False).reshape(rows, 4 * head)
    chip_rows = ordered(mine, swap(theirs, "core"), core)
    piece = jnp.swapaxes(ordered(chip_rows, swap(chip_rows, "roll"), roll), 0, 1).reshape(span, 4 * head)

    block = jnp.stack([tokens[0].T, cotangent[0].T])
    pair = ordered(block, swap(block, "ylo"), ylo)
    behind, ahead = turn(pair, "x", 1), turn(pair, "x", -1)
    across = [turn(behind[:, 0], "x", 1), turn(ahead[:, 1], "x", -1)]

    def ring_order(i):
        full = jnp.zeros((nx,) + across[i].shape, across[i].dtype)
        for by, part in ((0, pair[:, i]), (1, behind[:, i]), (-1, ahead[:, i]), (2, across[i])):
            full = put(full, part, (x - by) % nx)
        return full.reshape(-1, here)

    features, upstream = ring_order(0), ring_order(1)
    model = features.shape[0]
    own = jnp.concatenate([features, jnp.broadcast_to((doc_ids + 1).astype(BF16), (16, here))])
    other = swap(own, "core")
    up_other = swap(upstream, "core")
    place = jnp.stack([z, core]).astype(jnp.int32)
    (halo,) = call(halo_kernel, [((HALO, model + 128), BF16)], place, own, other)
    halo = shift(halo, "z", 1)
    upstream, up_other = upstream.reshape(nz, span, here), up_other.reshape(nz, span, here)

    arrived = [piece]
    right = left = piece
    for k in range(1, nz // 2 + 1):
        right = turn(right, "z", 1)
        arrived.append(right)
        if k < nz // 2:
            left = turn(left, "z", -1)
            arrived.append(left)
    blocks, doc_columns, doc_row, projected, grow, beta, _ = call(
        gather_kernel,
        [
            ((nz, span, length + HALO), BF16), ((length, 8), F32), ((1, length), F32),
            ((length + HALO, 3 * head), F32), ((length, 3 * head), F32), ((length, head), F32), ((length, head), F32),
        ],
        place, decay_log, own, other, halo, gate_down.reshape(nz, span, head), beta_weight.T, gate_up, *arrived[:-1],
    )
    total, inverse, scores, wu, qo, maps, device_map, device_map16 = call(
        pre_kernel,
        [
            ((length, 3 * head), F32), ((length, length), F32), ((length, length), F32), ((length, 2 * head), F32),
            ((length, 2 * head), F32), ((length // BLOCK, head, 2 * head), F32), ((head, 2 * head), F32),
            ((head, 2 * head), BF16),
        ],
        place, blocks, arrived[-1], projected, grow, beta, conv_weight, doc_columns, doc_row,
        scratch=[pltpu.VMEM((length + HALO, 3 * head), F32)],
    )
    device_map, device_map16, late = lax.optimization_barrier((device_map, device_map16, place))
    (d_hidden,) = call(hidden_grad_kernel, [((length, head), F32)], late, upstream, up_other, *arrived)

    one, two = shift(device_map, "z", 1), shift(device_map16, "z", 2).astype(F32)
    joined = product(one[:, :head], two, (1, 0), HIGH)
    near = jnp.concatenate([joined[:, :head], joined[:, head:] + one[:, head:]], axis=1)
    far = shift(near[:, head:].astype(BF16), "z", 2)
    far_map = shift(near[:, :head].astype(BF16), "z", -3)
    hidden, d_out, pseudo, states, from_out, d_enter = call(
        mid_kernel,
        [
            ((length, head), BF16), ((length, head), F32), ((length, head), F32), ((length // BLOCK, head, head), F32),
            ((length // BLOCK, head, head), F32), ((head, head), F32),
        ],
        near, far, maps, wu, qo, d_hidden, norm_gain[None],
    )
    d_two = d_enter + lax.dot_general(
        device_map[:, :head], shift(d_enter, "z", -1), (((0,), (0,)), ((), ())), precision=HIGH
    )
    d_two, d_two16, late, far_map = lax.optimization_barrier((d_two, d_two.astype(BF16), hidden, far_map))
    d_near, d_far = shift(d_two, "z", -1), shift(d_two16, "z", -3)
    (last,) = call(last_kernel, [((nz, span, head), F32)], place, late, upstream, up_other)
    d_projected, power, right, left = call(
        post_kernel,
        [((length + HALO, 3 * head), BF16), ((8, 4 * head), F32)] + [((span + 16, 4 * head), BF16)] * 2,
        place, d_near, d_far, far_map, maps, from_out, states, pseudo, d_out, inverse, scores, grow, total, beta,
        doc_columns, doc_row, conv_weight, blocks, last,
        scratch=[pltpu.VMEM((length + HALO, 3 * head), F32)],
    )

    own_power = power[:1]

    def part(by):
        index = (z + by) % nz
        first = jnp.dot(pick(blocks, index), d_projected, preferred_element_type=F32)
        return jnp.concatenate([first, pick(last, index)], axis=1)

    def add(packed, by):
        total, power = unpack(packed)
        return total + part(by), jnp.maximum(power, own_power) + 1.0

    half = nz // 2
    late, d_projected = lax.optimization_barrier((hidden, d_projected))
    right, left = turn(right, "z", 1), turn(left, "z", -1)
    (share,) = call(share_kernel, [((2, nz, span, here), F32)], place, late, *arrived)
    right, left, share = lax.optimization_barrier((right, left, share))
    right = turn(pack(*add(right, half - 1)), "z", 1)
    left = turn(pack(*add(left, 2 - half)), "z", -1)
    from_core = swap((pick(share, 1 - core) * LIFT).astype(F16), "core")
    right, left, from_core = lax.optimization_barrier((right, left, from_core))
    right = turn(pack(*add(right, half - 2)), "z", 1)
    left = turn(pack(*add(left, 3 - half)), "z", -1)
    shared = (pick(share, core) * LIFT + from_core.astype(F32)).reshape(nx, 2, span, here)
    from_ylo = swap(lax.dynamic_index_in_dim(shared, 1 - ylo, 1, keepdims=False).astype(F16), "ylo")
    right, left, from_ylo = lax.optimization_barrier((right, left, from_ylo))
    right = turn(pack(*add(right, half - 3)), "z", 1)
    shared = lax.dynamic_index_in_dim(shared, ylo, 1, keepdims=False) + from_ylo.astype(F32)
    from_x = [turn(pick(shared, (x + by) % nx).astype(F16), "x", by) for by in (1, -1, 2)]
    layer_out = ((pick(shared, x) + sum(f.astype(F32) for f in from_x)) * (1.0 / LIFT)).T.astype(BF16)[None]
    total, power = add(right, 0)
    more, more_power = unpack(left)
    packed = pack(total + more, jnp.maximum(power, more_power) + 1.0)
    grad = unpack(packed)[0] + unpack(swap(packed, "roll"))[0]
    fresh = (piece.astype(F32) - RATE * grad).astype(BF16).reshape(2, span // 2, 4 * head)
    kept, sent = pick(fresh, core), pick(fresh, 1 - core)
    heads = ordered(kept, swap(sent, "core"), core).reshape(2, span // 2, 4, head)
    engine_tiles = jnp.moveaxis(heads, 0, 2).reshape(span // 2, 4, 2 * head)
    return (layer_out, engine_tiles)


def solution(mesh):
    fine = Mesh(mesh.devices.reshape(8, 2, 4, 2, 2), ("z", "core", "x", "ylo", "roll"))
    seq, mp = ("z", "core"), ("x", "ylo")
    in_specs = (
        P("roll", seq, mp),
        P("roll", seq, mp),
        P("roll", seq),
        P(("z", "core", "roll"), None, mp),
        P(None, None, mp),
        P(),
        P(None, mp),
        P(mp),
        P(None, mp),
        P(),
    )
    out_specs = (P("roll", seq, mp), P(seq, None, mp))
    return jax.shard_map(per_device, mesh=fine, in_specs=in_specs, out_specs=out_specs, check_vma=False)
```
